32 devices in a mesh: ctx: 8 (over z, core), fsdp: 4 (over y, x).
Axes of the slice: x: 2, y: 2, z: 4, core: 2. Of those that a mesh axis runs over, the one named last changes fastest.
Arguments:
- hidden: bfloat16 [2, 4, 512, 2048], P(None, 'fsdp', 'ctx'), may hold values from -6 to 6
- cotangent: bfloat16 [2, 4, 512, 2048], P(None, 'fsdp', 'ctx'), may hold values from -6 to 6
- lengths: int32 [2, 4], P(None, 'fsdp'), may hold values from 128 to 512, as said below
- norm_gain: float32 [2048], replicated, may hold values from 0.5 to 1.5
- input_weight: bfloat16 [2048, 8512], P('fsdp'), may hold values from -0.125 to 0.125
- conv_w: float32 [4, 4352], replicated, may hold values from -3 to 3
- conv_b: float32 [4352], replicated, may hold values from -3 to 3
- dt_bias: float32 [64], replicated, may hold values from -4 to -2
- a_log: float32 [64], replicated, may hold values from -10 to -0.5
- d_skip: float32 [64], replicated, may hold values from 0.5 to 1.5
- gate_gain: float32 [4096], replicated, may hold values from 0.5 to 1.5
- output_weight: bfloat16 [4096, 2048], P('fsdp'), may hold values from -0.09375 to 0.09375
Outputs:
- out: bfloat16 [2, 4, 512, 2048], P(None, 'fsdp', 'ctx')
- d_hidden: float32 [2, 4, 512, 2048], P(None, 'fsdp', 'ctx')
- grad_norm_gain: float32 [2048], replicated
- grad_in_w: float32 [2048, 8512], P(('ctx', 'fsdp'))
- grad_conv_w: float32 [4, 4352], replicated
- grad_conv_b: float32 [4352], replicated
- grad_dt_bias: float32 [64], replicated
- grad_a_log: float32 [64], replicated
- grad_d_skip: float32 [64], replicated
- grad_gate_gain: float32 [4096], replicated
- grad_out_w: float32 [4096, 2048], P(('ctx', 'fsdp'))
The draws below stay inside these ranges and needn't reach their ends.
Inputs may be any that keep to these rules, and one draw needn't show every extreme that they name: `lengths`: some sequence has all 512 slots live in every draw.
All inputs are finite; a program needn't handle non-finite values.
Results may differ from the reference program's by a relative error of at most 0.012.
The reference program's roundings to bfloat16 on the way count: a program that leaves them out, or rounds other values in their place, can miss the bound.
Values may be sent and summed in bfloat16 or wider, within the bound.
A program may use at most 384 MiB of HBM per device.

```python
import math
import jax
import jax.numpy as jnp
from jax import lax

D = 2048
HEADS = 64
HEAD_DIM = 64
N_STATE = 128
CONV_K = 4
BLK = 64
MBS = 2
DI = 4096
CH = 4352
E = 8512
SEQ_LEN = 512
BATCH = 4


def draw_lengths(key, part):
    drawn_lengths = jax.random.randint(key, (MBS, BATCH), SEQ_LEN // 4, SEQ_LEN + 1, dtype=jnp.int32)
    return drawn_lengths.at[0, 0].set(SEQ_LEN)


def draw_a_log(key, part):
    uniform_draw = jax.random.uniform(key, (HEADS,), jnp.float32)
    lower_log = jnp.log(2.0 / SEQ_LEN)
    upper_log = jnp.log(0.5)
    return (lower_log + uniform_draw * (upper_log - lower_log)).astype(jnp.float32)


def block_scale(own_key, dims, split, least, largest):
    loudness, own = 1.0, jax.random.fold_in(own_key, 6)
    for position, shards_of in split:
        steps = jnp.exp(jax.random.uniform(jax.random.fold_in(own, position), (shards_of,), jnp.float32, least / len(split), largest / len(split)))
        loudness = loudness * jnp.repeat(steps, dims[position] // shards_of).reshape([-1 if axis == position else 1 for axis in range(len(dims))])
    return loudness


def bell_draw(rng, dims, scale, reach, shards=(), held_as=jnp.bfloat16):
    factor_of = block_scale(rng, dims, shards, -0.22, 0.18) if shards else 1.0
    entries = jax.random.normal(rng, dims, jnp.float32) * scale * factor_of
    return jnp.minimum(jnp.maximum(entries, -reach), reach).astype(held_as)


def setup_inputs(seed: int = 0) -> dict:
    key_of = jax.random.split(jax.random.key(seed), 13)
    hidden = bell_draw(key_of[0], (MBS, BATCH, SEQ_LEN, D), 1.0, 6.0, ((1, 4), (2, 8)))
    cotangent = bell_draw(key_of[1], (MBS, BATCH, SEQ_LEN, D), 1.0, 6.0, ((1, 4), (2, 8)))
    lengths = draw_lengths(jax.random.fold_in(key_of[12], 71), 0)
    norm_gain = jnp.clip(1.0 + 0.1 * jax.random.normal(key_of[3], (D,), jnp.float32), 0.5, 1.5)
    input_weight = bell_draw(key_of[4], (D, E), D ** -0.5, 0.125, ((0, 4),))
    conv_w = bell_draw(key_of[5], (CONV_K, CH), CONV_K ** -0.5, 3.0, (), jnp.float32)
    conv_b = bell_draw(key_of[6], (CH,), 0.5, 3.0, (), jnp.float32)
    dt_bias = jnp.clip(jax.random.uniform(key_of[7], (HEADS,), jnp.float32, -4.0, -2.0), -4.0, -2.0)
    a_log = draw_a_log(jax.random.fold_in(key_of[12], 71), 0)
    d_skip = jnp.clip(jax.random.uniform(key_of[9], (HEADS,), jnp.float32, 0.5, 1.5), 0.5, 1.5)
    gate_gain = jnp.clip(1.0 + 0.1 * jax.random.normal(key_of[10], (DI,), jnp.float32), 0.5, 1.5)
    output_weight = bell_draw(key_of[11], (DI, D), DI ** -0.5, 0.09375, ((0, 4),))
    return {"hidden": hidden, "cotangent": cotangent, "lengths": lengths, "norm_gain": norm_gain, "input_weight": input_weight, "conv_w": conv_w, "conv_b": conv_b, "dt_bias": dt_bias, "a_log": a_log, "d_skip": d_skip, "gate_gain": gate_gain, "output_weight": output_weight}


EPS = 1e-05
EXACT_MATMUL = lax.Precision.HIGHEST

@jax.custom_vjp
def lower_triangle(v):
    return lax.optimization_barrier(v.astype(jnp.bfloat16)).astype(jnp.float32)

@jax.custom_vjp
def lower_triangle_reverse(v):
    return v

def low_keep(v):
    return (lower_triangle(v), None)

def low_pass(kept, grad):
    return (grad,)

def back_keep(v):
    return (v, None)

def back_low(kept, grad):
    return (lower_triangle(grad),)
lower_triangle.defvjp(low_keep, low_pass)
lower_triangle_reverse.defvjp(back_keep, back_low)

def rms_scale(values, gain_vec):
    return values * lax.rsqrt(lax.optimization_barrier(jnp.mean(values * values, axis=-1, keepdims=True)) + EPS) * gain_vec

def conv_front(window, dt_raw, conv_w, conv_b, dt_bias, live_mask):
    length = dt_raw.shape[1]
    pre_act = conv_b + conv_w[0] * window[:, 0:length]
    for offset in range(1, CONV_K):
        pre_act = pre_act + conv_w[offset] * window[:, offset:offset + length]
    activated = jax.nn.silu(pre_act)
    x_seq = activated[:, :, :DI]
    b_in = activated[:, :, DI:DI + N_STATE]
    c_out = activated[:, :, DI + N_STATE:]
    step_size = jax.nn.softplus(dt_raw + dt_bias) * live_mask
    return (x_seq, b_in, c_out, step_size)

def block_log(step_size, a_log):
    return jnp.cumsum(step_size * -jnp.exp(a_log), axis=1)

def block_state(x_seq, b_in, step_size, log_decay):
    seq_rows, length = (step_size.shape[0], step_size.shape[1])
    last_log = log_decay[:, length - 1:, :]
    weighting = jnp.exp(last_log - log_decay) * step_size
    x_heads = x_seq.reshape(seq_rows, length, HEADS, HEAD_DIM) * weighting[:, :, :, None]
    local_state = jnp.einsum('sqhp,sqn->shpn', x_heads, b_in, precision=EXACT_MATMUL)
    return (jnp.exp(last_log[:, 0, :]), local_state)

def ssd_out(x_seq, b_in, c_out, step_size, log_decay, state_in, d_skip):
    seq_rows, length = (step_size.shape[0], step_size.shape[1])
    x_heads = x_seq.reshape(seq_rows, length, HEADS, HEAD_DIM)
    gram_mat = jnp.einsum('stn,skn->stk', c_out, b_in, precision=EXACT_MATMUL)
    by_head = jnp.transpose(log_decay, (0, 2, 1))
    causal = jnp.arange(length)[:, None] >= jnp.arange(length)[None, :]
    spread = by_head[:, :, :, None] - by_head[:, :, None, :]
    kernel = jnp.where(causal, jnp.exp(jnp.where(causal, spread, 0.0)), 0.0) * gram_mat[:, None]
    inputs = x_heads * step_size[:, :, :, None]
    within = jnp.einsum('shtk,skhp->sthp', kernel, inputs, precision=EXACT_MATMUL)
    carried = jnp.einsum('stn,shpn->sthp', c_out, state_in, precision=EXACT_MATMUL) * jnp.exp(log_decay)[:, :, :, None]
    result = within + carried + d_skip[:, None] * x_heads
    return result.reshape(seq_rows, length, DI)

def gate_norm(mixed_out, gate_in, gate_gain):
    return rms_scale(mixed_out * jax.nn.silu(gate_in), gate_gain)

def block(hidden, live_mask, norm_gain, input_weight, conv_w, conv_b, dt_bias, a_log, d_skip, gate_gain, output_weight):
    groups, length = (hidden.shape[0], hidden.shape[1])
    normalized_rows = lower_triangle(rms_scale(hidden, norm_gain))
    projected_rows = lower_triangle_reverse(lower_triangle(jnp.einsum('twy,ya->twa', normalized_rows, input_weight, precision=EXACT_MATMUL)))
    gate_in = projected_rows[:, :, :DI]
    conv_in = projected_rows[:, :, DI:DI + CH]
    dt_raw = projected_rows[:, :, DI + CH:]
    window = jnp.concatenate([jnp.zeros((groups, CONV_K - 1, CH), jnp.float32), conv_in], axis=1)
    x_seq, b_in, c_out, step_size = conv_front(window, dt_raw, conv_w, conv_b, dt_bias, live_mask)
    blocks = length // BLK

    def to_blocks(values):
        return jnp.moveaxis(values.reshape(groups, blocks, BLK, values.shape[-1]), 1, 0)

    def one_block(carry_state, pieces):
        x_part, b_part, c_part, step_part = pieces
        log_decay = block_log(step_part, a_log)
        mixed_part = ssd_out(x_part, b_part, c_part, step_part, log_decay, carry_state, d_skip)
        block_decay, local_state = block_state(x_part, b_part, step_part, log_decay)
        return (block_decay[:, :, None, None] * carry_state + local_state, mixed_part)
    start_state = jnp.zeros((groups, HEADS, HEAD_DIM, N_STATE), jnp.float32)
    final_state, results = lax.scan(jax.checkpoint(one_block), start_state, (to_blocks(x_seq), to_blocks(b_in), to_blocks(c_out), to_blocks(step_size)))
    mixed_out = jnp.moveaxis(results, 0, 1).reshape(groups, length, DI)
    gated_result = lower_triangle(gate_norm(mixed_out, gate_in, gate_gain))
    return jnp.einsum('zyf,fg->zyg', gated_result, output_weight, precision=EXACT_MATMUL) + hidden

def reference(hidden, cotangent, lengths, norm_gain, input_weight, conv_w, conv_b, dt_bias, a_log, d_skip, gate_gain, output_weight):
    seq_total = MBS * BATCH
    group_size = math.gcd(seq_total, max(1, 4096 // SEQ_LEN))
    steps_count = seq_total // group_size
    params = (norm_gain, input_weight.astype(jnp.float32), conv_w, conv_b, dt_bias, a_log, d_skip, gate_gain, output_weight.astype(jnp.float32))
    inputs_all = hidden.astype(jnp.float32).reshape(steps_count, group_size, SEQ_LEN, D)
    cot_all = cotangent.astype(jnp.float32).reshape(steps_count, group_size, SEQ_LEN, D)
    positions = jnp.arange(SEQ_LEN, dtype=jnp.int32)
    live_all = (positions[None, :] < lengths.reshape(seq_total)[:, None]).astype(jnp.float32)
    live_all = live_all.reshape(steps_count, group_size, SEQ_LEN, 1)

    def group_step(totals, pieces):
        source, cot_piece, live_piece = pieces

        def run_block(values, *weights):
            return block(values, live_piece, *weights)
        result, pullback = jax.vjp(run_block, source, *params)
        grads = pullback(cot_piece)
        summed = tuple((total_part + grad_part for total_part, grad_part in zip(totals, grads[1:])))
        return (summed, (result.astype(jnp.bfloat16), grads[0]))
    start_totals = tuple((jnp.zeros(param.shape, jnp.float32) for param in params))
    totals, (results, grad_inputs) = lax.scan(group_step, start_totals, (inputs_all, cot_all, live_all))
    out = results.reshape(MBS, BATCH, SEQ_LEN, D)
    d_hidden = grad_inputs.reshape(MBS, BATCH, SEQ_LEN, D)
    return (out, d_hidden, totals[0], totals[1], totals[2], totals[3], totals[4], totals[5], totals[6], totals[7], totals[8])
```

```python
import functools

import jax
import jax.numpy as jnp
from jax import lax
from jax.experimental import pallas as pl
from jax.experimental.pallas import tpu as pltpu
from jax.sharding import PartitionSpec as P

D = 2048
HEADS = 64
HEAD_DIM = 64
N_STATE = 128
CONV_K = 4
DI = 4096
CH = DI + 2 * N_STATE
LANES = 128
EPS = 1e-05
F32 = jnp.float32
BF16 = jnp.bfloat16
EXACT = lax.Precision.HIGHEST
VMEM_LIMIT = 60 * 1024 * 1024


def dot(a, b, ca=1, cb=0):
    return lax.dot_general(
        a.astype(BF16), b.astype(BF16), (((ca,), (cb,)), ((), ())), preferred_element_type=F32
    )


def dot_exact(a, b):
    return lax.dot_general(
        a, b, (((1,), (0,)), ((), ())), precision=EXACT, preferred_element_type=F32
    )


def to_lanes(per_head, width):
    q = per_head.shape[0]
    low = lax.broadcasted_iota(jnp.int32, (q, LANES), 1) < HEAD_DIM
    pairs = []
    for j in range(width // LANES):
        first = jnp.broadcast_to(per_head[:, 2 * j : 2 * j + 1], (q, LANES))
        second = jnp.broadcast_to(per_head[:, 2 * j + 1 : 2 * j + 2], (q, LANES))
        pairs.append(jnp.where(low, first, second))
    return jnp.concatenate(pairs, axis=1)


def head_sum_matrix(width):
    channel = lax.broadcasted_iota(jnp.int32, (width, LANES), 0) // HEAD_DIM
    return (channel == lax.broadcasted_iota(jnp.int32, (width, LANES), 1)).astype(F32)


def split_heads(pair):
    low = lax.broadcasted_iota(jnp.int32, pair.shape, 1) < HEAD_DIM
    zero = jnp.zeros_like(pair)
    return jnp.concatenate([jnp.where(low, pair, zero), jnp.where(low, zero, pair)], axis=0)


def triangle(q, lower):
    rows = lax.broadcasted_iota(jnp.int32, (q, q), 0)
    cols = lax.broadcasted_iota(jnp.int32, (q, q), 1)
    return (rows >= cols) if lower else (rows <= cols)


def softplus(z):
    return jnp.maximum(z, 0.0) + jnp.log(1.0 + jnp.exp(-jnp.abs(z)))


def live_column(lengths_ref, s, chunk, q):
    slots = chunk * q + lax.broadcasted_iota(jnp.int32, (q, LANES), 0)
    return (slots < lengths_ref[s]).astype(F32)


def decays(dt_raw, bias, rate, live):
    q = dt_raw.shape[0]
    z = dt_raw + bias
    step = softplus(z) * live
    cum = dot_exact(triangle(q, True).astype(F32), step * rate)
    return z, step, cum


def forward_kernel(
    cw, lengths, proj, conv_w, heads_par, chan_par, grad_gated, mixed_out, pre_out, state_out,
    stats_out, window, state,
):
    chunk = pl.program_id(0)
    seqs = proj.shape[1]
    q = proj.shape[0] * proj.shape[2]
    cc = cw + 2 * N_STATE
    causal = triangle(q, True)

    @pl.when(chunk == 0)
    def _():
        window[...] = jnp.zeros_like(window)
        state[...] = jnp.zeros_like(state)

    for s in range(seqs):
        rows = proj[:, s].reshape(q, proj.shape[3])
        gate = rows[:, :cw].astype(F32)
        window[s, 8 : 8 + q, :] = rows[:, cw : cw + cc].astype(F32)
        pre = conv_w[CONV_K : CONV_K + 1, :] + conv_w[0:1, :] * window[s, 5 : 5 + q, :]
        for k in range(1, CONV_K):
            pre = pre + conv_w[k : k + 1, :] * window[s, 5 + k : 5 + k + q, :]
        window[s, 0:8, :] = window[s, q : q + 8, :]
        pre_out[0, s] = pre
        act = pre * jax.nn.sigmoid(pre)
        x = act[:, :cw]
        b = act[:, cw : cw + N_STATE]
        c = act[:, cw + N_STATE :]
        live = live_column(lengths, s, chunk, q)
        _, step, cum = decays(
            rows[:, cw + cc :].astype(F32), heads_par[0:1, :], heads_par[1:2, :], live
        )
        cum_t = cum.T
        last = cum[q - 1 : q, :]
        u = x * to_lanes(step, cw)
        gram = dot(c, b, 1, 1)
        within = []
        for j in range(cw // LANES):
            kernels = []
            for h in (2 * j, 2 * j + 1):
                spread = jnp.where(causal, cum[:, h : h + 1] - cum_t[h : h + 1, :], -1e30)
                kernels.append((gram * jnp.exp(spread)).astype(BF16))
            both = jnp.concatenate(kernels, axis=1)
            within.append(dot(both, split_heads(u[:, j * LANES : (j + 1) * LANES])))
        before = state[s]
        state_out[0, s] = before
        mixed = (
            jnp.concatenate(within, axis=1)
            + dot(c, before) * to_lanes(jnp.exp(cum), cw)
            + chan_par[0:1, :] * x
        )
        mixed_out[0, s] = mixed
        left = to_lanes(jnp.exp(last - cum), cw)
        state[s] = before * to_lanes(jnp.exp(last), cw) + dot(b, left * u, 0, 0)
        g = mixed * gate * jax.nn.sigmoid(gate)
        gg = grad_gated[:, s].reshape(q, cw)
        ones = jnp.ones((8, cw), F32)
        first = lax.dot_general(
            ones, g * g, (((1,), (1,)), ((), ())), precision=EXACT, preferred_element_type=F32
        )
        second = lax.dot_general(
            ones, gg * chan_par[1:2, :] * g, (((1,), (1,)), ((), ())), precision=EXACT,
            preferred_element_type=F32,
        )
        stats_out[0, s, 0:1, :] = first[0:1, :]
        stats_out[0, s, 1:2, :] = second[0:1, :]


def backward_kernel(
    cw, chunks, lengths, proj, conv_w, heads_par, chan_par, grad_gated, mixed_in, pre_in, state_in,
    scale_in, dproj_out, dconv_out, dheads_out, dchan_out, window, state_grad,
):
    step_id = pl.program_id(0)
    chunk = chunks - 1 - step_id
    seqs = proj.shape[1]
    q = proj.shape[0] * proj.shape[2]
    blocks = proj.shape[0]
    cc = cw + 2 * N_STATE
    causal = triangle(q, True)
    sums = head_sum_matrix(cw)

    @pl.when(step_id == 0)
    def _():
        window[...] = jnp.zeros_like(window)
        state_grad[...] = jnp.zeros_like(state_grad)
        dconv_out[...] = jnp.zeros_like(dconv_out)
        dheads_out[...] = jnp.zeros_like(dheads_out)
        dchan_out[...] = jnp.zeros_like(dchan_out)

    for s in range(seqs):
        rows = proj[:, s].reshape(q, proj.shape[3])
        gate = rows[:, :cw].astype(F32)
        conv_in = rows[:, cw : cw + cc].astype(F32)
        pre = pre_in[0, s]
        mixed = mixed_in[0, s]
        gg = grad_gated[:, s].reshape(q, cw)
        scale = jnp.concatenate(
            [jnp.broadcast_to(scale_in[0, s, 0:1, :], (LANES, q)).T] * (cw // LANES), axis=1
        )
        pull = jnp.concatenate(
            [jnp.broadcast_to(scale_in[0, s, 1:2, :], (LANES, q)).T] * (cw // LANES), axis=1
        )
        sig = jax.nn.sigmoid(gate)
        silu = gate * sig
        g = mixed * silu
        dchan_out[1:2, :] += jnp.sum(gg * g * scale, axis=0, keepdims=True)
        dg = scale * (gg * chan_par[1:2, :] - g * pull)
        gm = dg * silu
        dgate = dg * mixed * (sig * (1.0 + gate * (1.0 - sig)))
        sig_pre = jax.nn.sigmoid(pre)
        act = pre * sig_pre
        x = act[:, :cw]
        b = act[:, cw : cw + N_STATE]
        c = act[:, cw + N_STATE :]
        live = live_column(lengths, s, chunk, q)
        z, step, cum = decays(
            rows[:, cw + cc :].astype(F32), heads_par[0:1, :], heads_par[1:2, :], live
        )
        cum_t = cum.T
        last = cum[q - 1 : q, :]
        step_l = to_lanes(step, cw)
        u = x * step_l
        gram = dot(c, b, 1, 1)
        dchan_out[0:1, :] += jnp.sum(gm * x, axis=0, keepdims=True)
        du = []
        dgram = jnp.zeros((q, q), F32)
        for j in range(cw // LANES):
            at = slice(j * LANES, (j + 1) * LANES)
            dkernels = dot(gm[:, at], split_heads(u[:, at]), 1, 1)
            kernels = []
            for i in range(2):
                h = 2 * j + i
                spread = jnp.where(causal, cum[:, h : h + 1] - cum_t[h : h + 1, :], -1e30)
                decay = jnp.exp(spread)
                dgram = dgram + dkernels[:, i * q : (i + 1) * q] * decay
                kernels.append((gram * decay).astype(BF16))
            both = jnp.concatenate(kernels, axis=0)
            du.append(dot(both, split_heads(gm[:, at]), 0, 0))
        before = state_in[0, s]
        after_grad = state_grad[s]
        v = gm * to_lanes(jnp.exp(cum), cw)
        left = to_lanes(jnp.exp(last - cum), cw)
        du_state = left * dot(b, after_grad)
        du = jnp.concatenate(du, axis=1) + du_state
        dc = dot(dgram, b) + dot(v, before, 1, 1)
        db = dot(dgram, c, 0, 0) + dot(left * u, after_grad, 1, 1)
        end = to_lanes(jnp.exp(last), cw)
        extra = jnp.sum(u * du_state, axis=0, keepdims=True) + end * jnp.sum(
            after_grad * before, axis=0, keepdims=True
        )
        state_grad[s] = end * after_grad + dot(c, v, 0, 0)
        last_row = (lax.broadcasted_iota(jnp.int32, (q, LANES), 0) == q - 1).astype(F32)
        dcum = dot_exact(gm * (mixed - chan_par[0:1, :] * x) - u * du, sums) + last_row * dot_exact(
            jnp.broadcast_to(extra, (8, cw)), sums
        )[0:1, :]
        dlog = dot_exact(triangle(q, False).astype(F32), dcum)
        rate = heads_par[1:2, :]
        dstep = dot_exact(x * du, sums) + dlog * rate
        dheads_out[1:2, :] += jnp.sum(dlog * step * rate, axis=0, keepdims=True)
        dz = dstep * live * jax.nn.sigmoid(z)
        dheads_out[0:1, :] += jnp.sum(dz, axis=0, keepdims=True)
        dx = step_l * du + chan_par[0:1, :] * gm
        dpre = jnp.concatenate([dx, db, dc], axis=1) * (sig_pre * (1.0 + pre * (1.0 - sig_pre)))
        window[s, 0:q, :] = dpre
        dconv_in = jnp.zeros((q, cc), F32)
        for k in range(CONV_K):
            ahead = CONV_K - 1 - k
            moved = window[s, ahead : ahead + q, :]
            dconv_in = dconv_in + conv_w[k : k + 1, :] * moved
            dconv_out[k : k + 1, :] += jnp.sum(conv_in * moved, axis=0, keepdims=True)
        dconv_out[CONV_K : CONV_K + 1, :] += jnp.sum(dpre, axis=0, keepdims=True)
        window[s, q : q + 8, :] = window[s, 0:8, :]
        dproj_out[:, s, :, :cw] = dgate.astype(BF16).reshape(blocks, q // blocks, cw)
        dproj_out[:, s, :, cw : cw + cc] = dconv_in.astype(BF16).reshape(blocks, q // blocks, cc)
        dproj_out[:, s, :, cw + cc :] = dz.astype(BF16).reshape(blocks, q // blocks, LANES)


def call_forward(cw, per, lengths, proj, conv_w, heads_par, chan_par, grad_gated):
    nc, seqs, length, cols = proj.shape
    chunks, q, cc = nc // per, per * length, cw + 2 * N_STATE
    whole = lambda a: pl.BlockSpec(a.shape, lambda i: (0,) * a.ndim)
    by_chunk = lambda n: pl.BlockSpec((1, seqs, n[0], n[1]), lambda i: (i, 0, 0, 0))
    tokens = lambda n: pl.BlockSpec((per, seqs, length, n), lambda i: (i, 0, 0, 0))
    return pl.pallas_call(
        functools.partial(forward_kernel, cw),
        grid=(chunks,),
        in_specs=[
            pl.BlockSpec(memory_space=pltpu.SMEM),
            tokens(cols),
            whole(conv_w),
            whole(heads_par),
            whole(chan_par),
            tokens(cw),
        ],
        out_specs=[
            by_chunk((q, cw)),
            by_chunk((q, cc)),
            by_chunk((N_STATE, cw)),
            by_chunk((8, q)),
        ],
        out_shape=[
            jax.ShapeDtypeStruct((chunks, seqs, q, cw), F32),
            jax.ShapeDtypeStruct((chunks, seqs, q, cc), F32),
            jax.ShapeDtypeStruct((chunks, seqs, N_STATE, cw), F32),
            jax.ShapeDtypeStruct((chunks, seqs, 8, q), F32),
        ],
        scratch_shapes=[
            pltpu.VMEM((seqs, q + 8, cc), F32),
            pltpu.VMEM((seqs, N_STATE, cw), F32),
        ],
        compiler_params=pltpu.CompilerParams(vmem_limit_bytes=VMEM_LIMIT),
        name="mixer_forward",
    )(lengths, proj, conv_w, heads_par, chan_par, grad_gated)


def call_backward(
    cw, per, lengths, proj, conv_w, heads_par, chan_par, grad_gated, mixed, pre, states, scales
):
    nc, seqs, length, cols = proj.shape
    chunks, q, cc = nc // per, per * length, cw + 2 * N_STATE
    whole = lambda shape: pl.BlockSpec(shape, lambda i: (0,) * len(shape))
    by_chunk = lambda n: pl.BlockSpec((1, seqs, n[0], n[1]), lambda i: (chunks - 1 - i, 0, 0, 0))
    tokens = lambda n: pl.BlockSpec(
        (per, seqs, length, n), lambda i: (chunks - 1 - i, 0, 0, 0)
    )
    return pl.pallas_call(
        functools.partial(backward_kernel, cw, chunks),
        grid=(chunks,),
        in_specs=[
            pl.BlockSpec(memory_space=pltpu.SMEM),
            tokens(cols),
            whole(conv_w.shape),
            whole(heads_par.shape),
            whole(chan_par.shape),
            tokens(cw),
            by_chunk((q, cw)),
            by_chunk((q, cc)),
            by_chunk((N_STATE, cw)),
            by_chunk((8, q)),
        ],
        out_specs=[
            tokens(cols),
            whole((8, cc)),
            whole((8, LANES)),
            whole((8, cw)),
        ],
        out_shape=[
            jax.ShapeDtypeStruct(proj.shape, BF16),
            jax.ShapeDtypeStruct((8, cc), F32),
            jax.ShapeDtypeStruct((8, LANES), F32),
            jax.ShapeDtypeStruct((8, cw), F32),
        ],
        scratch_shapes=[
            pltpu.VMEM((seqs, q + 8, cc), F32),
            pltpu.VMEM((seqs, N_STATE, cw), F32),
        ],
        compiler_params=pltpu.CompilerParams(vmem_limit_bytes=VMEM_LIMIT),
        name="mixer_backward",
    )(lengths, proj, conv_w, heads_par, chan_par, grad_gated, mixed, pre, states, scales)


def rms_scale(values, gain_vec):
    return values * lax.rsqrt(jnp.mean(values * values, axis=-1, keepdims=True) + EPS) * gain_vec


def local(
    hidden,
    cotangent,
    lengths,
    norm_gain,
    input_weight,
    conv_w,
    conv_b,
    dt_bias,
    a_log,
    d_skip,
    gate_gain,
    output_weight,
):
    nc, nf = lax.axis_size("ctx"), lax.axis_size("fsdp")
    me_c, me_f = lax.axis_index("ctx"), lax.axis_index("fsdp")
    mb_count, seq_rows, length = hidden.shape[0], hidden.shape[1], hidden.shape[2]
    seqs = mb_count * seq_rows
    mine = seqs * length
    heads = HEADS // nc
    cw = DI // nc
    cc = cw + 2 * N_STATE
    per = 2 if nc % 2 == 0 else 1
    q = per * length
    chunks = nc // per

    source = hidden.astype(F32).reshape(seqs, length, D)
    normed = rms_scale(source, norm_gain).astype(BF16)
    normed_all = lax.all_gather(normed, "ctx").reshape(nc * mine, D)
    cot = cotangent.reshape(seqs, length, D)
    cot_all = lax.all_gather(cot, "ctx").reshape(nc * mine, D)

    cut = lambda a, start, size, axis: lax.dynamic_slice_in_dim(a, start, size, axis)

    def my_columns(a, axis):
        return jnp.concatenate(
            [cut(a, cw * me_c, cw, axis), lax.slice_in_dim(a, DI, CH, axis=axis)], axis=axis
        )

    in_rows = jnp.concatenate(
        [
            cut(input_weight, cw * me_c, cw, 1),
            cut(input_weight, DI + cw * me_c, cw, 1),
            input_weight[:, 2 * DI : 2 * DI + 2 * N_STATE],
            jnp.pad(
                cut(input_weight, DI + CH + heads * me_c, heads, 1), ((0, 0), (0, LANES - heads))
            ),
        ],
        axis=1,
    )
    in_w = lax.all_gather(in_rows, "fsdp", axis=0, tiled=True)
    shard = output_weight.shape[0]
    offset = cw * me_c - shard * me_f
    held = jnp.logical_and(offset >= 0, offset < shard)
    part = cut(output_weight, jnp.clip(offset, 0, shard - cw), cw, 0)
    out_w = lax.psum(jnp.where(held, part, jnp.zeros_like(part)), "fsdp")

    conv_par = jnp.concatenate(
        [my_columns(conv_w, 1), my_columns(conv_b[None], 1), jnp.zeros((3, cc), F32)], axis=0
    )
    per_head = lambda a: cut(a, heads * me_c, heads, 0)
    pad_heads = lambda a: jnp.pad(a, (0, LANES - heads))[None]
    rate = -jnp.exp(per_head(a_log))
    heads_par = jnp.concatenate(
        [pad_heads(per_head(dt_bias)), pad_heads(rate), jnp.zeros((6, LANES), F32)], axis=0
    )
    chan_par = jnp.concatenate(
        [
            jnp.repeat(per_head(d_skip), HEAD_DIM)[None],
            cut(gate_gain, cw * me_c, cw, 0)[None],
            jnp.zeros((6, cw), F32),
        ],
        axis=0,
    )
    seq_lengths = lengths.reshape(seqs)

    proj = dot(normed_all, in_w).astype(BF16).reshape(nc, seqs, length, -1)
    grad_gated = dot(cot_all, out_w, 1, 1).reshape(nc, seqs, length, cw)
    mixed, pre, states, stats = call_forward(
        cw, per, seq_lengths, proj, conv_par, heads_par, chan_par, grad_gated
    )
    totals = lax.psum(stats[:, :, 0:2], "ctx") / DI
    scale = lax.rsqrt(totals[:, :, 0] + EPS)
    pull = scale * scale * totals[:, :, 1]
    scales = jnp.pad(jnp.stack([scale, pull], axis=2), ((0, 0), (0, 0), (0, 6), (0, 0)))

    by_chunk = lambda a: jnp.moveaxis(
        a.reshape(chunks, seqs, per, length, a.shape[-1]), 2, 1
    ).reshape(nc, seqs, length, a.shape[-1])
    gate = proj[..., :cw].astype(F32)
    g = by_chunk(mixed) * jax.nn.silu(gate)
    gated = (g * by_chunk(scale[..., None]) * chan_par[1]).astype(BF16).reshape(nc * mine, cw)
    branch = dot(gated, out_w).astype(BF16).reshape(nc, mine, D)
    out = lax.psum_scatter(branch, "ctx", scatter_dimension=0).astype(F32) + source.reshape(mine, D)
    grad_out = lax.psum_scatter(
        dot(gated, cot_all, 0, 0).astype(BF16), "fsdp", scatter_dimension=0, tiled=True
    ).astype(F32)

    dproj, dconv, dheads, dchan = call_backward(
        cw, per, seq_lengths, proj, conv_par, heads_par, chan_par, grad_gated, mixed, pre, states,
        scales,
    )
    dproj = dproj.reshape(nc * mine, -1)
    dnormed = dot(dproj, in_w, 1, 1).astype(BF16).reshape(nc, mine, D)
    dnormed = lax.psum_scatter(dnormed, "ctx", scatter_dimension=0).astype(F32)
    _, norm_pull = jax.vjp(rms_scale, source, norm_gain)
    dsource, dnorm_gain = norm_pull(dnormed.reshape(seqs, length, D))
    d_hidden = dsource + cot.astype(F32)

    rows = D // (nc * nf)
    partial = dot(normed_all, dproj, 0, 0).astype(BF16).reshape(nc, nf, rows, -1)
    partial = lax.psum_scatter(partial, "fsdp", scatter_dimension=1)
    pieces = lax.all_to_all(partial, "ctx", split_axis=0, concat_axis=0, tiled=True)
    side = lambda a: jnp.moveaxis(a, 0, 1).reshape(rows, -1)
    grad_in = jnp.concatenate(
        [
            side(pieces[:, :, :cw]),
            side(pieces[:, :, cw : 2 * cw]),
            jnp.sum(pieces[:, :, 2 * cw : 2 * cw + 2 * N_STATE].astype(F32), axis=0).astype(BF16),
            side(pieces[:, :, 2 * cw + 2 * N_STATE : 2 * cw + 2 * N_STATE + heads]),
        ],
        axis=1,
    ).astype(F32)

    place = lambda a, start, size: lax.dynamic_update_slice_in_dim(
        jnp.zeros(a.shape[:-1] + (size,), F32), a, start, a.ndim - 1
    )
    dconv = jnp.concatenate(
        [place(dconv[: CONV_K + 1, :cw], cw * me_c, DI), dconv[: CONV_K + 1, cw:]], axis=1
    )
    dskip = jnp.sum(dchan[0].reshape(heads, HEAD_DIM), axis=1)
    small = (
        dnorm_gain,
        dconv,
        place(dheads[0, :heads], heads * me_c, HEADS),
        place(dheads[1, :heads], heads * me_c, HEADS),
        place(dskip, heads * me_c, HEADS),
        place(dchan[1], cw * me_c, DI),
    )
    dnorm_gain, dconv, dbias, dalog, dskip, dgain = lax.psum(small, ("ctx", "fsdp"))
    shape = hidden.shape
    return (
        out.astype(BF16).reshape(shape),
        d_hidden.reshape(shape),
        dnorm_gain,
        grad_in,
        dconv[:CONV_K],
        dconv[CONV_K],
        dbias,
        dalog,
        dskip,
        dgain,
        grad_out,
    )


def solution(mesh):
    tokens, rows, every = P(None, "fsdp", "ctx", None), P("fsdp", None), P()
    spread = P(("ctx", "fsdp"), None)
    in_specs = (
        tokens, tokens, P(None, "fsdp"), every, rows, every, every, every, every, every, every, rows,
    )
    out_specs = (
        tokens, tokens, every, spread, every, every, every, every, every, every, spread,
    )
    return jax.shard_map(local, mesh=mesh, in_specs=in_specs, out_specs=out_specs, check_vma=False)
```

```python
import functools

import jax
import jax.numpy as jnp
from jax import lax
from jax.experimental import pallas as pl
from jax.experimental.pallas import tpu as pltpu
from jax.sharding import PartitionSpec as P

D = 2048
HEADS = 64
HEAD_DIM = 64
N_STATE = 128
CONV_K = 4
DI = 4096
CH = DI + 2 * N_STATE
LANES = 128
EPS = 1e-05
F32 = jnp.float32
BF16 = jnp.bfloat16
EXACT = lax.Precision.HIGHEST
VMEM_LIMIT = 60 * 1024 * 1024


def dot(a, b, ca=1, cb=0):
    return lax.dot_general(
        a.astype(BF16), b.astype(BF16), (((ca,), (cb,)), ((), ())), preferred_element_type=F32
    )


def dot_exact(a, b):
    return lax.dot_general(
        a, b, (((1,), (0,)), ((), ())), precision=EXACT, preferred_element_type=F32
    )


def to_lanes(per_head, width):
    q = per_head.shape[0]
    low = lax.broadcasted_iota(jnp.int32, (q, LANES), 1) < HEAD_DIM
    pairs = []
    for j in range(width // LANES):
        first = jnp.broadcast_to(per_head[:, 2 * j : 2 * j + 1], (q, LANES))
        second = jnp.broadcast_to(per_head[:, 2 * j + 1 : 2 * j + 2], (q, LANES))
        pairs.append(jnp.where(low, first, second))
    return jnp.concatenate(pairs, axis=1)


def head_sum_matrix(width):
    channel = lax.broadcasted_iota(jnp.int32, (width, LANES), 0) // HEAD_DIM
    return (channel == lax.broadcasted_iota(jnp.int32, (width, LANES), 1)).astype(F32)


def split_heads(pair):
    low = lax.broadcasted_iota(jnp.int32, pair.shape, 1) < HEAD_DIM
    zero = jnp.zeros_like(pair)
    return jnp.concatenate([jnp.where(low, pair, zero), jnp.where(low, zero, pair)], axis=0)


def triangle(q, lower):
    rows = lax.broadcasted_iota(jnp.int32, (q, q), 0)
    cols = lax.broadcasted_iota(jnp.int32, (q, q), 1)
    return (rows >= cols) if lower else (rows <= cols)


def softplus(z):
    return jnp.maximum(z, 0.0) + jnp.log(1.0 + jnp.exp(-jnp.abs(z)))


def live_column(lengths_ref, s, chunk, q):
    slots = chunk * q + lax.broadcasted_iota(jnp.int32, (q, LANES), 0)
    return (slots < lengths_ref[s]).astype(F32)


def decays(dt_raw, bias, rate, live):
    q = dt_raw.shape[0]
    z = dt_raw + bias
    step = softplus(z) * live
    cum = dot_exact(triangle(q, True).astype(F32), step * rate)
    return z, step, cum


def forward_kernel(
    cw, lengths, proj, conv_w, heads_par, chan_par, grad_gated, mixed_out, pre_out, state_out,
    stats_out, window, state,
):
    chunk = pl.program_id(0)
    seqs = proj.shape[1]
    q = proj.shape[0] * proj.shape[2]
    cc = cw + 2 * N_STATE
    causal = triangle(q, True)

    @pl.when(chunk == 0)
    def _():
        window[...] = jnp.zeros_like(window)
        state[...] = jnp.zeros_like(state)

    for s in range(seqs):
        rows = proj[:, s].reshape(q, proj.shape[3])
        gate = rows[:, :cw].astype(F32)
        window[s, 8 : 8 + q, :] = rows[:, cw : cw + cc].astype(F32)
        pre = conv_w[CONV_K : CONV_K + 1, :] + conv_w[0:1, :] * window[s, 5 : 5 + q, :]
        for k in range(1, CONV_K):
            pre = pre + conv_w[k : k + 1, :] * window[s, 5 + k : 5 + k + q, :]
        window[s, 0:8, :] = window[s, q : q + 8, :]
        pre_out[0, s] = pre
        act = pre * jax.nn.sigmoid(pre)
        x = act[:, :cw]
        b = act[:, cw : cw + N_STATE]
        c = act[:, cw + N_STATE :]
        live = live_column(lengths, s, chunk, q)
        _, step, cum = decays(
            rows[:, cw + cc :].astype(F32), heads_par[0:1, :], heads_par[1:2, :], live
        )
        cum_t = cum.T
        last = cum[q - 1 : q, :]
        u = x * to_lanes(step, cw)
        gram = dot(c, b, 1, 1)
        within = []
        for j in range(cw // LANES):
            kernels = []
            for h in (2 * j, 2 * j + 1):
                spread = jnp.where(causal, cum[:, h : h + 1] - cum_t[h : h + 1, :], -1e30)
                kernels.append((gram * jnp.exp(spread)).astype(BF16))
            both = jnp.concatenate(kernels, axis=1)
            within.append(dot(both, split_heads(u[:, j * LANES : (j + 1) * LANES])))
        before = state[s]
        state_out[0, s] = before
        mixed = (
            jnp.concatenate(within, axis=1)
            + dot(c, before) * to_lanes(jnp.exp(cum), cw)
            + chan_par[0:1, :] * x
        )
        mixed_out[0, s] = mixed
        left = to_lanes(jnp.exp(last - cum), cw)
        state[s] = before * to_lanes(jnp.exp(last), cw) + dot(b, left * u, 0, 0)
        g = mixed * gate * jax.nn.sigmoid(gate)
        gg = grad_gated[:, s].reshape(q, cw)
        ones = jnp.ones((8, cw), F32)
        first = lax.dot_general(
            ones, g * g, (((1,), (1,)), ((), ())), precision=EXACT, preferred_element_type=F32
        )
        second = lax.dot_general(
            ones, gg * chan_par[1:2, :] * g, (((1,), (1,)), ((), ())), precision=EXACT,
            preferred_element_type=F32,
        )
        stats_out[0, s, 0:1, :] = first[0:1, :]
        stats_out[0, s, 1:2, :] = second[0:1, :]


def backward_kernel(
    cw, chunks, lengths, proj, conv_w, heads_par, chan_par, grad_gated, mixed_in, pre_in, state_in,
    scale_in, dproj_out, dconv_out, dheads_out, dchan_out, window, state_grad,
):
    step_id = pl.program_id(0)
    chunk = chunks - 1 - step_id
    seqs = proj.shape[1]
    q = proj.shape[0] * proj.shape[2]
    blocks = proj.shape[0]
    cc = cw + 2 * N_STATE
    causal = triangle(q, True)
    sums = head_sum_matrix(cw)

    @pl.when(step_id == 0)
    def _():
        window[...] = jnp.zeros_like(window)
        state_grad[...] = jnp.zeros_like(state_grad)
        dconv_out[...] = jnp.zeros_like(dconv_out)
        dheads_out[...] = jnp.zeros_like(dheads_out)
        dchan_out[...] = jnp.zeros_like(dchan_out)

    for s in range(seqs):
        rows = proj[:, s].reshape(q, proj.shape[3])
        gate = rows[:, :cw].astype(F32)
        conv_in = rows[:, cw : cw + cc].astype(F32)
        pre = pre_in[0, s]
        mixed = mixed_in[0, s]
        gg = grad_gated[:, s].reshape(q, cw)
        scale = jnp.concatenate(
            [jnp.broadcast_to(scale_in[0, s, 0:1, :], (LANES, q)).T] * (cw // LANES), axis=1
        )
        pull = jnp.concatenate(
            [jnp.broadcast_to(scale_in[0, s, 1:2, :], (LANES, q)).T] * (cw // LANES), axis=1
        )
        sig = jax.nn.sigmoid(gate)
        silu = gate * sig
        g = mixed * silu
        dchan_out[1:2, :] += jnp.sum(gg * g * scale, axis=0, keepdims=True)
        dg = scale * (gg * chan_par[1:2, :] - g * pull)
        gm = dg * silu
        dgate = dg * mixed * (sig * (1.0 + gate * (1.0 - sig)))
        sig_pre = jax.nn.sigmoid(pre)
        act = pre * sig_pre
        x = act[:, :cw]
        b = act[:, cw : cw + N_STATE]
        c = act[:, cw + N_STATE :]
        live = live_column(lengths, s, chunk, q)
        z, step, cum = decays(
            rows[:, cw + cc :].astype(F32), heads_par[0:1, :], heads_par[1:2, :], live
        )
        cum_t = cum.T
        last = cum[q - 1 : q, :]
        step_l = to_lanes(step, cw)
        u = x * step_l
        gram = dot(c, b, 1, 1)
        dchan_out[0:1, :] += jnp.sum(gm * x, axis=0, keepdims=True)
        du = []
        dgram = jnp.zeros((q, q), F32)
        for j in range(cw // LANES):
            at = slice(j * LANES, (j + 1) * LANES)
            dkernels = dot(gm[:, at], split_heads(u[:, at]), 1, 1)
            kernels = []
            for i in range(2):
                h = 2 * j + i
                spread = jnp.where(causal, cum[:, h : h + 1] - cum_t[h : h + 1, :], -1e30)
                decay = jnp.exp(spread)
                dgram = dgram + dkernels[:, i * q : (i + 1) * q] * decay
                kernels.append((gram * decay).astype(BF16))
            both = jnp.concatenate(kernels, axis=0)
            du.append(dot(both, split_heads(gm[:, at]), 0, 0))
        before = state_in[0, s]
        after_grad = state_grad[s]
        v = gm * to_lanes(jnp.exp(cum), cw)
        left = to_lanes(jnp.exp(last - cum), cw)
        du_state = left * dot(b, after_grad)
        du = jnp.concatenate(du, axis=1) + du_state
        dc = dot(dgram, b) + dot(v, before, 1, 1)
        db = dot(dgram, c, 0, 0) + dot(left * u, after_grad, 1, 1)
        end = to_lanes(jnp.exp(last), cw)
        extra = jnp.sum(u * du_state, axis=0, keepdims=True) + end * jnp.sum(
            after_grad * before, axis=0, keepdims=True
        )
        state_grad[s] = end * after_grad + dot(c, v, 0, 0)
        last_row = (lax.broadcasted_iota(jnp.int32, (q, LANES), 0) == q - 1).astype(F32)
        dcum = dot_exact(gm * (mixed - chan_par[0:1, :] * x) - u * du, sums) + last_row * dot_exact(
            jnp.broadcast_to(extra, (8, cw)), sums
        )[0:1, :]
        dlog = dot_exact(triangle(q, False).astype(F32), dcum)
        rate = heads_par[1:2, :]
        dstep = dot_exact(x * du, sums) + dlog * rate
        dheads_out[1:2, :] += jnp.sum(dlog * step * rate, axis=0, keepdims=True)
        dz = dstep * live * jax.nn.sigmoid(z)
        dheads_out[0:1, :] += jnp.sum(dz, axis=0, keepdims=True)
        dx = step_l * du + chan_par[0:1, :] * gm
        dpre = jnp.concatenate([dx, db, dc], axis=1) * (sig_pre * (1.0 + pre * (1.0 - sig_pre)))
        window[s, 0:q, :] = dpre
        dconv_in = jnp.zeros((q, cc), F32)
        for k in range(CONV_K):
            ahead = CONV_K - 1 - k
            moved = window[s, ahead : ahead + q, :]
            dconv_in = dconv_in + conv_w[k : k + 1, :] * moved
            dconv_out[k : k + 1, :] += jnp.sum(conv_in * moved, axis=0, keepdims=True)
        dconv_out[CONV_K : CONV_K + 1, :] += jnp.sum(dpre, axis=0, keepdims=True)
        window[s, q : q + 8, :] = window[s, 0:8, :]
        dproj_out[:, s, :, :cw] = dgate.astype(BF16).reshape(blocks, q // blocks, cw)
        dproj_out[:, s, :, cw : cw + cc] = dconv_in.astype(BF16).reshape(blocks, q // blocks, cc)
        dproj_out[:, s, :, cw + cc :] = dz.astype(BF16).reshape(blocks, q // blocks, LANES)


def call_forward(cw, per, lengths, proj, conv_w, heads_par, chan_par, grad_gated):
    nc, seqs, length, cols = proj.shape
    chunks, q, cc = nc // per, per * length, cw + 2 * N_STATE
    whole = lambda a: pl.BlockSpec(a.shape, lambda i: (0,) * a.ndim)
    by_chunk = lambda n: pl.BlockSpec((1, seqs, n[0], n[1]), lambda i: (i, 0, 0, 0))
    tokens = lambda n: pl.BlockSpec((per, seqs, length, n), lambda i: (i, 0, 0, 0))
    return pl.pallas_call(
        functools.partial(forward_kernel, cw),
        grid=(chunks,),
        in_specs=[
            pl.BlockSpec(memory_space=pltpu.SMEM),
            tokens(cols),
            whole(conv_w),
            whole(heads_par),
            whole(chan_par),
            tokens(cw),
        ],
        out_specs=[
            by_chunk((q, cw)),
            by_chunk((q, cc)),
            by_chunk((N_STATE, cw)),
            by_chunk((8, q)),
        ],
        out_shape=[
            jax.ShapeDtypeStruct((chunks, seqs, q, cw), F32),
            jax.ShapeDtypeStruct((chunks, seqs, q, cc), F32),
            jax.ShapeDtypeStruct((chunks, seqs, N_STATE, cw), F32),
            jax.ShapeDtypeStruct((chunks, seqs, 8, q), F32),
        ],
        scratch_shapes=[
            pltpu.VMEM((seqs, q + 8, cc), F32),
            pltpu.VMEM((seqs, N_STATE, cw), F32),
        ],
        compiler_params=pltpu.CompilerParams(vmem_limit_bytes=VMEM_LIMIT),
        name="mixer_forward",
    )(lengths, proj, conv_w, heads_par, chan_par, grad_gated)


def call_backward(
    cw, per, lengths, proj, conv_w, heads_par, chan_par, grad_gated, mixed, pre, states, scales
):
    nc, seqs, length, cols = proj.shape
    chunks, q, cc = nc // per, per * length, cw + 2 * N_STATE
    whole = lambda shape: pl.BlockSpec(shape, lambda i: (0,) * len(shape))
    by_chunk = lambda n: pl.BlockSpec((1, seqs, n[0], n[1]), lambda i: (chunks - 1 - i, 0, 0, 0))
    tokens = lambda n: pl.BlockSpec(
        (per, seqs, length, n), lambda i: (chunks - 1 - i, 0, 0, 0)
    )
    return pl.pallas_call(
        functools.partial(backward_kernel, cw, chunks),
        grid=(chunks,),
        in_specs=[
            pl.BlockSpec(memory_space=pltpu.SMEM),
            tokens(cols),
            whole(conv_w.shape),
            whole(heads_par.shape),
            whole(chan_par.shape),
            tokens(cw),
            by_chunk((q, cw)),
            by_chunk((q, cc)),
            by_chunk((N_STATE, cw)),
            by_chunk((8, q)),
        ],
        out_specs=[
            tokens(cols),
            whole((8, cc)),
            whole((8, LANES)),
            whole((8, cw)),
        ],
        out_shape=[
            jax.ShapeDtypeStruct(proj.shape, BF16),
            jax.ShapeDtypeStruct((8, cc), F32),
            jax.ShapeDtypeStruct((8, LANES), F32),
            jax.ShapeDtypeStruct((8, cw), F32),
        ],
        scratch_shapes=[
            pltpu.VMEM((seqs, q + 8, cc), F32),
            pltpu.VMEM((seqs, N_STATE, cw), F32),
        ],
        compiler_params=pltpu.CompilerParams(vmem_limit_bytes=VMEM_LIMIT),
        name="mixer_backward",
    )(lengths, proj, conv_w, heads_par, chan_par, grad_gated, mixed, pre, states, scales)


MESH = pl.DeviceIdType.MESH


class push:
    def __init__(self, src, dst, send_sem, recv_sem, device):
        self.args = (src, dst, send_sem, recv_sem, device, MESH)

    def start(self):
        pltpu.make_async_remote_copy(*self.args).start()

    def wait_send(self):
        pltpu.make_async_remote_copy(*self.args).wait_send()

    def wait_recv(self):
        pltpu.make_async_remote_copy(*self.args).wait_recv()

    def wait(self):
        self.wait_send()
        self.wait_recv()


def greet(devices_and_tests):
    barrier = pltpu.get_barrier_semaphore()
    count = 0
    for device, there in devices_and_tests:
        if there is None:
            pl.semaphore_signal(barrier, inc=1, device_id=device, device_id_type=MESH)
            count = count + 1
        else:
            @pl.when(there)
            def _():
                pl.semaphore_signal(barrier, inc=1, device_id=device, device_id_type=MESH)

            count = count + there.astype(jnp.int32)
    pl.semaphore_wait(barrier, count)


def line_of(nc):
    me = lax.axis_index("ctx")
    return nc // 2, me // 2, lax.rem(me, 2)


def square_partners():
    me = lax.axis_index("fsdp")
    high, low = me // 2, lax.rem(me, 2)
    return me, high * 2 + (1 - low), (1 - high) * 2 + low


def gather_neighbours(nc, nf):
    nz, z, k = line_of(nc)
    me_f = lax.axis_index("fsdp")
    found = [
        ({"ctx": 2 * z + 1 - k}, None),
        ({"ctx": 2 * (z + 1) + k}, z < nz - 1),
        ({"ctx": 2 * (z - 1) + k}, z > 0),
    ]
    if nf == 4:
        _, fx, fy = square_partners()
        found += [({"fsdp": fx}, None), ({"fsdp": fy}, None)]
    else:
        found += [({"fsdp": lax.rem(me_f + j, nf)}, None) for j in range(1, nf)]
    return found


class LineGather:
    def __init__(self, nc, own, every, sems):
        self.nz, self.z, self.k = line_of(nc)
        self.own, self.every = own, every
        self.up, self.down, self.side, self.got, self.got_side, self.here = sems

    def slot(self, place, core=None):
        return self.every.at[2 * place + (self.k if core is None else core)]

    def copies(self, d, below):
        z, k = self.z, self.k
        origin = z - d if below else z + d
        src = self.own if d == 0 else self.slot(origin)
        to = z + 1 if below else z - 1
        on = push(
            src, self.slot(origin), (self.up if below else self.down).at[d], self.got.at[origin],
            {"ctx": 2 * to + k},
        )
        side = push(
            src, self.slot(origin), self.side.at[origin], self.got_side.at[origin],
            {"ctx": 2 * z + 1 - k},
        )
        there = origin >= 0 if below else origin <= self.nz - 1
        further = to <= self.nz - 1 if below else to >= 0
        return origin, on, side, there, further

    def begin(self):
        pltpu.make_async_copy(self.own, self.slot(self.z), self.here).start()
        for below in (True, False):
            _, on, side, _, further = self.copies(0, below)
            pl.when(further)(on.start)
        side.start()

    def step(self, d):
        for below in (True, False):
            origin, on, side, there, further = self.copies(d, below)

            @pl.when(there)
            def _():
                on.wait_recv()
                side.start()
                pl.when(further)(on.start)

    def end(self):
        z, k, nz = self.z, self.k, self.nz
        pltpu.make_async_copy(self.own, self.slot(z), self.here).wait()
        for place in range(nz):
            arrived = self.every.at[2 * place + 1 - k]
            push(
                arrived, arrived, self.side.at[place], self.got_side.at[place], {"ctx": 2 * z + 1 - k}
            ).wait()
        for d in range(nz - 1):
            for below in (True, False):
                _, on, _, there, further = self.copies(d, below)
                pl.when(jnp.logical_and(there, further))(on.wait_send)


class SquareGather:
    def __init__(self, nf, own, every, sems):
        self.nf, self.own, self.every = nf, own, every
        self.send, self.got, self.here = sems
        self.half = own.shape[0] // 2

    def first(self):
        me = lax.axis_index("fsdp")
        if self.nf == 4:
            _, fx, fy = square_partners()
            peers = [(fx, fx), (fy, fy)]
        else:
            peers = [
                (lax.rem(me + j, self.nf), lax.rem(me + self.nf - j, self.nf))
                for j in range(1, self.nf)
            ]
        return [
            (
                push(self.own, self.every.at[me], self.send.at[j], self.got.at[j], {"fsdp": to}),
                push(self.own, self.every.at[frm], self.send.at[j], self.got.at[j], {"fsdp": to}),
            )
            for j, (to, frm) in enumerate(peers)
        ]

    def second(self):
        me, fx, fy = square_partners()
        far = 3 - me
        pairs = []
        for j, (via, to) in enumerate(((fx, fy), (fy, fx))):
            rows = pl.ds(j * self.half, self.half)
            args = (self.send.at[2 + j], self.got.at[2 + j], {"fsdp": to})
            there, here = self.every.at[via, rows], self.every.at[far, rows]
            pairs.append((push(there, there, *args), push(here, here, *args)))
        return pairs

    def begin(self):
        me = lax.axis_index("fsdp")
        pltpu.make_async_copy(self.own, self.every.at[me], self.here).start()
        for out, _ in self.first():
            out.start()

    def step(self):
        for j, (_, arrived) in enumerate(self.first()):
            arrived.wait_recv()
            if self.nf == 4:
                self.second()[j][0].start()

    def end(self):
        me = lax.axis_index("fsdp")
        pltpu.make_async_copy(self.own, self.every.at[me], self.here).wait()
        for out, _ in self.first():
            out.wait_send()
        if self.nf == 4:
            for out, arrived in self.second():
                arrived.wait_recv()
                out.wait_send()


class Spread:
    def __init__(self, nf, source, own, every, sems):
        self.nf, self.source, self.own, self.every = nf, source, own, every
        self.send, self.got, self.here = sems
        self.mine = lax.axis_index("fsdp") == source

    def copies(self):
        me = lax.axis_index("fsdp")
        return [
            push(
                self.own, self.every, self.send.at[j], self.got.at[0], {"fsdp": lax.rem(me + j, self.nf)}
            )
            for j in range(1, self.nf)
        ]

    def begin(self):
        @pl.when(self.mine)
        def _():
            pltpu.make_async_copy(self.own, self.every, self.here).start()
            for out in self.copies():
                out.start()

    def step(self):
        pass

    def end(self):
        @pl.when(self.mine)
        def _():
            pltpu.make_async_copy(self.own, self.every, self.here).wait()
            for out in self.copies():
                out.wait_send()

        if self.nf > 1:

            @pl.when(jnp.logical_not(self.mine))
            def _():
                self.copies()[0].wait_recv()


def gather_kernel(
    nc, nf, spread, normed, cot, in_rows, out_rows, normed_all, cot_all, in_all, out_all,
    line_sems, in_sems, out_sems, here,
):
    nz = nc // 2
    lines = [
        LineGather(
            nc, own, every, [line_sems.at[i, j] for j in range(5)] + [here.at[i]]
        )
        for i, (own, every) in enumerate(((normed, normed_all), (cot, cot_all)))
    ]
    weights = SquareGather(nf, in_rows, in_all, [in_sems.at[0], in_sems.at[1], here.at[2]])
    out_args = (out_rows, out_all, [out_sems.at[0], out_sems.at[1], here.at[3]])
    if spread:
        outs = Spread(nf, lax.axis_index("ctx") // spread, *out_args)
    else:
        outs = SquareGather(nf, *out_args)
    greet(gather_neighbours(nc, nf))
    weights.begin()
    lines[0].begin()
    for d in range(1, nz):
        lines[0].step(d)
        if d == 1:
            lines[1].begin()
    weights.step()
    outs.begin()
    for d in range(1, nz):
        lines[1].step(d)
    if nz == 1:
        lines[1].begin()
    outs.step()
    for part in (weights, lines[0], lines[1], outs):
        part.end()


def call_gather(nc, nf, spread, normed, cot, in_rows, out_rows):
    every = lambda a, n: jax.ShapeDtypeStruct((n,) + a.shape, a.dtype)
    nz = nc // 2
    places = max(nf, 4)
    anywhere = pl.BlockSpec(memory_space=pl.ANY)
    return pl.pallas_call(
        functools.partial(gather_kernel, nc, nf, spread),
        in_specs=[anywhere] * 4,
        out_specs=[anywhere] * 4,
        out_shape=[
            every(normed, nc),
            every(cot, nc),
            every(in_rows, nf),
            jax.ShapeDtypeStruct(out_rows.shape, BF16) if spread else every(out_rows, nf),
        ],
        scratch_shapes=[
            pltpu.SemaphoreType.DMA((2, 5, nz)),
            pltpu.SemaphoreType.DMA((2, places)),
            pltpu.SemaphoreType.DMA((2, places)),
            pltpu.SemaphoreType.DMA((4,)),
        ],
        compiler_params=pltpu.CompilerParams(
            collective_id=0, has_side_effects=True, vmem_limit_bytes=VMEM_LIMIT
        ),
        name="gather",
    )(normed, cot, in_rows, out_rows)


def add_over_ctx_kernel(nc, own, total, held, send, got):
    me = lax.axis_index("ctx")
    peers = [(lax.rem(me + j, nc), lax.rem(me + nc - j, nc)) for j in range(1, nc)]
    greet([({"ctx": to}, None) for to, _ in peers])
    for j, (to, _) in enumerate(peers):
        push(own, held.at[me], send.at[j], got.at[j], {"ctx": to}).start()
    held[me] = own[...]
    for j, (to, frm) in enumerate(peers):
        push(own, held.at[frm], send.at[j], got.at[j], {"ctx": to}).wait()
    result = held[0]
    for c in range(1, nc):
        result = result + held[c]
    total[...] = result


def add_over_ctx(nc, own):
    return pl.pallas_call(
        functools.partial(add_over_ctx_kernel, nc),
        in_specs=[pl.BlockSpec(memory_space=pltpu.VMEM)],
        out_specs=pl.BlockSpec(memory_space=pltpu.VMEM),
        out_shape=jax.ShapeDtypeStruct(own.shape, F32),
        scratch_shapes=[
            pltpu.VMEM((nc,) + own.shape, F32),
            pltpu.SemaphoreType.DMA((nc,)),
            pltpu.SemaphoreType.DMA((nc,)),
        ],
        compiler_params=pltpu.CompilerParams(collective_id=1, has_side_effects=True),
        name="add_over_ctx",
    )(own)


def rms_scale(values, gain_vec):
    return values * lax.rsqrt(jnp.mean(values * values, axis=-1, keepdims=True) + EPS) * gain_vec


def local(
    hidden,
    cotangent,
    lengths,
    norm_gain,
    input_weight,
    conv_w,
    conv_b,
    dt_bias,
    a_log,
    d_skip,
    gate_gain,
    output_weight,
):
    nc, nf = lax.axis_size("ctx"), lax.axis_size("fsdp")
    me_c, me_f = lax.axis_index("ctx"), lax.axis_index("fsdp")
    mb_count, seq_rows, length = hidden.shape[0], hidden.shape[1], hidden.shape[2]
    seqs = mb_count * seq_rows
    mine = seqs * length
    heads = HEADS // nc
    cw = DI // nc
    cc = cw + 2 * N_STATE
    per = 2 if nc % 2 == 0 else 1
    q = per * length
    chunks = nc // per

    span = nf if (DI // nf // nc) % LANES == 0 else 1
    wide, apart = cw // span, DI // span
    cut = lambda a, start, size, axis: lax.dynamic_slice_in_dim(a, start, size, axis)

    def my_blocks(a, base, axis, unit):
        return jnp.concatenate(
            [
                cut(a, base + (i * apart + wide * me_c) // unit, wide // unit, axis)
                for i in range(span)
            ],
            axis=axis,
        )

    source = hidden.astype(F32).reshape(seqs, length, D)
    normed = rms_scale(source, norm_gain).astype(BF16)
    cot = cotangent.reshape(mine, D)
    in_rows = jnp.concatenate(
        [
            my_blocks(input_weight, 0, 1, 1),
            my_blocks(input_weight, DI, 1, 1),
            input_weight[:, 2 * DI : 2 * DI + 2 * N_STATE],
            jnp.pad(
                my_blocks(input_weight, DI + CH, 1, HEAD_DIM), ((0, 0), (0, LANES - heads))
            ),
        ],
        axis=1,
    )
    shard = output_weight.shape[0]
    if span > 1:
        out_rows = cut(output_weight, wide * me_c, wide, 0)
        spread = 0
    else:
        spread = shard // cw
        out_rows = cut(output_weight, cw * lax.rem(me_c, spread), cw, 0)
    normed_all, cot_all, in_w, out_w = call_gather(
        nc, nf, spread, normed.reshape(mine, D), cot, in_rows, out_rows
    )
    normed_all, cot_all = normed_all.reshape(nc * mine, D), cot_all.reshape(nc * mine, D)
    in_w, out_w = in_w.reshape(D, -1), out_w.reshape(cw, D)

    my_columns = lambda a: jnp.concatenate(
        [my_blocks(a, 0, 1, 1), lax.slice_in_dim(a, DI, CH, axis=1)], axis=1
    )
    conv_par = jnp.concatenate(
        [my_columns(conv_w), my_columns(conv_b[None]), jnp.zeros((3, cc), F32)], axis=0
    )
    per_head = lambda a: my_blocks(a, 0, 0, HEAD_DIM)
    pad_heads = lambda a: jnp.pad(a, (0, LANES - heads))[None]
    rate = -jnp.exp(per_head(a_log))
    heads_par = jnp.concatenate(
        [pad_heads(per_head(dt_bias)), pad_heads(rate), jnp.zeros((6, LANES), F32)], axis=0
    )
    chan_par = jnp.concatenate(
        [
            jnp.repeat(per_head(d_skip), HEAD_DIM)[None],
            my_blocks(gate_gain, 0, 0, 1)[None],
            jnp.zeros((6, cw), F32),
        ],
        axis=0,
    )
    seq_lengths = lengths.reshape(seqs)

    proj = dot(normed_all, in_w).astype(BF16).reshape(nc, seqs, length, -1)
    grad_gated = dot(cot_all, out_w, 1, 1).reshape(nc, seqs, length, cw)
    mixed, pre, states, stats = call_forward(
        cw, per, seq_lengths, proj, conv_par, heads_par, chan_par, grad_gated
    )
    totals = add_over_ctx(nc, stats[:, :, 0:2].reshape(chunks * seqs * 2, q)) / DI
    totals = totals.reshape(chunks, seqs, 2, q)
    scale = lax.rsqrt(totals[:, :, 0] + EPS)
    pull = scale * scale * totals[:, :, 1]
    scales = jnp.pad(jnp.stack([scale, pull], axis=2), ((0, 0), (0, 0), (0, 6), (0, 0)))

    by_chunk = lambda a: jnp.moveaxis(
        a.reshape(chunks, seqs, per, length, a.shape[-1]), 2, 1
    ).reshape(nc, seqs, length, a.shape[-1])
    gate = proj[..., :cw].astype(F32)
    g = by_chunk(mixed) * jax.nn.silu(gate)
    gated = (g * by_chunk(scale[..., None]) * chan_par[1]).astype(BF16).reshape(nc * mine, cw)
    branch = dot(gated, out_w).astype(BF16).reshape(nc, mine, D)
    out = lax.psum_scatter(branch, "ctx", scatter_dimension=0).astype(F32) + source.reshape(mine, D)
    grad_out = lax.psum_scatter(
        dot(gated, cot_all, 0, 0).astype(BF16), "fsdp", scatter_dimension=0, tiled=True
    )
    if span > 1:
        route = [(c * nf + f, f * nc + c) for c in range(nc) for f in range(nf)]
        grad_out = lax.ppermute(grad_out, ("ctx", "fsdp"), route)
    grad_out = grad_out.astype(F32)

    dproj, dconv, dheads, dchan = call_backward(
        cw, per, seq_lengths, proj, conv_par, heads_par, chan_par, grad_gated, mixed, pre, states,
        scales,
    )
    dproj = dproj.reshape(nc * mine, -1)
    dnormed = dot(dproj, in_w, 1, 1).astype(BF16).reshape(nc, mine, D)
    dnormed = lax.psum_scatter(dnormed, "ctx", scatter_dimension=0).astype(F32)
    _, norm_pull = jax.vjp(rms_scale, source, norm_gain)
    dsource, dnorm_gain = norm_pull(dnormed.reshape(seqs, length, D))
    d_hidden = dsource + cot.astype(F32).reshape(seqs, length, D)

    rows = D // (nc * nf)
    partial = dot(normed_all, dproj, 0, 0).astype(BF16).reshape(nc, nf, rows, -1)
    partial = lax.psum_scatter(partial, "fsdp", scatter_dimension=1)
    pieces = lax.all_to_all(partial, "ctx", split_axis=0, concat_axis=0, tiled=True)
    side = lambda a: jnp.transpose(
        a.reshape(nc, rows, span, -1), (1, 2, 0, 3)
    ).reshape(rows, -1)
    grad_in = jnp.concatenate(
        [
            side(pieces[:, :, :cw]),
            side(pieces[:, :, cw : 2 * cw]),
            jnp.sum(pieces[:, :, 2 * cw : 2 * cw + 2 * N_STATE].astype(F32), axis=0).astype(BF16),
            side(pieces[:, :, 2 * cw + 2 * N_STATE : 2 * cw + 2 * N_STATE + heads]),
        ],
        axis=1,
    ).astype(F32)

    def place(a, unit):
        axis, size = a.ndim - 1, wide // unit
        whole = jnp.zeros(a.shape[:-1] + (DI // unit,), F32)
        for i in range(span):
            part = lax.slice_in_dim(a, i * size, (i + 1) * size, axis=axis)
            whole = lax.dynamic_update_slice_in_dim(
                whole, part, (i * apart + wide * me_c) // unit, axis
            )
        return whole

    dconv = jnp.concatenate(
        [place(dconv[: CONV_K + 1, :cw], 1), dconv[: CONV_K + 1, cw:]], axis=1
    )
    dskip = jnp.sum(dchan[0].reshape(heads, HEAD_DIM), axis=1)
    small = (
        dnorm_gain,
        dconv,
        place(dheads[0, :heads], HEAD_DIM),
        place(dheads[1, :heads], HEAD_DIM),
        place(dskip, HEAD_DIM),
        place(dchan[1], 1),
    )
    dnorm_gain, dconv, dbias, dalog, dskip, dgain = lax.psum(small, ("ctx", "fsdp"))
    shape = hidden.shape
    return (
        out.astype(BF16).reshape(shape),
        d_hidden.reshape(shape),
        dnorm_gain,
        grad_in,
        dconv[:CONV_K],
        dconv[CONV_K],
        dbias,
        dalog,
        dskip,
        dgain,
        grad_out,
    )


def solution(mesh):
    tokens, rows, every = P(None, "fsdp", "ctx", None), P("fsdp", None), P()
    spread = P(("ctx", "fsdp"), None)
    in_specs = (
        tokens, tokens, P(None, "fsdp"), every, rows, every, every, every, every, every, every, rows,
    )
    out_specs = (
        tokens, tokens, every, spread, every, every, every, every, every, every, spread,
    )
    return jax.shard_map(local, mesh=mesh, in_specs=in_specs, out_specs=out_specs, check_vma=False)
```

```python
import functools

import jax
import jax.numpy as jnp
from jax import lax
from jax.experimental import pallas as pl
from jax.experimental.pallas import tpu as pltpu
from jax.sharding import PartitionSpec as P

D = 2048
HEADS = 64
HEAD_DIM = 64
N_STATE = 128
CONV_K = 4
DI = 4096
CH = DI + 2 * N_STATE
LANES = 128
EPS = 1e-05
F32 = jnp.float32
BF16 = jnp.bfloat16
EXACT = lax.Precision.HIGHEST
VMEM_LIMIT = 60 * 1024 * 1024


def dot(a, b, ca=1, cb=0):
    return lax.dot_general(
        a.astype(BF16), b.astype(BF16), (((ca,), (cb,)), ((), ())), preferred_element_type=F32
    )


def dot_exact(a, b):
    return lax.dot_general(
        a, b, (((1,), (0,)), ((), ())), precision=EXACT, preferred_element_type=F32
    )


def to_lanes(per_head, width):
    q = per_head.shape[0]
    low = lax.broadcasted_iota(jnp.int32, (q, LANES), 1) < HEAD_DIM
    pairs = []
    for j in range(width // LANES):
        first = jnp.broadcast_to(per_head[:, 2 * j : 2 * j + 1], (q, LANES))
        second = jnp.broadcast_to(per_head[:, 2 * j + 1 : 2 * j + 2], (q, LANES))
        pairs.append(jnp.where(low, first, second))
    return jnp.concatenate(pairs, axis=1)


def head_sum_matrix(width):
    channel = lax.broadcasted_iota(jnp.int32, (width, LANES), 0) // HEAD_DIM
    return (channel == lax.broadcasted_iota(jnp.int32, (width, LANES), 1)).astype(F32)


def split_heads(pair):
    low = lax.broadcasted_iota(jnp.int32, pair.shape, 1) < HEAD_DIM
    zero = jnp.zeros_like(pair)
    return jnp.concatenate([jnp.where(low, pair, zero), jnp.where(low, zero, pair)], axis=0)


def triangle(q, lower):
    rows = lax.broadcasted_iota(jnp.int32, (q, q), 0)
    cols = lax.broadcasted_iota(jnp.int32, (q, q), 1)
    return (rows >= cols) if lower else (rows <= cols)


def softplus(z):
    return jnp.maximum(z, 0.0) + jnp.log(1.0 + jnp.exp(-jnp.abs(z)))


def live_column(lengths_ref, s, chunk, q):
    slots = chunk * q + lax.broadcasted_iota(jnp.int32, (q, LANES), 0)
    return (slots < lengths_ref[s]).astype(F32)


def decays(dt_raw, bias, rate, live):
    q = dt_raw.shape[0]
    z = dt_raw + bias
    step = softplus(z) * live
    cum = dot_exact(triangle(q, True).astype(F32), step * rate)
    return z, step, cum


def forward_kernel(
    cw, lengths, proj, conv_w, heads_par, chan_par, grad_gated, mixed_out, pre_out, state_out,
    stats_out, window, state,
):
    chunk = pl.program_id(0)
    seqs = proj.shape[1]
    q = proj.shape[0] * proj.shape[2]
    cc = cw + 2 * N_STATE
    causal = triangle(q, True)

    @pl.when(chunk == 0)
    def _():
        window[...] = jnp.zeros_like(window)
        state[...] = jnp.zeros_like(state)

    for s in range(seqs):
        rows = proj[:, s].reshape(q, proj.shape[3])
        gate = rows[:, :cw].astype(F32)
        window[s, 8 : 8 + q, :] = rows[:, cw : cw + cc].astype(F32)
        pre = conv_w[CONV_K : CONV_K + 1, :] + conv_w[0:1, :] * window[s, 5 : 5 + q, :]
        for k in range(1, CONV_K):
            pre = pre + conv_w[k : k + 1, :] * window[s, 5 + k : 5 + k + q, :]
        window[s, 0:8, :] = window[s, q : q + 8, :]
        pre_out[0, s] = pre
        act = pre * jax.nn.sigmoid(pre)
        x = act[:, :cw]
        b = act[:, cw : cw + N_STATE]
        c = act[:, cw + N_STATE :]
        live = live_column(lengths, s, chunk, q)
        _, step, cum = decays(
            rows[:, cw + cc :].astype(F32), heads_par[0:1, :], heads_par[1:2, :], live
        )
        cum_t = cum.T
        last = cum[q - 1 : q, :]
        u = x * to_lanes(step, cw)
        gram = dot(c, b, 1, 1)
        within = []
        for j in range(cw // LANES):
            kernels = []
            for h in (2 * j, 2 * j + 1):
                spread = jnp.where(causal, cum[:, h : h + 1] - cum_t[h : h + 1, :], -1e30)
                kernels.append((gram * jnp.exp(spread)).astype(BF16))
            both = jnp.concatenate(kernels, axis=1)
            within.append(dot(both, split_heads(u[:, j * LANES : (j + 1) * LANES])))
        before = state[s]
        state_out[0, s] = before
        mixed = (
            jnp.concatenate(within, axis=1)
            + dot(c, before) * to_lanes(jnp.exp(cum), cw)
            + chan_par[0:1, :] * x
        )
        mixed_out[0, s] = mixed
        left = to_lanes(jnp.exp(last - cum), cw)
        state[s] = before * to_lanes(jnp.exp(last), cw) + dot(b, left * u, 0, 0)
        g = mixed * gate * jax.nn.sigmoid(gate)
        gg = grad_gated[:, s].reshape(q, cw)
        ones = jnp.ones((8, cw), F32)
        first = lax.dot_general(
            ones, g * g, (((1,), (1,)), ((), ())), precision=EXACT, preferred_element_type=F32
        )
        second = lax.dot_general(
            ones, gg * chan_par[1:2, :] * g, (((1,), (1,)), ((), ())), precision=EXACT,
            preferred_element_type=F32,
        )
        stats_out[0, s, 0:1, :] = first[0:1, :]
        stats_out[0, s, 1:2, :] = second[0:1, :]


def backward_kernel(
    cw, chunks, lengths, proj, conv_w, heads_par, chan_par, grad_gated, mixed_in, pre_in, state_in,
    scale_in, dproj_out, dconv_out, dheads_out, dchan_out, window, state_grad,
):
    step_id = pl.program_id(0)
    chunk = chunks - 1 - step_id
    seqs = proj.shape[1]
    q = proj.shape[0] * proj.shape[2]
    blocks = proj.shape[0]
    cc = cw + 2 * N_STATE
    causal = triangle(q, True)
    sums = head_sum_matrix(cw)

    @pl.when(step_id == 0)
    def _():
        window[...] = jnp.zeros_like(window)
        state_grad[...] = jnp.zeros_like(state_grad)
        dconv_out[...] = jnp.zeros_like(dconv_out)
        dheads_out[...] = jnp.zeros_like(dheads_out)
        dchan_out[...] = jnp.zeros_like(dchan_out)

    for s in range(seqs):
        rows = proj[:, s].reshape(q, proj.shape[3])
        gate = rows[:, :cw].astype(F32)
        conv_in = rows[:, cw : cw + cc].astype(F32)
        pre = pre_in[0, s]
        mixed = mixed_in[0, s]
        gg = grad_gated[:, s].reshape(q, cw)
        scale = jnp.concatenate(
            [jnp.broadcast_to(scale_in[0, s, 0:1, :], (LANES, q)).T] * (cw // LANES), axis=1
        )
        pull = jnp.concatenate(
            [jnp.broadcast_to(scale_in[0, s, 1:2, :], (LANES, q)).T] * (cw // LANES), axis=1
        )
        sig = jax.nn.sigmoid(gate)
        silu = gate * sig
        g = mixed * silu
        dchan_out[1:2, :] += jnp.sum(gg * g * scale, axis=0, keepdims=True)
        dg = scale * (gg * chan_par[1:2, :] - g * pull)
        gm = dg * silu
        dgate = dg * mixed * (sig * (1.0 + gate * (1.0 - sig)))
        sig_pre = jax.nn.sigmoid(pre)
        act = pre * sig_pre
        x = act[:, :cw]
        b = act[:, cw : cw + N_STATE]
        c = act[:, cw + N_STATE :]
        live = live_column(lengths, s, chunk, q)
        z, step, cum = decays(
            rows[:, cw + cc :].astype(F32), heads_par[0:1, :], heads_par[1:2, :], live
        )
        cum_t = cum.T
        last = cum[q - 1 : q, :]
        step_l = to_lanes(step, cw)
        u = x * step_l
        gram = dot(c, b, 1, 1)
        dchan_out[0:1, :] += jnp.sum(gm * x, axis=0, keepdims=True)
        du = []
        dgram = jnp.zeros((q, q), F32)
        for j in range(cw // LANES):
            at = slice(j * LANES, (j + 1) * LANES)
            dkernels = dot(gm[:, at], split_heads(u[:, at]), 1, 1)
            kernels = []
            for i in range(2):
                h = 2 * j + i
                spread = jnp.where(causal, cum[:, h : h + 1] - cum_t[h : h + 1, :], -1e30)
                decay = jnp.exp(spread)
                dgram = dgram + dkernels[:, i * q : (i + 1) * q] * decay
                kernels.append((gram * decay).astype(BF16))
            both = jnp.concatenate(kernels, axis=0)
            du.append(dot(both, split_heads(gm[:, at]), 0, 0))
        before = state_in[0, s]
        after_grad = state_grad[s]
        v = gm * to_lanes(jnp.exp(cum), cw)
        left = to_lanes(jnp.exp(last - cum), cw)
        du_state = left * dot(b, after_grad)
        du = jnp.concatenate(du, axis=1) + du_state
        dc = dot(dgram, b) + dot(v, before, 1, 1)
        db = dot(dgram, c, 0, 0) + dot(left * u, after_grad, 1, 1)
        end = to_lanes(jnp.exp(last), cw)
        extra = jnp.sum(u * du_state, axis=0, keepdims=True) + end * jnp.sum(
            after_grad * before, axis=0, keepdims=True
        )
        state_grad[s] = end * after_grad + dot(c, v, 0, 0)
        last_row = (lax.broadcasted_iota(jnp.int32, (q, LANES), 0) == q - 1).astype(F32)
        dcum = dot_exact(gm * (mixed - chan_par[0:1, :] * x) - u * du, sums) + last_row * dot_exact(
            jnp.broadcast_to(extra, (8, cw)), sums
        )[0:1, :]
        dlog = dot_exact(triangle(q, False).astype(F32), dcum)
        rate = heads_par[1:2, :]
        dstep = dot_exact(x * du, sums) + dlog * rate
        dheads_out[1:2, :] += jnp.sum(dlog * step * rate, axis=0, keepdims=True)
        dz = dstep * live * jax.nn.sigmoid(z)
        dheads_out[0:1, :] += jnp.sum(dz, axis=0, keepdims=True)
        dx = step_l * du + chan_par[0:1, :] * gm
        dpre = jnp.concatenate([dx, db, dc], axis=1) * (sig_pre * (1.0 + pre * (1.0 - sig_pre)))
        window[s, 0:q, :] = dpre
        dconv_in = jnp.zeros((q, cc), F32)
        for k in range(CONV_K):
            ahead = CONV_K - 1 - k
            moved = window[s, ahead : ahead + q, :]
            dconv_in = dconv_in + conv_w[k : k + 1, :] * moved
            dconv_out[k : k + 1, :] += jnp.sum(conv_in * moved, axis=0, keepdims=True)
        dconv_out[CONV_K : CONV_K + 1, :] += jnp.sum(dpre, axis=0, keepdims=True)
        window[s, q : q + 8, :] = window[s, 0:8, :]
        dproj_out[:, s, :, :cw] = dgate.astype(BF16).reshape(blocks, q // blocks, cw)
        dproj_out[:, s, :, cw : cw + cc] = dconv_in.astype(BF16).reshape(blocks, q // blocks, cc)
        dproj_out[:, s, :, cw + cc :] = dz.astype(BF16).reshape(blocks, q // blocks, LANES)


def call_forward(cw, per, lengths, proj, conv_w, heads_par, chan_par, grad_gated):
    nc, seqs, length, cols = proj.shape
    chunks, q, cc = nc // per, per * length, cw + 2 * N_STATE
    whole = lambda a: pl.BlockSpec(a.shape, lambda i: (0,) * a.ndim)
    by_chunk = lambda n: pl.BlockSpec((1, seqs, n[0], n[1]), lambda i: (i, 0, 0, 0))
    tokens = lambda n: pl.BlockSpec((per, seqs, length, n), lambda i: (i, 0, 0, 0))
    return pl.pallas_call(
        functools.partial(forward_kernel, cw),
        grid=(chunks,),
        in_specs=[
            pl.BlockSpec(memory_space=pltpu.SMEM),
            tokens(cols),
            whole(conv_w),
            whole(heads_par),
            whole(chan_par),
            tokens(cw),
        ],
        out_specs=[
            by_chunk((q, cw)),
            by_chunk((q, cc)),
            by_chunk((N_STATE, cw)),
            by_chunk((8, q)),
        ],
        out_shape=[
            jax.ShapeDtypeStruct((chunks, seqs, q, cw), F32),
            jax.ShapeDtypeStruct((chunks, seqs, q, cc), F32),
            jax.ShapeDtypeStruct((chunks, seqs, N_STATE, cw), F32),
            jax.ShapeDtypeStruct((chunks, seqs, 8, q), F32),
        ],
        scratch_shapes=[
            pltpu.VMEM((seqs, q + 8, cc), F32),
            pltpu.VMEM((seqs, N_STATE, cw), F32),
        ],
        compiler_params=pltpu.CompilerParams(vmem_limit_bytes=VMEM_LIMIT),
        name="mixer_forward",
    )(lengths, proj, conv_w, heads_par, chan_par, grad_gated)


def call_backward(
    cw, per, lengths, proj, conv_w, heads_par, chan_par, grad_gated, mixed, pre, states, scales
):
    nc, seqs, length, cols = proj.shape
    chunks, q, cc = nc // per, per * length, cw + 2 * N_STATE
    whole = lambda shape: pl.BlockSpec(shape, lambda i: (0,) * len(shape))
    by_chunk = lambda n: pl.BlockSpec((1, seqs, n[0], n[1]), lambda i: (chunks - 1 - i, 0, 0, 0))
    tokens = lambda n: pl.BlockSpec(
        (per, seqs, length, n), lambda i: (chunks - 1 - i, 0, 0, 0)
    )
    return pl.pallas_call(
        functools.partial(backward_kernel, cw, chunks),
        grid=(chunks,),
        in_specs=[
            pl.BlockSpec(memory_space=pltpu.SMEM),
            tokens(cols),
            whole(conv_w.shape),
            whole(heads_par.shape),
            whole(chan_par.shape),
            tokens(cw),
            by_chunk((q, cw)),
            by_chunk((q, cc)),
            by_chunk((N_STATE, cw)),
            by_chunk((8, q)),
        ],
        out_specs=[
            tokens(cols),
            whole((8, cc)),
            whole((8, LANES)),
            whole((8, cw)),
        ],
        out_shape=[
            jax.ShapeDtypeStruct(proj.shape, BF16),
            jax.ShapeDtypeStruct((8, cc), F32),
            jax.ShapeDtypeStruct((8, LANES), F32),
            jax.ShapeDtypeStruct((8, cw), F32),
        ],
        scratch_shapes=[
            pltpu.VMEM((seqs, q + 8, cc), F32),
            pltpu.VMEM((seqs, N_STATE, cw), F32),
        ],
        compiler_params=pltpu.CompilerParams(vmem_limit_bytes=VMEM_LIMIT),
        name="mixer_backward",
    )(lengths, proj, conv_w, heads_par, chan_par, grad_gated, mixed, pre, states, scales)


MESH = pl.DeviceIdType.MESH


class push:
    def __init__(self, src, dst, send_sem, recv_sem, device):
        self.args = (src, dst, send_sem, recv_sem, device, MESH)

    def start(self):
        pltpu.make_async_remote_copy(*self.args).start()

    def wait_send(self):
        pltpu.make_async_remote_copy(*self.args).wait_send()

    def wait_recv(self):
        pltpu.make_async_remote_copy(*self.args).wait_recv()

    def wait(self):
        self.wait_send()
        self.wait_recv()


def greet(devices_and_tests):
    barrier = pltpu.get_barrier_semaphore()
    count = 0
    for device, there in devices_and_tests:
        if there is None:
            pl.semaphore_signal(barrier, inc=1, device_id=device, device_id_type=MESH)
            count = count + 1
        else:
            @pl.when(there)
            def _():
                pl.semaphore_signal(barrier, inc=1, device_id=device, device_id_type=MESH)

            count = count + there.astype(jnp.int32)
    pl.semaphore_wait(barrier, count)


def line_of(nc):
    me = lax.axis_index("ctx")
    return nc // 2, me // 2, lax.rem(me, 2)


def square_partners():
    me = lax.axis_index("fsdp")
    high, low = me // 2, lax.rem(me, 2)
    return me, high * 2 + (1 - low), (1 - high) * 2 + low


def gather_neighbours(nc, nf):
    nz, z, k = line_of(nc)
    me_f = lax.axis_index("fsdp")
    found = [
        ({"ctx": 2 * z + 1 - k}, None),
        ({"ctx": 2 * (z + 1) + k}, z < nz - 1),
        ({"ctx": 2 * (z - 1) + k}, z > 0),
    ]
    if nf == 4:
        _, fx, fy = square_partners()
        found += [({"fsdp": fx}, None), ({"fsdp": fy}, None)]
    else:
        found += [({"fsdp": lax.rem(me_f + j, nf)}, None) for j in range(1, nf)]
    return found


class LineGather:
    def __init__(self, nc, own, every, sems):
        self.nz, self.z, self.k = line_of(nc)
        self.own, self.every = own, every
        self.up, self.down, self.side, self.got, self.got_side, self.here = sems

    def slot(self, place, core=None):
        return self.every.at[2 * place + (self.k if core is None else core)]

    def copies(self, d, below):
        z, k = self.z, self.k
        origin = z - d if below else z + d
        src = self.own if d == 0 else self.slot(origin)
        to = z + 1 if below else z - 1
        on = push(
            src, self.slot(origin), (self.up if below else self.down).at[d], self.got.at[origin],
            {"ctx": 2 * to + k},
        )
        side = push(
            src, self.slot(origin), self.side.at[origin], self.got_side.at[origin],
            {"ctx": 2 * z + 1 - k},
        )
        there = origin >= 0 if below else origin <= self.nz - 1
        further = to <= self.nz - 1 if below else to >= 0
        return origin, on, side, there, further

    def begin(self):
        pltpu.make_async_copy(self.own, self.slot(self.z), self.here).start()
        for below in (True, False):
            _, on, side, _, further = self.copies(0, below)
            pl.when(further)(on.start)
        side.start()

    def step(self, d):
        for below in (True, False):
            origin, on, side, there, further = self.copies(d, below)

            @pl.when(there)
            def _():
                on.wait_recv()
                side.start()
                pl.when(further)(on.start)

    def end(self):
        z, k, nz = self.z, self.k, self.nz
        pltpu.make_async_copy(self.own, self.slot(z), self.here).wait()
        for place in range(nz):
            arrived = self.every.at[2 * place + 1 - k]
            push(
                arrived, arrived, self.side.at[place], self.got_side.at[place], {"ctx": 2 * z + 1 - k}
            ).wait()
        for d in range(nz - 1):
            for below in (True, False):
                _, on, _, there, further = self.copies(d, below)
                pl.when(jnp.logical_and(there, further))(on.wait_send)


class SquareGather:
    def __init__(self, nf, own, every, sems):
        self.nf, self.own, self.every = nf, own, every
        self.send, self.got, self.here = sems
        self.half = own.shape[0] // 2

    def first(self):
        me = lax.axis_index("fsdp")
        if self.nf == 4:
            _, fx, fy = square_partners()
            peers = [(fx, fx), (fy, fy)]
        else:
            peers = [
                (lax.rem(me + j, self.nf), lax.rem(me + self.nf - j, self.nf))
                for j in range(1, self.nf)
            ]
        return [
            (
                push(self.own, self.every.at[me], self.send.at[j], self.got.at[j], {"fsdp": to}),
                push(self.own, self.every.at[frm], self.send.at[j], self.got.at[j], {"fsdp": to}),
            )
            for j, (to, frm) in enumerate(peers)
        ]

    def second(self):
        me, fx, fy = square_partners()
        far = 3 - me
        pairs = []
        for j, (via, to) in enumerate(((fx, fy), (fy, fx))):
            rows = pl.ds(j * self.half, self.half)
            args = (self.send.at[2 + j], self.got.at[2 + j], {"fsdp": to})
            there, here = self.every.at[via, rows], self.every.at[far, rows]
            pairs.append((push(there, there, *args), push(here, here, *args)))
        return pairs

    def begin(self):
        me = lax.axis_index("fsdp")
        pltpu.make_async_copy(self.own, self.every.at[me], self.here).start()
        for out, _ in self.first():
            out.start()

    def step(self):
        for j, (_, arrived) in enumerate(self.first()):
            arrived.wait_recv()
            if self.nf == 4:
                self.second()[j][0].start()

    def end(self):
        me = lax.axis_index("fsdp")
        pltpu.make_async_copy(self.own, self.every.at[me], self.here).wait()
        for out, _ in self.first():
            out.wait_send()
        if self.nf == 4:
            for out, arrived in self.second():
                arrived.wait_recv()
                out.wait_send()


class Spread:
    def __init__(self, nf, source, own, every, sems):
        self.nf, self.source, self.own, self.every = nf, source, own, every
        self.send, self.got, self.here = sems
        self.mine = lax.axis_index("fsdp") == source

    def copies(self):
        me = lax.axis_index("fsdp")
        return [
            push(
                self.own, self.every, self.send.at[j], self.got.at[0], {"fsdp": lax.rem(me + j, self.nf)}
            )
            for j in range(1, self.nf)
        ]

    def begin(self):
        @pl.when(self.mine)
        def _():
            pltpu.make_async_copy(self.own, self.every, self.here).start()
            for out in self.copies():
                out.start()

    def step(self):
        pass

    def end(self):
        @pl.when(self.mine)
        def _():
            pltpu.make_async_copy(self.own, self.every, self.here).wait()
            for out in self.copies():
                out.wait_send()

        if self.nf > 1:

            @pl.when(jnp.logical_not(self.mine))
            def _():
                self.copies()[0].wait_recv()


def gather_kernel(
    nc, nf, spread, normed, cot, in_rows, out_rows, normed_all, cot_all, in_all, out_all,
    line_sems, in_sems, out_sems, here,
):
    nz = nc // 2
    lines = [
        LineGather(
            nc, own, every, [line_sems.at[i, j] for j in range(5)] + [here.at[i]]
        )
        for i, (own, every) in enumerate(((normed, normed_all), (cot, cot_all)))
    ]
    weights = SquareGather(nf, in_rows, in_all, [in_sems.at[0], in_sems.at[1], here.at[2]])
    out_args = (out_rows, out_all, [out_sems.at[0], out_sems.at[1], here.at[3]])
    if spread:
        outs = Spread(nf, lax.axis_index("ctx") // spread, *out_args)
    else:
        outs = SquareGather(nf, *out_args)
    greet(gather_neighbours(nc, nf))
    weights.begin()
    lines[0].begin()
    for d in range(1, nz):
        lines[0].step(d)
        if d == 1:
            lines[1].begin()
    weights.step()
    outs.begin()
    for d in range(1, nz):
        lines[1].step(d)
    if nz == 1:
        lines[1].begin()
    outs.step()
    for part in (weights, lines[0], lines[1], outs):
        part.end()


def call_gather(nc, nf, spread, normed, cot, in_rows, out_rows):
    every = lambda a, n: jax.ShapeDtypeStruct((n,) + a.shape, a.dtype)
    nz = nc // 2
    places = max(nf, 4)
    anywhere = pl.BlockSpec(memory_space=pl.ANY)
    return pl.pallas_call(
        functools.partial(gather_kernel, nc, nf, spread),
        in_specs=[anywhere] * 4,
        out_specs=[anywhere] * 4,
        out_shape=[
            every(normed, nc),
            every(cot, nc),
            every(in_rows, nf),
            jax.ShapeDtypeStruct(out_rows.shape, BF16) if spread else every(out_rows, nf),
        ],
        scratch_shapes=[
            pltpu.SemaphoreType.DMA((2, 5, nz)),
            pltpu.SemaphoreType.DMA((2, places)),
            pltpu.SemaphoreType.DMA((2, places)),
            pltpu.SemaphoreType.DMA((4,)),
        ],
        compiler_params=pltpu.CompilerParams(
            collective_id=0, has_side_effects=True, vmem_limit_bytes=VMEM_LIMIT
        ),
        name="gather",
    )(normed, cot, in_rows, out_rows)


def add_over_ctx_kernel(nc, own, total, held, send, got):
    me = lax.axis_index("ctx")
    peers = [(lax.rem(me + j, nc), lax.rem(me + nc - j, nc)) for j in range(1, nc)]
    greet([({"ctx": to}, None) for to, _ in peers])
    for j, (to, _) in enumerate(peers):
        push(own, held.at[me], send.at[j], got.at[j], {"ctx": to}).start()
    held[me] = own[...]
    for j, (to, frm) in enumerate(peers):
        push(own, held.at[frm], send.at[j], got.at[j], {"ctx": to}).wait()
    result = held[0]
    for c in range(1, nc):
        result = result + held[c]
    total[...] = result


def add_over_ctx(nc, own):
    return pl.pallas_call(
        functools.partial(add_over_ctx_kernel, nc),
        in_specs=[pl.BlockSpec(memory_space=pltpu.VMEM)],
        out_specs=pl.BlockSpec(memory_space=pltpu.VMEM),
        out_shape=jax.ShapeDtypeStruct(own.shape, F32),
        scratch_shapes=[
            pltpu.VMEM((nc,) + own.shape, F32),
            pltpu.SemaphoreType.DMA((nc,)),
            pltpu.SemaphoreType.DMA((nc,)),
        ],
        compiler_params=pltpu.CompilerParams(collective_id=1, has_side_effects=True),
        name="add_over_ctx",
    )(own)


def add_rows(into, other, rows=16):
    def body(i, _):
        at = pl.ds(pl.multiple_of(i * rows, rows), rows)
        into[at] = (into[at].astype(F32) + other[at].astype(F32)).astype(into.dtype)
        return 0

    lax.fori_loop(0, into.shape[0] // rows, body, 0)


class LineReduce:
    def __init__(self, nc, parts, acc, landed, sems):
        self.nz, self.z, self.k = line_of(nc)
        self.parts, self.acc, self.landed = parts, acc, landed
        self.side, self.got_side, self.send, self.got = sems

    def to_side(self, place):
        other = {"ctx": 2 * self.z + 1 - self.k}
        return push(
            self.parts.at[2 * place + 1 - self.k], self.acc.at[place], self.side.at[place],
            self.got_side.at[place], other,
        )

    def begin(self):
        for place in range(self.nz):
            self.to_side(place).start()

    def merge(self):
        for place in range(self.nz):
            self.to_side(place).wait_recv()
            add_rows(self.acc.at[place], self.parts.at[2 * place + self.k])

    def along(self, place, up):
        way = 0 if up else 1
        return push(
            self.acc.at[place], self.landed.at[way, place], self.send.at[way, place],
            self.got.at[way, place], {"ctx": 2 * (self.z + (1 if up else -1)) + self.k},
        )

    def arrive(self, place, up, into):
        self.along(place, up).wait_recv()
        add_rows(into, self.landed.at[0 if up else 1, place])

    def moves(self):
        for i in range(self.nz - 1):
            yield i, self.nz - 1 - i, True
            yield i, i, False

    def step(self, i):
        z, nz = self.z, self.nz
        for at, place, up in self.moves():
            if at != i:
                continue

            @pl.when(z < place if up else z > place)
            def _():
                @pl.when(z > 0 if up else z < nz - 1)
                def _():
                    self.arrive(place, up, self.acc.at[place])

                self.along(place, up).start()

    def final(self, total):
        z, nz = self.z, self.nz
        total[...] = self.acc[z].astype(F32)

        @pl.when(z > 0)
        def _():
            self.arrive(z, True, total)

        @pl.when(z < nz - 1)
        def _():
            self.arrive(z, False, total)

    def end(self):
        for place in range(self.nz):
            self.to_side(place).wait_send()
        for _, place, up in self.moves():
            pl.when(self.z < place if up else self.z > place)(self.along(place, up).wait_send)


class SquareReduce:
    def __init__(self, nf, parts, landed, total, sems):
        self.nf, self.parts, self.landed, self.total = nf, parts, landed, total
        self.send, self.got = sems
        self.half = parts.shape[1] // 2

    @staticmethod
    def landing(nf, shape):
        blocks, rows, cols = shape
        return (6, blocks // 2, rows, cols) if nf == 4 else (nf, blocks, rows, cols)

    def copy(self, n, src, to):
        return push(src, self.landed.at[n], self.send.at[n], self.got.at[n], {"fsdp": to})

    def way(self, h):
        me, fx, fy = square_partners()
        first, second = (fx, fy) if h == 0 else (fy, fx)
        return me, first, second, pl.ds(h * self.half, self.half)

    def firsts(self, h):
        me, first, second, at = self.way(h)
        return (
            self.copy(3 * h, self.parts.at[3 - me, at], first),
            self.copy(3 * h + 1, self.parts.at[first, at], first),
        )

    def second_(self, h):
        _, _, second, _ = self.way(h)
        return self.copy(3 * h + 2, self.landed.at[3 * h], second)

    def others(self):
        me = lax.axis_index("fsdp")
        tos = [lax.rem(me + j, self.nf) for j in range(1, self.nf)]
        return [self.copy(j + 1, self.parts.at[to], to) for j, to in enumerate(tos)]

    def begin(self):
        if self.nf == 4:
            for i in range(2):
                for h in range(2):
                    self.firsts(h)[i].start()
        else:
            for out in self.others():
                out.start()

    def add(self, into, other):
        for b in range(into.shape[0]):
            add_rows(into.at[b], other.at[b], min(16, into.shape[1]))

    def step(self):
        if self.nf == 4:
            for h in range(2):
                _, _, second, at = self.way(h)
                self.firsts(h)[0].wait_recv()
                self.add(self.landed.at[3 * h], self.parts.at[second, at])
                self.second_(h).start()

    def final(self, h):
        me = lax.axis_index("fsdp")
        at = pl.ds(h * self.half, self.half)
        if self.nf == 4:
            self.firsts(h)[1].wait_recv()
            into = self.total.at[at]
            into[...] = self.parts[me, at]
            self.add(into, self.landed.at[3 * h + 1])
            self.second_(h).wait_recv()
            self.add(into, self.landed.at[3 * h + 2])
        else:
            into = self.total.at[at]
            into[...] = self.parts[me, at]
            for j, out in enumerate(self.others()):
                if h == 0:
                    out.wait_recv()
                self.add(into, self.landed.at[j + 1, at])

    def end(self):
        if self.nf == 4:
            for h in range(2):
                for out in (*self.firsts(h), self.second_(h)):
                    out.wait_send()
        else:
            for out in self.others():
                out.wait_send()


class Exchange:
    def __init__(self, axis, n, own, every, sems):
        self.axis, self.n, self.own, self.every = axis, n, own, every
        self.send, self.got = sems

    def copies(self):
        me = lax.axis_index(self.axis)
        for j in range(1, self.n):
            to, frm = lax.rem(me + j, self.n), lax.rem(me + self.n - j, self.n)
            args = (self.send.at[j], self.got.at[j], {self.axis: to})
            yield push(self.own, self.every.at[me], *args), push(self.own, self.every.at[frm], *args)

    def begin(self):
        self.every[lax.axis_index(self.axis)] = self.own[...]
        for out, _ in self.copies():
            out.start()

    def wait(self):
        for out, arrived in self.copies():
            arrived.wait_recv()
            out.wait_send()

    def total(self):
        result = self.every[0]
        for i in range(1, self.n):
            result = result + self.every[i]
        return result


def scatter_kernel(
    nc, nf, strided, dnormed, gin, gout, small, hidden, cot, gain,
    d_hidden, pieces, gout_mine, small_all, gain_all,
    acc, landed, total, in_landed, in_sum, out_landed, out_sum,
    small_held, small_sum, gain_held, gain_own, gain_sum,
    line_side, line_sems, in_sems, out_sems, piece_sems, small_sems, here,
):
    nz, _, _ = line_of(nc)
    me_c, me_f = lax.axis_index("ctx"), lax.axis_index("fsdp")
    line = LineReduce(
        nc, dnormed, acc, landed,
        (line_side.at[0], line_side.at[1], line_sems.at[0], line_sems.at[1]),
    )
    ins = SquareReduce(nf, gin, in_landed, in_sum, (in_sems.at[0], in_sems.at[1]))
    outs = SquareReduce(nf, gout, out_landed, out_sum, (out_sems.at[0], out_sems.at[1]))
    pair = lambda i: (small_sems.at[i, 0], small_sems.at[i, 1])
    smalls = (
        Exchange("fsdp", nf, small, small_held, pair(0)),
        Exchange("ctx", nc, small_sum, small_all, pair(1)),
    )
    gains = (
        Exchange("fsdp", nf, gain_own, gain_held, pair(2)),
        Exchange("ctx", nc, gain_sum, gain_all, pair(3)),
    )
    found = [({"ctx": lax.rem(me_c + j, nc)}, None) for j in range(1, nc)]
    found += [({"fsdp": lax.rem(me_f + j, nf)}, None) for j in range(1, nf)]
    if strided:
        lead, place = me_f * nc + me_c, me_c * nf + me_f
        target = {"ctx": lead // nf, "fsdp": lax.rem(lead, nf)}
        source = {"ctx": lax.rem(place, nc), "fsdp": place // nc}
        away = lead != place
        found += [(target, away), (source, away)]
    greet(found)

    ins.begin()
    line.begin()
    smalls[0].begin()
    line.merge()
    for i in range(nz - 1):
        line.step(i)
        if i == 0:
            smalls[0].wait()
            small_sum[...] = smalls[0].total()
            smalls[1].begin()
    ins.step()
    outs.begin()
    line.final(total)
    gain_own[...] = jnp.zeros_like(gain_own)
    block = 16

    def norm_back(i, _):
        at = pl.ds(pl.multiple_of(i * block, block), block)
        src = hidden[at].astype(F32)
        dn = total[at]
        scale = lax.rsqrt(jnp.mean(src * src, axis=1, keepdims=True) + EPS)
        h = dn * gain[0:1, :]
        pull = jnp.mean(h * src, axis=1, keepdims=True) * scale * scale
        d_hidden[at] = scale * (h - src * pull) + cot[at].astype(F32)
        gain_own[0:1, :] += jnp.sum(dn * src * scale, axis=0, keepdims=True)
        return 0

    lax.fori_loop(0, hidden.shape[0] // block, norm_back, 0)
    gains[0].begin()

    def piece(c):
        return push(
            in_sum.at[c], pieces.at[me_c], piece_sems.at[0, c], piece_sems.at[1, me_c], {"ctx": c}
        )

    def piece_from(c):
        return push(in_sum.at[c], pieces.at[c], piece_sems.at[0, c], piece_sems.at[1, c], {"ctx": c})

    stay = pltpu.make_async_copy(in_sum.at[me_c], pieces.at[me_c], here.at[0])
    half = nc // 2
    for h in range(2):
        ins.final(h)
        for j in range(half):
            c = h * half + lax.rem(me_c + j, half)
            pl.when(c != me_c)(piece(c).start)
            pl.when(c == me_c)(stay.start)
    gains[0].wait()
    gain_sum[...] = gains[0].total()
    gains[1].begin()
    outs.step()
    outs.final(0)
    outs.final(1)
    if strided:
        route = push(out_sum, gout_mine, piece_sems.at[0, nc], piece_sems.at[1, nc], target)
        pl.when(away)(route.start)

        @pl.when(jnp.logical_not(away))
        def _():
            pltpu.make_async_copy(out_sum, gout_mine, here.at[1]).start()

    else:
        gout_mine[...] = out_sum[...]
    smalls[1].wait()
    gains[1].wait()
    line.end()
    ins.end()
    outs.end()
    stay.wait()
    for c in range(nc):

        @pl.when(c != me_c)
        def _():
            piece_from(c).wait_recv()
            piece(c).wait_send()

    if strided:

        @pl.when(away)
        def _():
            route.wait_recv()
            route.wait_send()

        @pl.when(jnp.logical_not(away))
        def _():
            pltpu.make_async_copy(out_sum, gout_mine, here.at[1]).wait()


def call_scatter(nc, nf, strided, dnormed, gin, gout, small, hidden, cot, gain):
    nz = nc // 2
    mine = hidden.shape[0]
    vmem = pl.BlockSpec(memory_space=pltpu.VMEM)
    dma = pltpu.SemaphoreType.DMA
    count = max(nf, 6)
    return pl.pallas_call(
        functools.partial(scatter_kernel, nc, nf, strided),
        in_specs=[vmem] * 7,
        out_specs=[vmem] * 5,
        out_shape=[
            jax.ShapeDtypeStruct((mine, D), F32),
            jax.ShapeDtypeStruct(gin.shape[1:], BF16),
            jax.ShapeDtypeStruct(gout.shape[1:], BF16),
            jax.ShapeDtypeStruct((nc,) + small.shape, F32),
            jax.ShapeDtypeStruct((nc, 8, D), F32),
        ],
        scratch_shapes=[
            pltpu.VMEM((nz, mine, D), BF16),
            pltpu.VMEM((2, nz, mine, D), BF16),
            pltpu.VMEM((mine, D), F32),
            pltpu.VMEM(SquareReduce.landing(nf, gin.shape[1:]), BF16),
            pltpu.VMEM(gin.shape[1:], BF16),
            pltpu.VMEM(SquareReduce.landing(nf, gout.shape[1:]), BF16),
            pltpu.VMEM(gout.shape[1:], BF16),
            pltpu.VMEM((nf,) + small.shape, F32),
            pltpu.VMEM(small.shape, F32),
            pltpu.VMEM((nf, 8, D), F32),
            pltpu.VMEM((8, D), F32),
            pltpu.VMEM((8, D), F32),
            dma((2, nz)),
            dma((2, 2, nz)),
            dma((2, count)),
            dma((2, count)),
            dma((2, nc + 1)),
            dma((4, 2, max(nc, nf))),
            dma((2,)),
        ],
        compiler_params=pltpu.CompilerParams(
            collective_id=2, has_side_effects=True, vmem_limit_bytes=VMEM_LIMIT
        ),
        name="scatter",
    )(dnormed, gin, gout, small, hidden, cot, gain)


def rms_scale(values, gain_vec):
    return values * lax.rsqrt(jnp.mean(values * values, axis=-1, keepdims=True) + EPS) * gain_vec


def local(
    hidden,
    cotangent,
    lengths,
    norm_gain,
    input_weight,
    conv_w,
    conv_b,
    dt_bias,
    a_log,
    d_skip,
    gate_gain,
    output_weight,
):
    nc, nf = lax.axis_size("ctx"), lax.axis_size("fsdp")
    me_c, me_f = lax.axis_index("ctx"), lax.axis_index("fsdp")
    mb_count, seq_rows, length = hidden.shape[0], hidden.shape[1], hidden.shape[2]
    seqs = mb_count * seq_rows
    mine = seqs * length
    heads = HEADS // nc
    cw = DI // nc
    cc = cw + 2 * N_STATE
    per = 2 if nc % 2 == 0 else 1
    q = per * length
    chunks = nc // per

    span = nf if (DI // nf // nc) % LANES == 0 else 1
    wide, apart = cw // span, DI // span
    cut = lambda a, start, size, axis: lax.dynamic_slice_in_dim(a, start, size, axis)

    def my_blocks(a, base, axis, unit):
        return jnp.concatenate(
            [
                cut(a, base + (i * apart + wide * me_c) // unit, wide // unit, axis)
                for i in range(span)
            ],
            axis=axis,
        )

    source = hidden.astype(F32).reshape(seqs, length, D)
    normed = rms_scale(source, norm_gain).astype(BF16)
    cot = cotangent.reshape(mine, D)
    in_rows = jnp.concatenate(
        [
            my_blocks(input_weight, 0, 1, 1),
            my_blocks(input_weight, DI, 1, 1),
            input_weight[:, 2 * DI : 2 * DI + 2 * N_STATE],
            jnp.pad(
                my_blocks(input_weight, DI + CH, 1, HEAD_DIM), ((0, 0), (0, LANES - heads))
            ),
        ],
        axis=1,
    )
    shard = output_weight.shape[0]
    if span > 1:
        out_rows = cut(output_weight, wide * me_c, wide, 0)
        spread = 0
    else:
        spread = shard // cw
        out_rows = cut(output_weight, cw * lax.rem(me_c, spread), cw, 0)
    normed_all, cot_all, in_w, out_w = call_gather(
        nc, nf, spread, normed.reshape(mine, D), cot, in_rows, out_rows
    )
    normed_all, cot_all = normed_all.reshape(nc * mine, D), cot_all.reshape(nc * mine, D)
    in_w, out_w = in_w.reshape(D, -1), out_w.reshape(cw, D)

    my_columns = lambda a: jnp.concatenate(
        [my_blocks(a, 0, 1, 1), lax.slice_in_dim(a, DI, CH, axis=1)], axis=1
    )
    conv_par = jnp.concatenate(
        [my_columns(conv_w), my_columns(conv_b[None]), jnp.zeros((3, cc), F32)], axis=0
    )
    per_head = lambda a: my_blocks(a, 0, 0, HEAD_DIM)
    pad_heads = lambda a: jnp.pad(a, (0, LANES - heads))[None]
    rate = -jnp.exp(per_head(a_log))
    heads_par = jnp.concatenate(
        [pad_heads(per_head(dt_bias)), pad_heads(rate), jnp.zeros((6, LANES), F32)], axis=0
    )
    chan_par = jnp.concatenate(
        [
            jnp.repeat(per_head(d_skip), HEAD_DIM)[None],
            my_blocks(gate_gain, 0, 0, 1)[None],
            jnp.zeros((6, cw), F32),
        ],
        axis=0,
    )
    seq_lengths = lengths.reshape(seqs)

    proj = dot(normed_all, in_w).astype(BF16).reshape(nc, seqs, length, -1)
    grad_gated = dot(cot_all, out_w, 1, 1).reshape(nc, seqs, length, cw)
    mixed, pre, states, stats = call_forward(
        cw, per, seq_lengths, proj, conv_par, heads_par, chan_par, grad_gated
    )
    totals = add_over_ctx(nc, stats[:, :, 0:2].reshape(chunks * seqs * 2, q)) / DI
    totals = totals.reshape(chunks, seqs, 2, q)
    scale = lax.rsqrt(totals[:, :, 0] + EPS)
    pull = scale * scale * totals[:, :, 1]
    scales = jnp.pad(jnp.stack([scale, pull], axis=2), ((0, 0), (0, 0), (0, 6), (0, 0)))

    by_chunk = lambda a: jnp.moveaxis(
        a.reshape(chunks, seqs, per, length, a.shape[-1]), 2, 1
    ).reshape(nc, seqs, length, a.shape[-1])
    gate = proj[..., :cw].astype(F32)
    g = by_chunk(mixed) * jax.nn.silu(gate)
    gated = (g * by_chunk(scale[..., None]) * chan_par[1]).astype(BF16).reshape(nc * mine, cw)
    branch = dot(gated, out_w).astype(BF16).reshape(nc, mine, D)
    branch, scales = lax.optimization_barrier((branch, scales))
    out = lax.psum_scatter(branch, "ctx", scatter_dimension=0).astype(F32) + source.reshape(mine, D)

    dproj, dconv, dheads, dchan = call_backward(
        cw, per, seq_lengths, proj, conv_par, heads_par, chan_par, grad_gated, mixed, pre, states,
        scales,
    )
    dproj = dproj.reshape(nc * mine, -1)
    dnormed = dot(dproj, in_w, 1, 1).astype(BF16).reshape(nc, mine, D)
    rows = D // (nc * nf)
    gin = dot(normed_all, dproj, 0, 0).astype(BF16).reshape(nc, nf, rows, -1)
    gin = jnp.swapaxes(gin, 0, 1)
    gout = dot(gated, cot_all, 0, 0).astype(BF16).reshape(nf, 2, wide * span // nf // 2, D)
    lanes = lambda a: a.reshape(-1, LANES)
    small = jnp.concatenate(
        [lanes(dconv[: CONV_K + 1, :cw]), lanes(dchan[0:2]), dheads[0:2], lanes(dconv[: CONV_K + 1, cw:])],
        axis=0,
    )
    small_rows = small.shape[0]
    small = jnp.pad(small, ((0, -small_rows % 8), (0, 0)))
    d_hidden, pieces, gout, small_all, gain_all = call_scatter(
        nc, nf, span > 1, dnormed, gin, gout, small, hidden.reshape(mine, D), cot,
        jnp.broadcast_to(norm_gain[None], (8, D)),
    )
    grad_out = gout.reshape(-1, D).astype(F32)

    def ordered(a):
        a = jnp.moveaxis(a.reshape(a.shape[:-1] + (span, -1)), 0, -2)
        return a.reshape(a.shape[:-3] + (-1,))

    grad_in = jnp.concatenate(
        [
            ordered(pieces[:, :, :cw]),
            ordered(pieces[:, :, cw : 2 * cw]),
            jnp.sum(pieces[:, :, 2 * cw : 2 * cw + 2 * N_STATE].astype(F32), axis=0).astype(BF16),
            ordered(pieces[:, :, 2 * cw + 2 * N_STATE : 2 * cw + 2 * N_STATE + heads]),
        ],
        axis=1,
    ).astype(F32)
    at = 0
    taken = []
    for shape in ((CONV_K + 1, cw), (2, cw), (2, LANES), (CONV_K + 1, 2 * N_STATE)):
        n = shape[0] * shape[1] // LANES
        taken.append(small_all[:, at : at + n].reshape((nc,) + shape))
        at += n
    dconv = jnp.concatenate([ordered(taken[0]), jnp.sum(taken[3], axis=0)], axis=1)
    dskip = jnp.sum(taken[1][:, 0].reshape(nc, heads, HEAD_DIM), axis=2)
    shape = hidden.shape
    return (
        out.astype(BF16).reshape(shape),
        d_hidden.reshape(shape),
        jnp.sum(gain_all[:, 0], axis=0),
        grad_in,
        dconv[:CONV_K],
        dconv[CONV_K],
        ordered(taken[2][:, 0, :heads]),
        ordered(taken[2][:, 1, :heads]),
        ordered(dskip),
        ordered(taken[1][:, 1]),
        grad_out,
    )


def solution(mesh):
    tokens, rows, every = P(None, "fsdp", "ctx", None), P("fsdp", None), P()
    spread = P(("ctx", "fsdp"), None)
    in_specs = (
        tokens, tokens, P(None, "fsdp"), every, rows, every, every, every, every, every, every, rows,
    )
    out_specs = (
        tokens, tokens, every, spread, every, every, every, every, every, every, spread,
    )
    return jax.shard_map(local, mesh=mesh, in_specs=in_specs, out_specs=out_specs, check_vma=False)
```

```python
import functools

import jax
import jax.numpy as jnp
from jax import lax
from jax.experimental import pallas as pl
from jax.experimental.pallas import tpu as pltpu
from jax.sharding import PartitionSpec as P

D = 2048
HEADS = 64
HEAD_DIM = 64
N_STATE = 128
CONV_K = 4
DI = 4096
CH = DI + 2 * N_STATE
LANES = 128
EPS = 1e-05
F32 = jnp.float32
BF16 = jnp.bfloat16
EXACT = lax.Precision.HIGHEST
VMEM_LIMIT = 60 * 1024 * 1024


def dot(a, b, ca=1, cb=0):
    return lax.dot_general(
        a.astype(BF16), b.astype(BF16), (((ca,), (cb,)), ((), ())), preferred_element_type=F32
    )


def dot_exact(a, b):
    return lax.dot_general(
        a, b, (((1,), (0,)), ((), ())), precision=EXACT, preferred_element_type=F32
    )


def to_lanes(per_head, width):
    q = per_head.shape[0]
    low = lax.broadcasted_iota(jnp.int32, (q, LANES), 1) < HEAD_DIM
    pairs = []
    for j in range(width // LANES):
        first = jnp.broadcast_to(per_head[:, 2 * j : 2 * j + 1], (q, LANES))
        second = jnp.broadcast_to(per_head[:, 2 * j + 1 : 2 * j + 2], (q, LANES))
        pairs.append(jnp.where(low, first, second))
    return jnp.concatenate(pairs, axis=1)


def head_sum_matrix(width):
    channel = lax.broadcasted_iota(jnp.int32, (width, LANES), 0) // HEAD_DIM
    return (channel == lax.broadcasted_iota(jnp.int32, (width, LANES), 1)).astype(F32)


def split_heads(pair):
    low = lax.broadcasted_iota(jnp.int32, pair.shape, 1) < HEAD_DIM
    zero = jnp.zeros_like(pair)
    return jnp.concatenate([jnp.where(low, pair, zero), jnp.where(low, zero, pair)], axis=0)


def triangle(q, lower):
    rows = lax.broadcasted_iota(jnp.int32, (q, q), 0)
    cols = lax.broadcasted_iota(jnp.int32, (q, q), 1)
    return (rows >= cols) if lower else (rows <= cols)


def softplus(z):
    return jnp.maximum(z, 0.0) + jnp.log(1.0 + jnp.exp(-jnp.abs(z)))


def live_column(lengths_ref, s, chunk, q):
    slots = chunk * q + lax.broadcasted_iota(jnp.int32, (q, LANES), 0)
    return (slots < lengths_ref[s]).astype(F32)


def decays(dt_raw, bias, rate, live):
    q = dt_raw.shape[0]
    z = dt_raw + bias
    step = softplus(z) * live
    cum = dot_exact(triangle(q, True).astype(F32), step * rate)
    return z, step, cum


def head_pick(cw, span, me_c):
    mine, apart, each = cw // HEAD_DIM, HEADS // span, cw // HEAD_DIM // span
    lane = lax.broadcasted_iota(jnp.int32, (LANES, LANES), 1)
    head = (lane // each) * apart + me_c * each + lax.rem(lane, each)
    row = lax.broadcasted_iota(jnp.int32, (LANES, LANES), 0)
    return jnp.logical_and(row == head, lane < mine).astype(F32)


def forward_chunk(cw, chunk, s, lengths, proj, pick, conv_w, heads_par, chan_par, mixed_out, pre_out, state_out, window, state):
    per = 2 if proj.shape[0] % 2 == 0 else 1
    length = proj.shape[2]
    q = per * length
    cc = cw + 2 * N_STATE
    causal = triangle(q, True)
    at = pl.ds(chunk * per, per)
    rows = proj[at, s].reshape(q, proj.shape[3])
    window[s, 8 : 8 + q, :] = rows[:, cw : cw + cc].astype(F32)
    pre = conv_w[CONV_K : CONV_K + 1, :] + conv_w[0:1, :] * window[s, 5 : 5 + q, :]
    for k in range(1, CONV_K):
        pre = pre + conv_w[k : k + 1, :] * window[s, 5 + k : 5 + k + q, :]
    window[s, 0:8, :] = window[s, q : q + 8, :]
    pre_out[chunk, s] = pre
    act = pre * jax.nn.sigmoid(pre)
    x = act[:, :cw]
    b = act[:, cw : cw + N_STATE]
    c = act[:, cw + N_STATE :]
    live = live_column(lengths, s, chunk, q)
    _, step, cum = decays(
        dot(rows[:, cw + cc :], pick[...]), heads_par[0:1, :], heads_par[1:2, :], live
    )
    cum_t = cum.T
    last = cum[q - 1 : q, :]
    u = x * to_lanes(step, cw)
    gram = dot(c, b, 1, 1)
    within = []
    for j in range(cw // LANES):
        kernels = []
        for h in (2 * j, 2 * j + 1):
            spread = jnp.where(causal, cum[:, h : h + 1] - cum_t[h : h + 1, :], -1e30)
            kernels.append((gram * jnp.exp(spread)).astype(BF16))
        both = jnp.concatenate(kernels, axis=1)
        within.append(dot(both, split_heads(u[:, j * LANES : (j + 1) * LANES])))
    before = state[s]
    state_out[chunk, s] = before
    mixed_out[chunk, s] = (
        jnp.concatenate(within, axis=1)
        + dot(c, before) * to_lanes(jnp.exp(cum), cw)
        + chan_par[0:1, :] * x
    )
    left = to_lanes(jnp.exp(last - cum), cw)
    state[s] = before * to_lanes(jnp.exp(last), cw) + dot(b, left * u, 0, 0)


def backward_kernel(
    cw, chunks, lengths, proj, pick, conv_w, heads_par, chan_par, grad_gated, mixed_in, pre_in, state_in,
    scale_in, dproj_out, dconv_out, dheads_out, dchan_out, window, state_grad,
):
    step_id = pl.program_id(0)
    chunk = chunks - 1 - step_id
    seqs = proj.shape[1]
    q = proj.shape[0] * proj.shape[2]
    blocks = proj.shape[0]
    cc = cw + 2 * N_STATE
    causal = triangle(q, True)
    sums = head_sum_matrix(cw)

    @pl.when(step_id == 0)
    def _():
        window[...] = jnp.zeros_like(window)
        state_grad[...] = jnp.zeros_like(state_grad)
        dconv_out[...] = jnp.zeros_like(dconv_out)
        dheads_out[...] = jnp.zeros_like(dheads_out)
        dchan_out[...] = jnp.zeros_like(dchan_out)

    for s in range(seqs):
        rows = proj[:, s].reshape(q, proj.shape[3])
        gate = rows[:, :cw].astype(F32)
        conv_in = rows[:, cw : cw + cc].astype(F32)
        pre = pre_in[0, s]
        mixed = mixed_in[0, s]
        gg = grad_gated[:, s].reshape(q, cw)
        scale = jnp.concatenate(
            [jnp.broadcast_to(scale_in[0, s, 0:1, :], (LANES, q)).T] * (cw // LANES), axis=1
        )
        pull = jnp.concatenate(
            [jnp.broadcast_to(scale_in[0, s, 1:2, :], (LANES, q)).T] * (cw // LANES), axis=1
        )
        sig = jax.nn.sigmoid(gate)
        silu = gate * sig
        g = mixed * silu
        dchan_out[1:2, :] += jnp.sum(gg * g * scale, axis=0, keepdims=True)
        dg = scale * (gg * chan_par[1:2, :] - g * pull)
        gm = dg * silu
        dgate = dg * mixed * (sig * (1.0 + gate * (1.0 - sig)))
        sig_pre = jax.nn.sigmoid(pre)
        act = pre * sig_pre
        x = act[:, :cw]
        b = act[:, cw : cw + N_STATE]
        c = act[:, cw + N_STATE :]
        live = live_column(lengths, s, chunk, q)
        z, step, cum = decays(
            dot(rows[:, cw + cc :], pick[...]), heads_par[0:1, :], heads_par[1:2, :], live
        )
        cum_t = cum.T
        last = cum[q - 1 : q, :]
        step_l = to_lanes(step, cw)
        u = x * step_l
        gram = dot(c, b, 1, 1)
        dchan_out[0:1, :] += jnp.sum(gm * x, axis=0, keepdims=True)
        du = []
        dgram = jnp.zeros((q, q), F32)
        for j in range(cw // LANES):
            at = slice(j * LANES, (j + 1) * LANES)
            dkernels = dot(gm[:, at], split_heads(u[:, at]), 1, 1)
            kernels = []
            for i in range(2):
                h = 2 * j + i
                spread = jnp.where(causal, cum[:, h : h + 1] - cum_t[h : h + 1, :], -1e30)
                decay = jnp.exp(spread)
                dgram = dgram + dkernels[:, i * q : (i + 1) * q] * decay
                kernels.append((gram * decay).astype(BF16))
            both = jnp.concatenate(kernels, axis=0)
            du.append(dot(both, split_heads(gm[:, at]), 0, 0))
        before = state_in[0, s]
        after_grad = state_grad[s]
        v = gm * to_lanes(jnp.exp(cum), cw)
        left = to_lanes(jnp.exp(last - cum), cw)
        du_state = left * dot(b, after_grad)
        du = jnp.concatenate(du, axis=1) + du_state
        dc = dot(dgram, b) + dot(v, before, 1, 1)
        db = dot(dgram, c, 0, 0) + dot(left * u, after_grad, 1, 1)
        end = to_lanes(jnp.exp(last), cw)
        extra = jnp.sum(u * du_state, axis=0, keepdims=True) + end * jnp.sum(
            after_grad * before, axis=0, keepdims=True
        )
        state_grad[s] = end * after_grad + dot(c, v, 0, 0)
        last_row = (lax.broadcasted_iota(jnp.int32, (q, LANES), 0) == q - 1).astype(F32)
        dcum = dot_exact(gm * (mixed - chan_par[0:1, :] * x) - u * du, sums) + last_row * dot_exact(
            jnp.broadcast_to(extra, (8, cw)), sums
        )[0:1, :]
        dlog = dot_exact(triangle(q, False).astype(F32), dcum)
        rate = heads_par[1:2, :]
        dstep = dot_exact(x * du, sums) + dlog * rate
        dheads_out[1:2, :] += jnp.sum(dlog * step * rate, axis=0, keepdims=True)
        dz = dstep * live * jax.nn.sigmoid(z)
        dheads_out[0:1, :] += jnp.sum(dz, axis=0, keepdims=True)
        dx = step_l * du + chan_par[0:1, :] * gm
        dpre = jnp.concatenate([dx, db, dc], axis=1) * (sig_pre * (1.0 + pre * (1.0 - sig_pre)))
        window[s, 0:q, :] = dpre
        dconv_in = jnp.zeros((q, cc), F32)
        for k in range(CONV_K):
            ahead = CONV_K - 1 - k
            moved = window[s, ahead : ahead + q, :]
            dconv_in = dconv_in + conv_w[k : k + 1, :] * moved
            dconv_out[k : k + 1, :] += jnp.sum(conv_in * moved, axis=0, keepdims=True)
        dconv_out[CONV_K : CONV_K + 1, :] += jnp.sum(dpre, axis=0, keepdims=True)
        window[s, q : q + 8, :] = window[s, 0:8, :]
        dproj_out[:, s, :, :cw] = dgate.astype(BF16).reshape(blocks, q // blocks, cw)
        dproj_out[:, s, :, cw : cw + cc] = dconv_in.astype(BF16).reshape(blocks, q // blocks, cc)
        dz = dot(dz, pick[...], 1, 1).astype(BF16)
        dproj_out[:, s, :, cw + cc :] = dz.reshape(blocks, q // blocks, LANES)


def call_backward(
    cw, per, lengths, proj, pick, conv_w, heads_par, chan_par, grad_gated, mixed, pre, states, scales
):
    nc, seqs, length, cols = proj.shape
    chunks, q, cc = nc // per, per * length, cw + 2 * N_STATE
    whole = lambda shape: pl.BlockSpec(shape, lambda i: (0,) * len(shape))
    by_chunk = lambda n: pl.BlockSpec((1, seqs, n[0], n[1]), lambda i: (chunks - 1 - i, 0, 0, 0))
    tokens = lambda n: pl.BlockSpec(
        (per, seqs, length, n), lambda i: (chunks - 1 - i, 0, 0, 0)
    )
    return pl.pallas_call(
        functools.partial(backward_kernel, cw, chunks),
        grid=(chunks,),
        in_specs=[
            pl.BlockSpec(memory_space=pltpu.SMEM),
            tokens(cols),
            whole(pick.shape),
            whole(conv_w.shape),
            whole(heads_par.shape),
            whole(chan_par.shape),
            tokens(cw),
            by_chunk((q, cw)),
            by_chunk((q, cc)),
            by_chunk((N_STATE, cw)),
            by_chunk((8, q)),
        ],
        out_specs=[
            tokens(cols),
            whole((8, cc)),
            whole((8, LANES)),
            whole((8, cw)),
        ],
        out_shape=[
            jax.ShapeDtypeStruct(proj.shape, BF16),
            jax.ShapeDtypeStruct((8, cc), F32),
            jax.ShapeDtypeStruct((8, LANES), F32),
            jax.ShapeDtypeStruct((8, cw), F32),
        ],
        scratch_shapes=[
            pltpu.VMEM((seqs, q + 8, cc), F32),
            pltpu.VMEM((seqs, N_STATE, cw), F32),
        ],
        compiler_params=pltpu.CompilerParams(vmem_limit_bytes=VMEM_LIMIT),
        name="mixer_backward",
    )(lengths, proj, pick, conv_w, heads_par, chan_par, grad_gated, mixed, pre, states, scales)


MESH = pl.DeviceIdType.MESH


class push:
    def __init__(self, src, dst, send_sem, recv_sem, device):
        self.args = (src, dst, send_sem, recv_sem, device, MESH)

    def start(self):
        pltpu.make_async_remote_copy(*self.args).start()

    def wait_send(self):
        pltpu.make_async_remote_copy(*self.args).wait_send()

    def wait_recv(self):
        pltpu.make_async_remote_copy(*self.args).wait_recv()

    def wait(self):
        self.wait_send()
        self.wait_recv()


def greet(devices_and_tests):
    barrier = pltpu.get_barrier_semaphore()
    count = 0
    for device, there in devices_and_tests:
        if there is None:
            pl.semaphore_signal(barrier, inc=1, device_id=device, device_id_type=MESH)
            count = count + 1
        else:
            @pl.when(there)
            def _():
                pl.semaphore_signal(barrier, inc=1, device_id=device, device_id_type=MESH)

            count = count + there.astype(jnp.int32)
    return lambda: pl.semaphore_wait(barrier, count)


def line_of(nc):
    me = lax.axis_index("ctx")
    return nc // 2, me // 2, lax.rem(me, 2)


def square_partners():
    me = lax.axis_index("fsdp")
    high, low = me // 2, lax.rem(me, 2)
    return me, high * 2 + (1 - low), (1 - high) * 2 + low


class LineGather:
    def __init__(self, nc, every, sems):
        self.nz, self.z, self.k = line_of(nc)
        self.every = every
        self.up, self.down, self.side, self.got, self.got_side = sems

    def slot(self, place):
        return self.every.at[2 * place + self.k]

    def copies(self, d, below):
        z, k = self.z, self.k
        origin = z - d if below else z + d
        to = z + 1 if below else z - 1
        on = push(
            self.slot(origin), self.slot(origin), (self.up if below else self.down).at[d],
            self.got.at[origin], {"ctx": 2 * to + k},
        )
        side = push(
            self.slot(origin), self.slot(origin), self.side.at[origin], self.got_side.at[origin],
            {"ctx": 2 * z + 1 - k},
        )
        there = origin >= 0 if below else origin <= self.nz - 1
        further = to <= self.nz - 1 if below else to >= 0
        return on, side, there, further

    def begin(self):
        for below in (True, False):
            on, side, _, further = self.copies(0, below)
            pl.when(further)(on.start)
        side.start()

    def step(self, d):
        for below in (True, False):
            on, side, there, further = self.copies(d, below)

            @pl.when(there)
            def _():
                on.wait_recv()
                pl.when(further)(on.start)
                side.start()

    def sides(self):
        for place in range(self.nz):
            arrived = self.every.at[2 * place + 1 - self.k]
            push(
                arrived, arrived, self.side.at[place], self.got_side.at[place],
                {"ctx": 2 * self.z + 1 - self.k},
            ).wait_recv()

    def end(self):
        for place in range(self.nz):
            arrived = self.every.at[2 * place + 1 - self.k]
            push(
                arrived, arrived, self.side.at[place], self.got_side.at[place],
                {"ctx": 2 * self.z + 1 - self.k},
            ).wait_send()
        for d in range(self.nz - 1):
            for below in (True, False):
                on, _, there, further = self.copies(d, below)
                pl.when(jnp.logical_and(there, further))(on.wait_send)


class SquareGather:
    def __init__(self, nf, every, sems):
        self.nf, self.every = nf, every
        self.send, self.got = sems
        self.half = every.shape[1] // 2

    def peers(self):
        me = lax.axis_index("fsdp")
        if self.nf == 4:
            _, fx, fy = square_partners()
            return [(fx, fx), (fy, fy)]
        return [
            (lax.rem(me + j, self.nf), lax.rem(me + self.nf - j, self.nf))
            for j in range(1, self.nf)
        ]

    def first(self):
        me = lax.axis_index("fsdp")
        for j, (to, frm) in enumerate(self.peers()):
            args = (self.send.at[j], self.got.at[j], {"fsdp": to})
            mine, theirs = self.every.at[me], self.every.at[frm]
            yield push(mine, mine, *args), push(theirs, theirs, *args)

    def second(self):
        me, fx, fy = square_partners()
        pairs = []
        for j, (via, to) in enumerate(((fx, fy), (fy, fx))):
            rows = pl.ds(j * self.half, self.half)
            args = (self.send.at[2 + j], self.got.at[2 + j], {"fsdp": to})
            there, here = self.every.at[via, rows], self.every.at[3 - me, rows]
            pairs.append((push(there, there, *args), push(here, here, *args)))
        return pairs

    def begin(self):
        for out, _ in self.first():
            out.start()

    def step(self):
        for j, (_, arrived) in enumerate(self.first()):
            arrived.wait_recv()
            if self.nf == 4:
                self.second()[j][0].start()

    def far(self):
        if self.nf == 4:
            for _, arrived in self.second():
                arrived.wait_recv()

    def end(self):
        for out, _ in self.first():
            out.wait_send()
        if self.nf == 4:
            for out, _ in self.second():
                out.wait_send()


class SquareSpread:
    def __init__(self, nf, source, every, sems):
        self.nf, self.every = nf, every
        self.send, self.got = sems
        self.mine = lax.axis_index("fsdp") == source

    def copies(self):
        me = lax.axis_index("fsdp")
        return [
            push(
                self.every, self.every, self.send.at[j], self.got.at[0],
                {"fsdp": lax.rem(me + j, self.nf)},
            )
            for j in range(1, self.nf)
        ]

    def begin(self):
        for out in self.copies():
            pl.when(self.mine)(out.start)

    def step(self):
        pass

    def far(self):
        if self.nf > 1:
            pl.when(jnp.logical_not(self.mine))(self.copies()[0].wait_recv)

    def end(self):
        for out in self.copies():
            pl.when(self.mine)(out.wait_send)


class Exchange:
    def __init__(self, axis, n, own, every, sems):
        self.axis, self.n, self.own, self.every = axis, n, own, every
        self.send, self.got = sems

    def copies(self):
        me = lax.axis_index(self.axis)
        for j in range(1, self.n):
            to, frm = lax.rem(me + j, self.n), lax.rem(me + self.n - j, self.n)
            args = (self.send.at[j], self.got.at[j], {self.axis: to})
            yield push(self.own, self.every.at[me], *args), push(self.own, self.every.at[frm], *args)

    def begin(self):
        self.every[lax.axis_index(self.axis)] = self.own[...]
        for out, _ in self.copies():
            out.start()

    def wait(self):
        for out, arrived in self.copies():
            arrived.wait_recv()
            out.wait_send()

    def total(self):
        result = self.every[0]
        for i in range(1, self.n):
            result = result + self.every[i]
        return result


def front_kernel(
    nc, nf, cw, span, lengths, hidden, cot, in_w, tail, out_w, norm_gain, conv_w, conv_b, heads_in, gate_gain,
    normed_out, cot_out, main_out, tail_out, rows_out, proj_out, gg_out, mixed_out, pre_out, states_out,
    scales, conv_par, heads_par, chan_par, pick,
    normed_v, cot_v, main_v, tail_v, rows_v, acc, proj, gg, mixed, pre, states, window, state,
    stats, stats_held,
    line_sems, main_sems, tail_sems, rows_sems, stat_sems, load_sems, keep_sems,
):
    nz, z, k = line_of(nc)
    me_c, me_f = lax.axis_index("ctx"), lax.axis_index("fsdp")
    wide, apart = cw // span, DI // span
    depth = in_w.shape[0]
    seqs, length = proj.shape[1], proj.shape[2]
    per = 2 if nc % 2 == 0 else 1
    q, chunks = per * length, nc // per

    found = [({"ctx": lax.rem(me_c + j, nc)}, None) for j in range(1, nc)]
    found += [({"fsdp": lax.rem(me_f + j, nf)}, None) for j in range(1, nf)]
    met = greet(found)

    loads = []

    def load(src, dst):
        copy = pltpu.make_async_copy(src, dst, load_sems.at[len(loads)])
        copy.start()
        loads.append(copy)

    for part in range(2):
        for i in range(span):
            start = pl.multiple_of(part * DI + i * apart + wide * me_c, LANES)
            load(
                in_w.at[:, pl.ds(start, wide)],
                main_v.at[me_f, :, pl.ds(part * cw + i * wide, wide)],
            )
    load(tail, tail_v.at[me_f])
    weight_loads = len(loads)
    load(cot, cot_v.at[me_c])
    if span > 1:
        load(out_w.at[pl.ds(pl.multiple_of(wide * me_c, 16), wide)], rows_v.at[me_f])
    else:
        lap = out_w.shape[0] // cw
        held = me_f == me_c // lap
        rows_load = pltpu.make_async_copy(
            out_w.at[pl.ds(pl.multiple_of(cw * lax.rem(me_c, lap), 16), cw)], rows_v.at[0],
            load_sems.at[len(loads)],
        )
        pl.when(held)(rows_load.start)

    def norm(i, _):
        at = pl.ds(pl.multiple_of(i * 16, 16), 16)
        src = hidden[at].astype(F32)
        mean = jnp.mean(src * src, axis=1, keepdims=True)
        normed_v[me_c, at] = (src * lax.rsqrt(mean + EPS) * norm_gain[...]).astype(BF16)
        return 0

    lax.fori_loop(0, hidden.shape[0] // 16, norm, 0)

    line = lambda i, every: LineGather(nc, every, [line_sems.at[i, j] for j in range(5)])
    normed_line, cot_line = line(0, normed_v), line(1, cot_v)
    main = SquareGather(nf, main_v, (main_sems.at[0], main_sems.at[1]))
    tails = SquareGather(nf, tail_v, (tail_sems.at[0], tail_sems.at[1]))
    if span > 1:
        rows = SquareGather(nf, rows_v, (rows_sems.at[0], rows_sems.at[1]))
    else:
        rows = SquareSpread(nf, me_c // lap, rows_v.at[0], (rows_sems.at[0], rows_sems.at[1]))
    kept = []

    def keep(src, dst):
        copy = pltpu.make_async_copy(src, dst, keep_sems.at[len(kept)])
        copy.start()
        kept.append(copy)

    for copy in loads[:weight_loads]:
        copy.wait()
    met()
    main.begin()
    normed_line.begin()
    tails.begin()

    pick[...] = head_pick(cw, span, me_c)
    conv_par[...] = jnp.zeros_like(conv_par)
    chan_par[...] = jnp.zeros_like(chan_par)
    for i in range(span):
        here = pl.ds(i * wide, wide)
        there = pl.ds(pl.multiple_of(i * apart + wide * me_c, LANES), wide)
        conv_par[0:CONV_K, here] = conv_w[:, there]
        conv_par[CONV_K : CONV_K + 1, here] = conv_b[:, there]
        chan_par[1:2, here] = gate_gain[:, there]
    conv_par[0:CONV_K, cw:] = conv_w[:, DI:CH]
    conv_par[CONV_K : CONV_K + 1, cw:] = conv_b[:, DI:CH]
    picked = dot_exact(heads_in[...], pick[...])
    heads_par[0:1, :] = picked[0:1, :]
    heads_par[1:2, :] = -jnp.exp(picked[1:2, :])
    heads_par[2:8, :] = jnp.zeros((6, LANES), F32)
    chan_par[0:1, :] = to_lanes(picked[2:3, :], cw)
    window[...] = jnp.zeros_like(window)
    state[...] = jnp.zeros_like(state)

    for copy in loads[weight_loads:]:
        copy.wait()
    if span == 1:
        pl.when(held)(rows_load.wait)
    for d in range(1, nz):
        normed_line.step(d)
        if d == 1:
            cot_line.begin()
    if nz == 1:
        cot_line.begin()
    main.step()
    tails.step()
    rows.begin()
    normed_line.sides()

    def project(depths, first, last):
        def body(c, _):
            sums = None
            for f in depths:
                a = normed_v[c, :, pl.ds(pl.multiple_of(f * depth, LANES), depth)]
                both = jnp.concatenate([dot(a, main_v[f]), dot(a, tail_v[f])], axis=1)
                sums = both if sums is None else sums + both
            if not first:
                sums = sums + acc[c]
            if last:
                proj[c] = sums.astype(BF16).reshape(proj.shape[1:])
            else:
                acc[c] = sums
            return 0

        lax.fori_loop(0, nc, body, 0)

    if nf == 4:
        _, fx, fy = square_partners()
        project([me_f], True, False)
        project([fx, fy], False, False)
        keep(normed_v, normed_out)
        if nz > 1:
            cot_line.step(1)
        main.far()
        tails.far()
        project([3 - me_f], False, True)
    else:
        keep(normed_v, normed_out)
        for j in range(nf):
            project([lax.rem(me_f + j, nf)], j == 0, j == nf - 1)
        if nz > 1:
            cot_line.step(1)
    keep(main_v, main_out)
    keep(tail_v, tail_out)
    keep(proj, proj_out)

    waiting = [lambda d=d: cot_line.step(d) for d in range(2, nz)]
    waiting.insert(min(1, len(waiting)), rows.step)
    for chunk in range(chunks):
        for s in range(seqs):
            forward_chunk(
                cw, chunk, s, lengths, proj, pick, conv_par, heads_par, chan_par, mixed, pre, states,
                window, state,
            )
        if waiting:
            waiting.pop(0)()
    while waiting:
        waiting.pop(0)()
    keep(mixed, mixed_out)
    keep(pre, pre_out)
    keep(states, states_out)

    rows.far()
    keep(rows_v, rows_out)
    cot_line.sides()
    keep(cot_v, cot_out)
    weights = rows_v[...].reshape(cw, D)
    for c in range(nc):
        gg[c] = dot(cot_v[c], weights, 1, 1).reshape(gg.shape[1:])
    keep(gg, gg_out)
    ones = jnp.ones((8, cw), F32)
    across = lambda a: lax.dot_general(
        ones, a, (((1,), (1,)), ((), ())), precision=EXACT, preferred_element_type=F32
    )[0:1, :]
    for chunk in range(chunks):
        for s in range(seqs):
            at = pl.ds(chunk * per, per)
            gate = proj[at, s].reshape(q, proj.shape[3])[:, :cw].astype(F32)
            g = mixed[chunk, s] * gate * jax.nn.sigmoid(gate)
            row = 2 * (chunk * seqs + s)
            stats[row : row + 1, :] = across(g * g)
            stats[row + 1 : row + 2, :] = across(
                gg[at, s].reshape(q, cw) * chan_par[1:2, :] * g
            )
    exchange = Exchange("ctx", nc, stats, stats_held, (stat_sems.at[0], stat_sems.at[1]))
    exchange.begin()
    exchange.wait()
    totals = exchange.total() * (1.0 / DI)
    for chunk in range(chunks):
        for s in range(seqs):
            row = 2 * (chunk * seqs + s)
            scale = lax.rsqrt(totals[row : row + 1, :] + EPS)
            scales[chunk, s, 0:1, :] = scale
            scales[chunk, s, 1:2, :] = scale * scale * totals[row + 1 : row + 2, :]
            scales[chunk, s, 2:8, :] = jnp.zeros((6, q), F32)
    for part in (main, tails, rows, normed_line, cot_line):
        part.end()
    for copy in kept:
        copy.wait()


def call_front(nc, nf, cw, span, lengths, hidden, cot, in_w, tail, out_w, norm_gain, conv_w, conv_b, heads_in, gate_gain):
    nz = nc // 2
    mine = hidden.shape[0]
    seqs = lengths.shape[0]
    length = mine // seqs
    per = 2 if nc % 2 == 0 else 1
    q, chunks, cc = per * length, nc // per, cw + 2 * N_STATE
    depth, wide = in_w.shape[0], cw // span
    cols = 2 * cw + tail.shape[1]
    vmem = pl.BlockSpec(memory_space=pltpu.VMEM)
    anywhere = pl.BlockSpec(memory_space=pl.ANY)
    dma = pltpu.SemaphoreType.DMA
    big = [
        ((nc, mine, D), BF16),
        ((nc, mine, D), BF16),
        ((nf, depth, 2 * cw), BF16),
        ((nf, depth, tail.shape[1]), BF16),
        ((span, wide, D), BF16),
        ((nc, seqs, length, cols), BF16),
        ((nc, seqs, length, cw), F32),
        ((chunks, seqs, q, cw), F32),
        ((chunks, seqs, q, cc), F32),
        ((chunks, seqs, N_STATE, cw), F32),
    ]
    small = [
        ((chunks, seqs, 8, q), F32),
        ((8, cc), F32),
        ((8, LANES), F32),
        ((8, cw), F32),
        ((LANES, LANES), F32),
    ]
    held = big[:5] + [((nc, mine, cols), F32)] + big[5:]
    held += [
        ((seqs, q + 8, cc), F32),
        ((seqs, N_STATE, cw), F32),
        ((2 * chunks * seqs, q), F32),
        ((nc, 2 * chunks * seqs, q), F32),
    ]
    places = max(nf, 4)
    return pl.pallas_call(
        functools.partial(front_kernel, nc, nf, cw, span),
        in_specs=[pl.BlockSpec(memory_space=pltpu.SMEM), vmem, vmem, anywhere, anywhere, anywhere]
        + [vmem] * 5,
        out_specs=[anywhere] * len(big) + [vmem] * len(small),
        out_shape=[jax.ShapeDtypeStruct(*a) for a in big + small],
        scratch_shapes=[pltpu.VMEM(*a) for a in held]
        + [
            dma((2, 5, nz)),
            dma((2, places)),
            dma((2, places)),
            dma((2, places)),
            dma((2, nc)),
            dma((2 * span + 3,)),
            dma((10,)),
        ],
        compiler_params=pltpu.CompilerParams(
            collective_id=0, has_side_effects=True, vmem_limit_bytes=VMEM_LIMIT
        ),
        name="front",
    )(lengths, hidden, cot, in_w, tail, out_w, norm_gain, conv_w, conv_b, heads_in, gate_gain)


def add_rows(into, other, rows=16):
    def body(i, _):
        at = pl.ds(pl.multiple_of(i * rows, rows), rows)
        into[at] = (into[at].astype(F32) + other[at].astype(F32)).astype(into.dtype)
        return 0

    lax.fori_loop(0, into.shape[0] // rows, body, 0)


class LineReduce:
    def __init__(self, nc, parts, acc, landed, sems):
        self.nz, self.z, self.k = line_of(nc)
        self.parts, self.acc, self.landed = parts, acc, landed
        self.side, self.got_side, self.send, self.got = sems

    def to_side(self, place):
        other = {"ctx": 2 * self.z + 1 - self.k}
        return push(
            self.parts.at[2 * place + 1 - self.k], self.acc.at[place], self.side.at[place],
            self.got_side.at[place], other,
        )

    def begin(self):
        for place in range(self.nz):
            self.to_side(place).start()

    def merge(self):
        for place in range(self.nz):
            self.to_side(place).wait_recv()
            add_rows(self.acc.at[place], self.parts.at[2 * place + self.k])

    def along(self, place, up):
        way = 0 if up else 1
        return push(
            self.acc.at[place], self.landed.at[way, place], self.send.at[way, place],
            self.got.at[way, place], {"ctx": 2 * (self.z + (1 if up else -1)) + self.k},
        )

    def arrive(self, place, up, into):
        self.along(place, up).wait_recv()
        add_rows(into, self.landed.at[0 if up else 1, place])

    def moves(self):
        for i in range(self.nz - 1):
            yield i, self.nz - 1 - i, True
            yield i, i, False

    def step(self, i):
        z, nz = self.z, self.nz
        for at, place, up in self.moves():
            if at != i:
                continue

            @pl.when(z < place if up else z > place)
            def _():
                @pl.when(z > 0 if up else z < nz - 1)
                def _():
                    self.arrive(place, up, self.acc.at[place])

                self.along(place, up).start()

    def final(self, total):
        z, nz = self.z, self.nz
        total[...] = self.acc[z].astype(F32)

        @pl.when(z > 0)
        def _():
            self.arrive(z, True, total)

        @pl.when(z < nz - 1)
        def _():
            self.arrive(z, False, total)

    def end(self):
        for place in range(self.nz):
            self.to_side(place).wait_send()
        for _, place, up in self.moves():
            pl.when(self.z < place if up else self.z > place)(self.along(place, up).wait_send)


class SquareReduce:
    def __init__(self, nf, parts, landed, total, sems):
        self.nf, self.parts, self.landed, self.total = nf, parts, landed, total
        self.send, self.got = sems
        self.half = parts.shape[1] // 2

    @staticmethod
    def landing(nf, shape):
        blocks, rows, cols = shape
        return (6, blocks // 2, rows, cols) if nf == 4 else (nf, blocks, rows, cols)

    def copy(self, n, src, to):
        return push(src, self.landed.at[n], self.send.at[n], self.got.at[n], {"fsdp": to})

    def way(self, h):
        me, fx, fy = square_partners()
        first, second = (fx, fy) if h == 0 else (fy, fx)
        return me, first, second, pl.ds(h * self.half, self.half)

    def firsts(self, h):
        me, first, second, at = self.way(h)
        return (
            self.copy(3 * h, self.parts.at[3 - me, at], first),
            self.copy(3 * h + 1, self.parts.at[first, at], first),
        )

    def second_(self, h):
        _, _, second, _ = self.way(h)
        return self.copy(3 * h + 2, self.landed.at[3 * h], second)

    def others(self):
        me = lax.axis_index("fsdp")
        tos = [lax.rem(me + j, self.nf) for j in range(1, self.nf)]
        return [self.copy(j + 1, self.parts.at[to], to) for j, to in enumerate(tos)]

    def begin(self):
        if self.nf == 4:
            for i in range(2):
                for h in range(2):
                    self.firsts(h)[i].start()
        else:
            for out in self.others():
                out.start()

    def add(self, into, other):
        for b in range(into.shape[0]):
            add_rows(into.at[b], other.at[b], min(16, into.shape[1]))

    def step(self):
        if self.nf == 4:
            for h in range(2):
                _, _, second, at = self.way(h)
                self.firsts(h)[0].wait_recv()
                self.add(self.landed.at[3 * h], self.parts.at[second, at])
                self.second_(h).start()

    def final(self, h):
        me = lax.axis_index("fsdp")
        at = pl.ds(h * self.half, self.half)
        if self.nf == 4:
            self.firsts(h)[1].wait_recv()
            into = self.total.at[at]
            into[...] = self.parts[me, at]
            self.add(into, self.landed.at[3 * h + 1])
            self.second_(h).wait_recv()
            self.add(into, self.landed.at[3 * h + 2])
        else:
            into = self.total.at[at]
            into[...] = self.parts[me, at]
            for j, out in enumerate(self.others()):
                if h == 0:
                    out.wait_recv()
                self.add(into, self.landed.at[j + 1, at])

    def end(self):
        if self.nf == 4:
            for h in range(2):
                for out in (*self.firsts(h), self.second_(h)):
                    out.wait_send()
        else:
            for out in self.others():
                out.wait_send()


def scatter_kernel(
    nc, nf, strided, dnormed, gin, gout, small, hidden, cot, gain,
    d_hidden, pieces, gout_mine, small_all, gain_all,
    acc, landed, total, in_landed, in_sum, out_landed, out_sum,
    small_held, small_sum, gain_held, gain_own, gain_sum,
    line_side, line_sems, in_sems, out_sems, piece_sems, small_sems, here,
):
    nz, _, _ = line_of(nc)
    me_c, me_f = lax.axis_index("ctx"), lax.axis_index("fsdp")
    line = LineReduce(
        nc, dnormed, acc, landed,
        (line_side.at[0], line_side.at[1], line_sems.at[0], line_sems.at[1]),
    )
    ins = SquareReduce(nf, gin, in_landed, in_sum, (in_sems.at[0], in_sems.at[1]))
    outs = SquareReduce(nf, gout, out_landed, out_sum, (out_sems.at[0], out_sems.at[1]))
    pair = lambda i: (small_sems.at[i, 0], small_sems.at[i, 1])
    smalls = (
        Exchange("fsdp", nf, small, small_held, pair(0)),
        Exchange("ctx", nc, small_sum, small_all, pair(1)),
    )
    gains = (
        Exchange("fsdp", nf, gain_own, gain_held, pair(2)),
        Exchange("ctx", nc, gain_sum, gain_all, pair(3)),
    )
    found = [({"ctx": lax.rem(me_c + j, nc)}, None) for j in range(1, nc)]
    found += [({"fsdp": lax.rem(me_f + j, nf)}, None) for j in range(1, nf)]
    if strided:
        lead, place = me_f * nc + me_c, me_c * nf + me_f
        target = {"ctx": lead // nf, "fsdp": lax.rem(lead, nf)}
        source = {"ctx": lax.rem(place, nc), "fsdp": place // nc}
        away = lead != place
        found += [(target, away), (source, away)]
    greet(found)()

    ins.begin()
    line.begin()
    smalls[0].begin()
    line.merge()
    for i in range(nz - 1):
        line.step(i)
        if i == 0:
            smalls[0].wait()
            small_sum[...] = smalls[0].total()
            smalls[1].begin()
    ins.step()
    outs.begin()
    line.final(total)
    gain_own[...] = jnp.zeros_like(gain_own)
    block = 16

    def norm_back(i, _):
        at = pl.ds(pl.multiple_of(i * block, block), block)
        src = hidden[at].astype(F32)
        dn = total[at]
        scale = lax.rsqrt(jnp.mean(src * src, axis=1, keepdims=True) + EPS)
        h = dn * gain[0:1, :]
        pull = jnp.mean(h * src, axis=1, keepdims=True) * scale * scale
        d_hidden[at] = scale * (h - src * pull) + cot[at].astype(F32)
        gain_own[0:1, :] += jnp.sum(dn * src * scale, axis=0, keepdims=True)
        return 0

    lax.fori_loop(0, hidden.shape[0] // block, norm_back, 0)
    gains[0].begin()

    def piece(c):
        return push(
            in_sum.at[c], pieces.at[me_c], piece_sems.at[0, c], piece_sems.at[1, me_c], {"ctx": c}
        )

    def piece_from(c):
        return push(in_sum.at[c], pieces.at[c], piece_sems.at[0, c], piece_sems.at[1, c], {"ctx": c})

    stay = pltpu.make_async_copy(in_sum.at[me_c], pieces.at[me_c], here.at[0])
    half = nc // 2
    for h in range(2):
        ins.final(h)
        for j in range(half):
            c = h * half + lax.rem(me_c + j, half)
            pl.when(c != me_c)(piece(c).start)
            pl.when(c == me_c)(stay.start)
    gains[0].wait()
    gain_sum[...] = gains[0].total()
    gains[1].begin()
    outs.step()
    outs.final(0)
    outs.final(1)
    if strided:
        route = push(out_sum, gout_mine, piece_sems.at[0, nc], piece_sems.at[1, nc], target)
        pl.when(away)(route.start)

        @pl.when(jnp.logical_not(away))
        def _():
            pltpu.make_async_copy(out_sum, gout_mine, here.at[1]).start()

    else:
        gout_mine[...] = out_sum[...]
    smalls[1].wait()
    gains[1].wait()
    line.end()
    ins.end()
    outs.end()
    stay.wait()
    for c in range(nc):

        @pl.when(c != me_c)
        def _():
            piece_from(c).wait_recv()
            piece(c).wait_send()

    if strided:

        @pl.when(away)
        def _():
            route.wait_recv()
            route.wait_send()

        @pl.when(jnp.logical_not(away))
        def _():
            pltpu.make_async_copy(out_sum, gout_mine, here.at[1]).wait()


def call_scatter(nc, nf, strided, dnormed, gin, gout, small, hidden, cot, gain):
    nz = nc // 2
    mine = hidden.shape[0]
    vmem = pl.BlockSpec(memory_space=pltpu.VMEM)
    dma = pltpu.SemaphoreType.DMA
    count = max(nf, 6)
    return pl.pallas_call(
        functools.partial(scatter_kernel, nc, nf, strided),
        in_specs=[vmem] * 7,
        out_specs=[vmem] * 5,
        out_shape=[
            jax.ShapeDtypeStruct((mine, D), F32),
            jax.ShapeDtypeStruct(gin.shape[1:], BF16),
            jax.ShapeDtypeStruct(gout.shape[1:], BF16),
            jax.ShapeDtypeStruct((nc,) + small.shape, F32),
            jax.ShapeDtypeStruct((nc, 8, D), F32),
        ],
        scratch_shapes=[
            pltpu.VMEM((nz, mine, D), BF16),
            pltpu.VMEM((2, nz, mine, D), BF16),
            pltpu.VMEM((mine, D), F32),
            pltpu.VMEM(SquareReduce.landing(nf, gin.shape[1:]), BF16),
            pltpu.VMEM(gin.shape[1:], BF16),
            pltpu.VMEM(SquareReduce.landing(nf, gout.shape[1:]), BF16),
            pltpu.VMEM(gout.shape[1:], BF16),
            pltpu.VMEM((nf,) + small.shape, F32),
            pltpu.VMEM(small.shape, F32),
            pltpu.VMEM((nf, 8, D), F32),
            pltpu.VMEM((8, D), F32),
            pltpu.VMEM((8, D), F32),
            dma((2, nz)),
            dma((2, 2, nz)),
            dma((2, count)),
            dma((2, count)),
            dma((2, nc + 1)),
            dma((4, 2, max(nc, nf))),
            dma((2,)),
        ],
        compiler_params=pltpu.CompilerParams(
            collective_id=2, has_side_effects=True, vmem_limit_bytes=VMEM_LIMIT
        ),
        name="scatter",
    )(dnormed, gin, gout, small, hidden, cot, gain)


def rms_scale(values, gain_vec):
    return values * lax.rsqrt(jnp.mean(values * values, axis=-1, keepdims=True) + EPS) * gain_vec


def local(
    hidden,
    cotangent,
    lengths,
    norm_gain,
    input_weight,
    conv_w,
    conv_b,
    dt_bias,
    a_log,
    d_skip,
    gate_gain,
    output_weight,
):
    nc, nf = lax.axis_size("ctx"), lax.axis_size("fsdp")
    me_c, me_f = lax.axis_index("ctx"), lax.axis_index("fsdp")
    mb_count, seq_rows, length = hidden.shape[0], hidden.shape[1], hidden.shape[2]
    seqs = mb_count * seq_rows
    mine = seqs * length
    heads = HEADS // nc
    cw = DI // nc
    cc = cw + 2 * N_STATE
    per = 2 if nc % 2 == 0 else 1
    q = per * length
    chunks = nc // per

    span = nf if (DI // nf // nc) % LANES == 0 else 1
    wide = cw // span
    source = hidden.astype(F32).reshape(seqs, length, D)
    cot = cotangent.reshape(mine, D)
    tail = input_weight[:, 2 * DI :]
    tail = jnp.pad(tail, ((0, 0), (0, -tail.shape[1] % LANES)))
    heads_in = jnp.pad(jnp.stack([dt_bias, a_log, d_skip]), ((0, 5), (0, LANES - HEADS)))
    seq_lengths = lengths.reshape(seqs)
    (
        normed_all, cot_all, main_w, tail_w, out_w, proj, grad_gated, mixed, pre, states,
        scales, conv_par, heads_par, chan_par, pick,
    ) = call_front(
        nc, nf, cw, span, seq_lengths, hidden.reshape(mine, D), cot, input_weight, tail, output_weight,
        norm_gain[None], conv_w, conv_b[None], heads_in, gate_gain[None],
    )
    normed_all, cot_all = normed_all.reshape(nc * mine, D), cot_all.reshape(nc * mine, D)
    out_w = out_w.reshape(cw, D)
    scale = scales[:, :, 0]

    by_chunk = lambda a: jnp.moveaxis(
        a.reshape(chunks, seqs, per, length, a.shape[-1]), 2, 1
    ).reshape(nc, seqs, length, a.shape[-1])
    gate = proj[..., :cw].astype(F32)
    g = by_chunk(mixed) * jax.nn.silu(gate)
    gated = (g * by_chunk(scale[..., None]) * chan_par[1]).astype(BF16).reshape(nc * mine, cw)
    branch = dot(gated, out_w).astype(BF16).reshape(nc, mine, D)
    branch, scales = lax.optimization_barrier((branch, scales))
    out = lax.psum_scatter(branch, "ctx", scatter_dimension=0).astype(F32) + source.reshape(mine, D)

    dproj, dconv, dheads, dchan = call_backward(
        cw, per, seq_lengths, proj, pick, conv_par, heads_par, chan_par, grad_gated, mixed, pre,
        states, scales,
    )
    dproj = dproj.reshape(nc * mine, -1)
    dnormed = dot(dproj[:, : 2 * cw], main_w.reshape(D, -1), 1, 1)
    dnormed = dnormed + dot(dproj[:, 2 * cw :], tail_w.reshape(D, -1), 1, 1)
    dnormed = dnormed.astype(BF16).reshape(nc, mine, D)
    rows = D // (nc * nf)
    gin = dot(normed_all, dproj, 0, 0).astype(BF16).reshape(nc, nf, rows, -1)
    gin = jnp.swapaxes(gin, 0, 1)
    gout = dot(gated, cot_all, 0, 0).astype(BF16).reshape(nf, 2, wide * span // nf // 2, D)
    lanes = lambda a: a.reshape(-1, LANES)
    small = jnp.concatenate(
        [lanes(dconv[: CONV_K + 1, :cw]), lanes(dchan[0:2]), dheads[0:2], lanes(dconv[: CONV_K + 1, cw:])],
        axis=0,
    )
    small_rows = small.shape[0]
    small = jnp.pad(small, ((0, -small_rows % 8), (0, 0)))
    d_hidden, pieces, gout, small_all, gain_all = call_scatter(
        nc, nf, span > 1, dnormed, gin, gout, small, hidden.reshape(mine, D), cot,
        jnp.broadcast_to(norm_gain[None], (8, D)),
    )
    grad_out = gout.reshape(-1, D).astype(F32)

    def ordered(a):
        a = jnp.moveaxis(a.reshape(a.shape[:-1] + (span, -1)), 0, -2)
        return a.reshape(a.shape[:-3] + (-1,))

    grad_in = jnp.concatenate(
        [
            ordered(pieces[:, :, :cw]),
            ordered(pieces[:, :, cw : 2 * cw]),
            jnp.sum(pieces[:, :, 2 * cw : 2 * cw + 2 * N_STATE + HEADS].astype(F32), axis=0).astype(
                BF16
            ),
        ],
        axis=1,
    ).astype(F32)
    at = 0
    taken = []
    for shape in ((CONV_K + 1, cw), (2, cw), (2, LANES), (CONV_K + 1, 2 * N_STATE)):
        n = shape[0] * shape[1] // LANES
        taken.append(small_all[:, at : at + n].reshape((nc,) + shape))
        at += n
    dconv = jnp.concatenate([ordered(taken[0]), jnp.sum(taken[3], axis=0)], axis=1)
    dskip = jnp.sum(taken[1][:, 0].reshape(nc, heads, HEAD_DIM), axis=2)
    shape = hidden.shape
    return (
        out.astype(BF16).reshape(shape),
        d_hidden.reshape(shape),
        jnp.sum(gain_all[:, 0], axis=0),
        grad_in,
        dconv[:CONV_K],
        dconv[CONV_K],
        ordered(taken[2][:, 0, :heads]),
        ordered(taken[2][:, 1, :heads]),
        ordered(dskip),
        ordered(taken[1][:, 1]),
        grad_out,
    )


def solution(mesh):
    tokens, rows, every = P(None, "fsdp", "ctx", None), P("fsdp", None), P()
    spread = P(("ctx", "fsdp"), None)
    in_specs = (
        tokens, tokens, P(None, "fsdp"), every, rows, every, every, every, every, every, every, rows,
    )
    out_specs = (
        tokens, tokens, every, spread, every, every, every, every, every, every, spread,
    )
    return jax.shard_map(local, mesh=mesh, in_specs=in_specs, out_specs=out_specs, check_vma=False)
```

```python
import functools

import jax
import jax.numpy as jnp
from jax import lax
from jax.experimental import pallas as pl
from jax.experimental.pallas import tpu as pltpu
from jax.sharding import PartitionSpec as P

D = 2048
HEADS = 64
HEAD_DIM = 64
N_STATE = 128
CONV_K = 4
DI = 4096
CH = DI + 2 * N_STATE
LANES = 128
EPS = 1e-05
F32 = jnp.float32
BF16 = jnp.bfloat16
EXACT = lax.Precision.HIGHEST
VMEM_LIMIT = 63 * 1024 * 1024


def dot(a, b, ca=1, cb=0):
    return lax.dot_general(
        a.astype(BF16), b.astype(BF16), (((ca,), (cb,)), ((), ())), preferred_element_type=F32
    )


def dot_exact(a, b):
    return lax.dot_general(
        a, b, (((1,), (0,)), ((), ())), precision=EXACT, preferred_element_type=F32
    )


def to_lanes(per_head, width):
    q = per_head.shape[0]
    low = lax.broadcasted_iota(jnp.int32, (q, LANES), 1) < HEAD_DIM
    pairs = []
    for j in range(width // LANES):
        first = jnp.broadcast_to(per_head[:, 2 * j : 2 * j + 1], (q, LANES))
        second = jnp.broadcast_to(per_head[:, 2 * j + 1 : 2 * j + 2], (q, LANES))
        pairs.append(jnp.where(low, first, second))
    return jnp.concatenate(pairs, axis=1)


def head_sum_matrix(width):
    channel = lax.broadcasted_iota(jnp.int32, (width, LANES), 0) // HEAD_DIM
    return (channel == lax.broadcasted_iota(jnp.int32, (width, LANES), 1)).astype(F32)


def split_heads(pair):
    low = lax.broadcasted_iota(jnp.int32, pair.shape, 1) < HEAD_DIM
    zero = jnp.zeros_like(pair)
    return jnp.concatenate([jnp.where(low, pair, zero), jnp.where(low, zero, pair)], axis=0)


def triangle(q, lower):
    rows = lax.broadcasted_iota(jnp.int32, (q, q), 0)
    cols = lax.broadcasted_iota(jnp.int32, (q, q), 1)
    return (rows >= cols) if lower else (rows <= cols)


def softplus(z):
    return jnp.maximum(z, 0.0) + jnp.log(1.0 + jnp.exp(-jnp.abs(z)))


def live_column(lengths_ref, s, chunk, q):
    slots = chunk * q + lax.broadcasted_iota(jnp.int32, (q, LANES), 0)
    return (slots < lengths_ref[s]).astype(F32)


def decays(dt_raw, bias, rate, live):
    q = dt_raw.shape[0]
    z = dt_raw + bias
    step = softplus(z) * live
    cum = dot_exact(triangle(q, True).astype(F32), step * rate)
    return z, step, cum


def head_pick(cw, span, me_c):
    mine, apart, each = cw // HEAD_DIM, HEADS // span, cw // HEAD_DIM // span
    lane = lax.broadcasted_iota(jnp.int32, (HEADS, LANES), 1)
    head = (lane // each) * apart + me_c * each + lax.rem(lane, each)
    row = lax.broadcasted_iota(jnp.int32, (HEADS, LANES), 0)
    return jnp.logical_and(row == head, lane < mine).astype(F32)


def forward_chunk(cw, chunk, s, lengths, proj, pick, conv_w, heads_par, chan_par, mixed_out, state_out, window, state):
    per = 2 if proj.shape[0] % 2 == 0 else 1
    length = proj.shape[2]
    q = per * length
    cc = cw + 2 * N_STATE
    causal = triangle(q, True)
    at = pl.ds(chunk * per, per)
    rows = proj[at, s].reshape(q, proj.shape[3])
    window[s, 8 : 8 + q, :] = rows[:, cw : cw + cc].astype(F32)
    pre = conv_w[CONV_K : CONV_K + 1, :] + conv_w[0:1, :] * window[s, 5 : 5 + q, :]
    for k in range(1, CONV_K):
        pre = pre + conv_w[k : k + 1, :] * window[s, 5 + k : 5 + k + q, :]
    window[s, 0:8, :] = window[s, q : q + 8, :]
    act = pre * jax.nn.sigmoid(pre)
    x = act[:, :cw]
    b = act[:, cw : cw + N_STATE]
    c = act[:, cw + N_STATE :]
    live = live_column(lengths, s, chunk, q)
    _, step, cum = decays(
        dot(rows[:, cw + cc :], pick[...]), heads_par[0:1, :], heads_par[1:2, :], live
    )
    cum_t = cum.T
    last = cum[q - 1 : q, :]
    u = x * to_lanes(step, cw)
    gram = dot(c, b, 1, 1)
    within = []
    for j in range(cw // LANES):
        kernels = []
        for h in (2 * j, 2 * j + 1):
            spread = jnp.where(causal, cum[:, h : h + 1] - cum_t[h : h + 1, :], -1e30)
            kernels.append((gram * jnp.exp(spread)).astype(BF16))
        both = jnp.concatenate(kernels, axis=1)
        within.append(dot(both, split_heads(u[:, j * LANES : (j + 1) * LANES])))
    before = state[s]
    state_out[chunk, s] = before.astype(BF16)
    mixed_out[chunk, s] = (
        jnp.concatenate(within, axis=1)
        + dot(c, before) * to_lanes(jnp.exp(cum), cw)
        + chan_par[0:1, :] * x
    )
    left = to_lanes(jnp.exp(last - cum), cw)
    state[s] = before * to_lanes(jnp.exp(last), cw) + dot(b, left * u, 0, 0)


def gate_chunk(cw, chunk, s, proj, scales, chan_par, gg, mixed, gated, dchan):
    per = proj.shape[0] // mixed.shape[0]
    length = proj.shape[2]
    q = per * length
    at = pl.ds(chunk * per, per)
    gate = proj[at, s, :, :cw].reshape(q, cw).astype(F32)
    column = lambda i: jnp.concatenate(
        [jnp.broadcast_to(scales[chunk, s, i : i + 1, :], (LANES, q)).T] * (cw // LANES), axis=1
    )
    scale, pull = column(0), column(1)
    grad = gg[at, s].reshape(q, cw)
    sig = jax.nn.sigmoid(gate)
    silu = gate * sig
    m = mixed[chunk, s]
    g = m * silu
    normal = g * scale
    gain = chan_par[1:2, :]
    gated[at, s] = (normal * gain).astype(BF16).reshape(per, length, cw)
    dchan[1:2, :] += jnp.sum(grad * normal, axis=0, keepdims=True)
    dg = scale * (grad * gain - g * pull)
    gg[at, s] = (dg * silu).reshape(per, length, cw)
    dgate = dg * m * (sig * (1.0 + gate * (1.0 - sig)))
    proj[at, s, :, :cw] = dgate.astype(BF16).reshape(per, length, cw)


def backward_chunk(
    cw, chunk, s, lengths, proj, pick, conv_w, heads_par, chan_par, gm_in, mixed_in, state_in,
    dconv, dheads, dchan, window, ahead, state_grad,
):
    per = proj.shape[0] // mixed_in.shape[0]
    length = proj.shape[2]
    q = per * length
    cc = cw + 2 * N_STATE
    causal = triangle(q, True)
    sums = head_sum_matrix(cw)
    at = pl.ds(chunk * per, per)
    rows = proj[at, s, :, cw:].reshape(q, proj.shape[3] - cw)
    conv_in = rows[:, :cc].astype(F32)
    mixed = mixed_in[chunk, s]
    gm = gm_in[at, s].reshape(q, cw)
    if chunk:
        tail = proj[chunk * per - 1, s, length - 16 :, cw : cw + cc].astype(F32)
        window[s, 0:8, :] = tail[8:16]
    else:
        window[s, 0:8, :] = jnp.zeros((8, cc), F32)
    window[s, 8 : 8 + q, :] = conv_in
    pre = conv_w[CONV_K : CONV_K + 1, :] + conv_w[0:1, :] * window[s, 5 : 5 + q, :]
    for k in range(1, CONV_K):
        pre = pre + conv_w[k : k + 1, :] * window[s, 5 + k : 5 + k + q, :]
    sig_pre = jax.nn.sigmoid(pre)
    act = pre * sig_pre
    x = act[:, :cw]
    b = act[:, cw : cw + N_STATE]
    c = act[:, cw + N_STATE :]
    live = live_column(lengths, s, chunk, q)
    z, step, cum = decays(dot(rows[:, cc:], pick[...]), heads_par[0:1, :], heads_par[1:2, :], live)
    cum_t = cum.T
    last = cum[q - 1 : q, :]
    step_l = to_lanes(step, cw)
    u = x * step_l
    gram = dot(c, b, 1, 1)
    dchan[0:1, :] += jnp.sum(gm * x, axis=0, keepdims=True)
    du = []
    dgram = jnp.zeros((q, q), F32)
    for j in range(cw // LANES):
        lanes = slice(j * LANES, (j + 1) * LANES)
        dkernels = dot(gm[:, lanes], split_heads(u[:, lanes]), 1, 1)
        kernels = []
        for i in range(2):
            h = 2 * j + i
            spread = jnp.where(causal, cum[:, h : h + 1] - cum_t[h : h + 1, :], -1e30)
            decay = jnp.exp(spread)
            dgram = dgram + dkernels[:, i * q : (i + 1) * q] * decay
            kernels.append((gram * decay).astype(BF16))
        both = jnp.concatenate(kernels, axis=0)
        du.append(dot(both, split_heads(gm[:, lanes]), 0, 0))
    before = state_in[chunk, s].astype(F32)
    after_grad = state_grad[s]
    v = gm * to_lanes(jnp.exp(cum), cw)
    left = to_lanes(jnp.exp(last - cum), cw)
    du_state = left * dot(b, after_grad)
    du = jnp.concatenate(du, axis=1) + du_state
    dc = dot(dgram, b) + dot(v, before, 1, 1)
    db = dot(dgram, c, 0, 0) + dot(left * u, after_grad, 1, 1)
    end = to_lanes(jnp.exp(last), cw)
    extra = jnp.sum(u * du_state, axis=0, keepdims=True) + end * jnp.sum(
        after_grad * before, axis=0, keepdims=True
    )
    state_grad[s] = end * after_grad + dot(c, v, 0, 0)
    last_row = (lax.broadcasted_iota(jnp.int32, (q, LANES), 0) == q - 1).astype(F32)
    dcum = dot_exact(gm * (mixed - chan_par[0:1, :] * x) - u * du, sums) + last_row * dot_exact(
        jnp.broadcast_to(extra, (8, cw)), sums
    )[0:1, :]
    dlog = dot_exact(triangle(q, False).astype(F32), dcum)
    rate = heads_par[1:2, :]
    dstep = dot_exact(x * du, sums) + dlog * rate
    dheads[1:2, :] += jnp.sum(dlog * step * rate, axis=0, keepdims=True)
    dz = dstep * live * jax.nn.sigmoid(z)
    dheads[0:1, :] += jnp.sum(dz, axis=0, keepdims=True)
    dx = step_l * du + chan_par[0:1, :] * gm
    dpre = jnp.concatenate([dx, db, dc], axis=1) * (sig_pre * (1.0 + pre * (1.0 - sig_pre)))
    ahead[s, 0:q, :] = dpre
    dconv_in = jnp.zeros((q, cc), F32)
    for k in range(CONV_K):
        first = CONV_K - 1 - k
        moved = ahead[s, first : first + q, :]
        dconv_in = dconv_in + conv_w[k : k + 1, :] * moved
        dconv[k : k + 1, :] += jnp.sum(conv_in * moved, axis=0, keepdims=True)
    dconv[CONV_K : CONV_K + 1, :] += jnp.sum(dpre, axis=0, keepdims=True)
    ahead[s, q : q + 8, :] = ahead[s, 0:8, :]
    proj[at, s, :, cw : cw + cc] = dconv_in.astype(BF16).reshape(per, length, cc)
    dz = dot(dz, pick[...], 1, 1).astype(BF16)
    proj[at, s, :, cw + cc :] = dz.reshape(per, length, HEADS)


def column_tiles(n, body, size=256):
    if n <= size:
        body(0, n)
        return

    def one(j, _):
        body(pl.multiple_of(j * size, size), size)
        return 0

    lax.fori_loop(0, n // size, one, 0)


MESH = pl.DeviceIdType.MESH


class push:
    def __init__(self, src, dst, send_sem, recv_sem, device):
        self.args = (src, dst, send_sem, recv_sem, device, MESH)

    def start(self):
        pltpu.make_async_remote_copy(*self.args).start()

    def wait_send(self):
        pltpu.make_async_remote_copy(*self.args).wait_send()

    def wait_recv(self):
        pltpu.make_async_remote_copy(*self.args).wait_recv()

    def wait(self):
        self.wait_send()
        self.wait_recv()


def greet(devices_and_tests):
    return signal_all(pltpu.get_barrier_semaphore(), devices_and_tests)


def signal_all(barrier, devices_and_tests):
    count = 0
    for device, there in devices_and_tests:
        if there is None:
            pl.semaphore_signal(barrier, inc=1, device_id=device, device_id_type=MESH)
            count = count + 1
        else:
            @pl.when(there)
            def _():
                pl.semaphore_signal(barrier, inc=1, device_id=device, device_id_type=MESH)

            count = count + there.astype(jnp.int32)
    return lambda: pl.semaphore_wait(barrier, count)


def line_of(nc):
    me = lax.axis_index("ctx")
    return nc // 2, me // 2, lax.rem(me, 2)


def square_partners():
    me = lax.axis_index("fsdp")
    high, low = me // 2, lax.rem(me, 2)
    return me, high * 2 + (1 - low), (1 - high) * 2 + low


class LineGather:
    def __init__(self, nc, every, sems):
        self.nz, self.z, self.k = line_of(nc)
        self.every = every
        self.up, self.down, self.side, self.got, self.got_side = sems

    def slot(self, place):
        return self.every.at[2 * place + self.k]

    def copies(self, d, below):
        z, k = self.z, self.k
        origin = z - d if below else z + d
        to = z + 1 if below else z - 1
        on = push(
            self.slot(origin), self.slot(origin), (self.up if below else self.down).at[d],
            self.got.at[origin], {"ctx": 2 * to + k},
        )
        side = push(
            self.slot(origin), self.slot(origin), self.side.at[origin], self.got_side.at[origin],
            {"ctx": 2 * z + 1 - k},
        )
        there = origin >= 0 if below else origin <= self.nz - 1
        further = to <= self.nz - 1 if below else to >= 0
        return on, side, there, further

    def begin(self):
        for below in (True, False):
            on, side, _, further = self.copies(0, below)
            pl.when(further)(on.start)
        side.start()

    def step(self, d):
        for below in (True, False):
            on, side, there, further = self.copies(d, below)

            @pl.when(there)
            def _():
                on.wait_recv()
                pl.when(further)(on.start)
                side.start()

    def sides(self, least, most):
        for place in range(self.nz):
            arrived = self.every.at[2 * place + 1 - self.k]
            apart = jnp.abs(place - self.z)
            pl.when(jnp.logical_and(apart >= least, apart <= most))(
                push(
                    arrived, arrived, self.side.at[place], self.got_side.at[place],
                    {"ctx": 2 * self.z + 1 - self.k},
                ).wait_recv
            )

    def end(self):
        for place in range(self.nz):
            arrived = self.every.at[2 * place + 1 - self.k]
            push(
                arrived, arrived, self.side.at[place], self.got_side.at[place],
                {"ctx": 2 * self.z + 1 - self.k},
            ).wait_send()
        for d in range(self.nz - 1):
            for below in (True, False):
                on, _, there, further = self.copies(d, below)
                pl.when(jnp.logical_and(there, further))(on.wait_send)


class SquareGather:
    def __init__(self, nf, every, sems):
        self.nf, self.every = nf, every
        self.send, self.got = sems
        self.half = every.shape[1] // 2

    def peers(self):
        me = lax.axis_index("fsdp")
        if self.nf == 4:
            _, fx, fy = square_partners()
            return [(fx, fx), (fy, fy)]
        return [
            (lax.rem(me + j, self.nf), lax.rem(me + self.nf - j, self.nf))
            for j in range(1, self.nf)
        ]

    def first(self):
        me = lax.axis_index("fsdp")
        for j, (to, frm) in enumerate(self.peers()):
            args = (self.send.at[j], self.got.at[j], {"fsdp": to})
            mine, theirs = self.every.at[me], self.every.at[frm]
            yield push(mine, mine, *args), push(theirs, theirs, *args)

    def second(self):
        me, fx, fy = square_partners()
        pairs = []
        for j, (via, to) in enumerate(((fx, fy), (fy, fx))):
            rows = pl.ds(j * self.half, self.half)
            args = (self.send.at[2 + j], self.got.at[2 + j], {"fsdp": to})
            there, here = self.every.at[via, rows], self.every.at[3 - me, rows]
            pairs.append((push(there, there, *args), push(here, here, *args)))
        return pairs

    def begin(self):
        for out, _ in self.first():
            out.start()

    def step(self):
        for j, (_, arrived) in enumerate(self.first()):
            arrived.wait_recv()
            if self.nf == 4:
                self.second()[j][0].start()

    def far(self):
        if self.nf == 4:
            for _, arrived in self.second():
                arrived.wait_recv()

    def end(self):
        for out, _ in self.first():
            out.wait_send()
        if self.nf == 4:
            for out, _ in self.second():
                out.wait_send()


class ChipGather:
    def __init__(self, nf, every, sems):
        self.nf, self.every = nf, every
        me = lax.axis_index("ctx")
        self.core, self.other = lax.rem(me, 2), {"ctx": me + 1 - 2 * lax.rem(me, 2)}
        self.half = every.shape[1] // 2
        mine = every.at[:, pl.ds(pl.multiple_of(self.core * self.half, 16), self.half)]
        self.square = SquareGather(nf, mine, sems[:2])
        self.send, self.got = sems[2:]

    def side(self, f, core):
        part = self.every.at[f, pl.ds(pl.multiple_of(core * self.half, 16), self.half)]
        return push(part, part, self.send.at[f], self.got.at[f], self.other)

    def near(self):
        return [frm for _, frm in self.square.peers()]

    def begin(self):
        self.square.begin()

    def step(self):
        self.square.step()
        for f in self.near():
            self.side(f, self.core).start()

    def sides(self):
        for f in self.near():
            self.side(f, 1 - self.core).wait_recv()

    def far(self):
        self.square.far()
        if self.nf == 4:
            f = 3 - lax.axis_index("fsdp")
            self.side(f, self.core).start()
            self.side(f, 1 - self.core).wait_recv()

    def end(self):
        self.square.end()
        for f in self.near():
            self.side(f, self.core).wait_send()
        if self.nf == 4:
            self.side(3 - lax.axis_index("fsdp"), self.core).wait_send()


class SquareSpread:
    def __init__(self, nf, source, every, sems):
        self.nf, self.every = nf, every
        self.send, self.got = sems
        self.mine = lax.axis_index("fsdp") == source

    def copies(self):
        me = lax.axis_index("fsdp")
        return [
            push(
                self.every, self.every, self.send.at[j], self.got.at[0],
                {"fsdp": lax.rem(me + j, self.nf)},
            )
            for j in range(1, self.nf)
        ]

    def begin(self):
        for out in self.copies():
            pl.when(self.mine)(out.start)

    def step(self):
        pass

    def far(self):
        if self.nf > 1:
            pl.when(jnp.logical_not(self.mine))(self.copies()[0].wait_recv)

    def end(self):
        for out in self.copies():
            pl.when(self.mine)(out.wait_send)


class Exchange:
    def __init__(self, axis, n, own, every, sems):
        self.axis, self.n, self.own, self.every = axis, n, own, every
        self.send, self.got = sems

    def copies(self):
        me = lax.axis_index(self.axis)
        for j in range(1, self.n):
            to, frm = lax.rem(me + j, self.n), lax.rem(me + self.n - j, self.n)
            args = (self.send.at[j], self.got.at[j], {self.axis: to})
            yield push(self.own, self.every.at[me], *args), push(self.own, self.every.at[frm], *args)

    def begin(self):
        self.every[lax.axis_index(self.axis)] = self.own[...]
        for out, _ in self.copies():
            out.start()

    def wait(self):
        for out, arrived in self.copies():
            arrived.wait_recv()
            out.wait_send()

    def total(self):
        result = self.every[0]
        for i in range(1, self.n):
            result = result + self.every[i]
        return result


def front_kernel(
    nc, nf, cw, span, lengths, hidden, cot, in_w, out_w, norm_gain, conv_w, conv_b, heads_in, gate_gain,
    normed_out, cot_out, main_out, tail_out, rows_out, proj_out, gg_out, mixed_out, states_out,
    scales, conv_par, heads_par, chan_par, pick,
    normed_t, cot_v, main_v, tail_v, rows_v, normed_v, acc, proj, gg, mixed, states, window, state,
    stats, stats_held,
    line_sems, main_sems, tail_sems, rows_sems, stat_sems, load_sems, keep_sems,
):
    nz, z, k = line_of(nc)
    me_c, me_f = lax.axis_index("ctx"), lax.axis_index("fsdp")
    wide, apart = cw // span, DI // span
    depth = in_w.shape[1]
    seqs, length = proj.shape[1], proj.shape[2]
    per = 2 if nc % 2 == 0 else 1
    q, chunks = per * length, nc // per

    found = [({"ctx": lax.rem(me_c + j, nc)}, None) for j in range(1, nc)]
    found += [({"fsdp": lax.rem(me_f + j, nf)}, None) for j in range(1, nf)]
    met = greet(found)

    loads = []

    def load(src, dst):
        copy = pltpu.make_async_copy(src, dst, load_sems.at[len(loads)])
        copy.start()
        loads.append(copy)

    for part in range(2):
        for i in range(span):
            start = pl.multiple_of(part * DI + i * apart + wide * me_c, LANES)
            load(in_w.at[pl.ds(start, wide)], main_v.at[me_f, pl.ds(part * cw + i * wide, wide)])
    load(in_w.at[pl.ds(2 * DI, tail_v.shape[1])], tail_v.at[me_f])
    weight_loads = len(loads)
    load(cot, cot_v.at[me_c])
    if span > 1:
        load(out_w.at[pl.ds(pl.multiple_of(wide * me_c, 16), wide)], rows_v.at[me_f])
    else:
        lap = out_w.shape[0] // cw
        held = me_f == me_c // lap
        rows_load = pltpu.make_async_copy(
            out_w.at[pl.ds(pl.multiple_of(cw * lax.rem(me_c, lap), 16), cw)], rows_v.at[0],
            load_sems.at[len(loads)],
        )
        pl.when(held)(rows_load.start)

    def norm(i, _):
        at = pl.ds(pl.multiple_of(i * 16, 16), 16)
        src = hidden[at].astype(F32)
        mean = jnp.mean(src * src, axis=1, keepdims=True)
        normed_v[me_c, at] = (src * lax.rsqrt(mean + EPS) * norm_gain[...]).astype(BF16)
        return 0

    lax.fori_loop(0, hidden.shape[0] // 16, norm, 0)

    line = lambda i, every: LineGather(nc, every, [line_sems.at[i, j] for j in range(5)])
    normed_line, cot_line = line(0, normed_v), line(1, cot_v)
    main = SquareGather(nf, main_v, (main_sems.at[0], main_sems.at[1]))
    tails = ChipGather(nf, tail_v, [tail_sems.at[i] for i in range(4)])
    if span > 1:
        rows = SquareGather(nf, rows_v, (rows_sems.at[0], rows_sems.at[1]))
    else:
        rows = SquareSpread(nf, me_c // lap, rows_v.at[0], (rows_sems.at[0], rows_sems.at[1]))
    kept = []

    def keep(src, dst):
        copy = pltpu.make_async_copy(src, dst, keep_sems.at[len(kept)])
        copy.start()
        kept.append(copy)

    for copy in loads[:weight_loads]:
        copy.wait()
    met()
    main.begin()
    normed_line.begin()
    tails.begin()

    pick[...] = head_pick(cw, span, me_c)
    conv_par[...] = jnp.zeros_like(conv_par)
    chan_par[...] = jnp.zeros_like(chan_par)
    for i in range(span):
        here = pl.ds(i * wide, wide)
        there = pl.ds(pl.multiple_of(i * apart + wide * me_c, LANES), wide)
        conv_par[0:CONV_K, here] = conv_w[:, there]
        conv_par[CONV_K : CONV_K + 1, here] = conv_b[:, there]
        chan_par[1:2, here] = gate_gain[:, there]
    conv_par[0:CONV_K, cw:] = conv_w[:, DI:CH]
    conv_par[CONV_K : CONV_K + 1, cw:] = conv_b[:, DI:CH]
    picked = dot_exact(heads_in[...], pick[...])
    heads_par[0:1, :] = picked[0:1, :]
    heads_par[1:2, :] = -jnp.exp(picked[1:2, :])
    heads_par[2:8, :] = jnp.zeros((6, LANES), F32)
    chan_par[0:1, :] = to_lanes(picked[2:3, :], cw)
    window[...] = jnp.zeros_like(window)
    state[...] = jnp.zeros_like(state)

    for copy in loads[weight_loads:]:
        copy.wait()
    if span == 1:
        pl.when(held)(rows_load.wait)
    slots = nc * normed_v.shape[1]

    def project(depths, first, last):
        def part(weights, base):
            def body(start, size):
                sums = None
                for f in depths:
                    a = normed_v[:, :, pl.ds(pl.multiple_of(f * depth, LANES), depth)]
                    term = dot(a.reshape(slots, depth), weights[f, pl.ds(start, size)], 1, 1)
                    sums = term if sums is None else sums + term
                here = pl.ds(base + start, size)
                if not first:
                    sums = sums + acc[:, here]
                if last:
                    proj[:, :, :, here] = sums.astype(BF16).reshape(proj.shape[:3] + (size,))
                else:
                    acc[:, here] = sums

            return body

        column_tiles(2 * cw, part(main_v, 0))
        column_tiles(tail_v.shape[1], part(tail_v, 2 * cw), tail_v.shape[1])

    for d in range(1, min(nz, 3)):
        normed_line.step(d)
    cot_line.begin()
    main.step()
    tails.step()
    for d in range(3, nz):
        normed_line.step(d)
    normed_line.sides(0, nz)
    tails.sides()
    if nf == 4:
        _, fx, fy = square_partners()
        project([me_f, fx, fy], True, False)
    if nz > 1:
        cot_line.step(1)
    main.far()
    tails.far()
    rows.begin()
    if nf == 4:
        project([3 - me_f], False, True)
    else:
        for j in range(nf):
            project([lax.rem(me_f + j, nf)], j == 0, j == nf - 1)
    keep(main_v, main_out)
    keep(tail_v, tail_out)
    keep(proj, proj_out)

    waiting = [lambda d=d: cot_line.step(d) for d in range(2, nz)]
    for chunk in range(chunks):
        for s in range(seqs):
            forward_chunk(
                cw, chunk, s, lengths, proj, pick, conv_par, heads_par, chan_par, mixed, states,
                window, state,
            )
        if chunk == chunks // 2 - 1:
            rows.step()
            if waiting:
                waiting.pop(0)()
    keep(mixed, mixed_out)
    keep(states, states_out)
    mine = normed_v.shape[1]

    def turn(c, _):
        normed_t[:, pl.ds(pl.multiple_of(c * mine, LANES), mine)] = normed_v[c].T
        return 0

    lax.fori_loop(0, nc, turn, 0)
    keep(normed_t, normed_out)
    rows.far()
    keep(rows_v, rows_out)
    while waiting:
        waiting.pop(0)()
    cot_line.sides(0, nz)
    keep(cot_v, cot_out)
    cots = cot_v[...].reshape(slots, D)
    weights = rows_v[...].reshape(cw, D)
    half = min(cw, 256)
    for i in range(cw // half):
        gg[:, :, :, i * half : (i + 1) * half] = dot(
            cots, weights[i * half : (i + 1) * half], 1, 1
        ).reshape(gg.shape[:3] + (half,))
    keep(gg, gg_out)

    def across(a):
        total = a[:, :LANES]
        for j in range(1, cw // LANES):
            total = total + a[:, j * LANES : (j + 1) * LANES]
        return jnp.sum(total.T, axis=0, keepdims=True)

    for chunk in range(chunks):
        for s in range(seqs):
            at = pl.ds(chunk * per, per)
            gate = proj[at, s, :, :cw].reshape(q, cw).astype(F32)
            g = mixed[chunk, s] * gate * jax.nn.sigmoid(gate)
            row = 2 * (chunk * seqs + s)
            stats[row : row + 1, :] = across(g * g)
            stats[row + 1 : row + 2, :] = across(
                gg[at, s].reshape(q, cw) * chan_par[1:2, :] * g
            )
    exchange = Exchange("ctx", nc, stats, stats_held, (stat_sems.at[0], stat_sems.at[1]))
    exchange.begin()
    exchange.wait()
    totals = exchange.total() * (1.0 / DI)
    for chunk in range(chunks):
        for s in range(seqs):
            row = 2 * (chunk * seqs + s)
            scale = lax.rsqrt(totals[row : row + 1, :] + EPS)
            scales[chunk, s, 0:1, :] = scale
            scales[chunk, s, 1:2, :] = scale * scale * totals[row + 1 : row + 2, :]
            scales[chunk, s, 2:8, :] = jnp.zeros((6, q), F32)
    for part in (main, tails, rows, normed_line, cot_line):
        part.end()
    for copy in kept:
        copy.wait()


def call_front(nc, nf, cw, span, lengths, hidden, cot, in_w, out_w, norm_gain, conv_w, conv_b, heads_in, gate_gain):
    nz = nc // 2
    mine = hidden.shape[0]
    seqs = lengths.shape[0]
    length = mine // seqs
    per = 2 if nc % 2 == 0 else 1
    q, chunks, cc = per * length, nc // per, cw + 2 * N_STATE
    depth, wide, ends = in_w.shape[1], cw // span, in_w.shape[0] - 2 * DI
    cols = 2 * cw + ends
    vmem = pl.BlockSpec(memory_space=pltpu.VMEM)
    anywhere = pl.BlockSpec(memory_space=pl.ANY)
    dma = pltpu.SemaphoreType.DMA
    big = [
        ((D, nc * mine), BF16),
        ((nc, mine, D), BF16),
        ((nf, 2 * cw, depth), BF16),
        ((nf, ends, depth), BF16),
        ((span, wide, D), BF16),
        ((nc, seqs, length, cols), BF16),
        ((nc, seqs, length, cw), F32),
        ((chunks, seqs, q, cw), F32),
        ((chunks, seqs, N_STATE, cw), BF16),
    ]
    small = [
        ((chunks, seqs, 8, q), F32),
        ((8, cc), F32),
        ((8, LANES), F32),
        ((8, cw), F32),
        ((HEADS, LANES), F32),
    ]
    held = big[:5] + [((nc, mine, D), BF16), ((nc * mine, cols), F32)] + big[5:]
    held += [
        ((seqs, q + 8, cc), F32),
        ((seqs, N_STATE, cw), F32),
        ((2 * chunks * seqs, q), F32),
        ((nc, 2 * chunks * seqs, q), F32),
    ]
    places = max(nf, 4)
    return pl.pallas_call(
        functools.partial(front_kernel, nc, nf, cw, span),
        in_specs=[pl.BlockSpec(memory_space=pltpu.SMEM), vmem, vmem, anywhere, anywhere]
        + [vmem] * 5,
        out_specs=[anywhere] * len(big) + [vmem] * len(small),
        out_shape=[jax.ShapeDtypeStruct(*a) for a in big + small],
        scratch_shapes=[pltpu.VMEM(*a) for a in held]
        + [
            dma((2, 5, nz)),
            dma((2, places)),
            dma((4, places)),
            dma((2, places)),
            dma((2, nc)),
            dma((2 * span + 3,)),
            dma((10,)),
        ],
        compiler_params=pltpu.CompilerParams(
            collective_id=0, has_side_effects=True, vmem_limit_bytes=VMEM_LIMIT
        ),
        name="front",
    )(lengths, hidden, cot, in_w, out_w, norm_gain, conv_w, conv_b, heads_in, gate_gain)


def add_rows(into, other, rows=16):
    def body(i, _):
        at = pl.ds(pl.multiple_of(i * rows, rows), rows)
        into[at] = (into[at].astype(F32) + other[at].astype(F32)).astype(into.dtype)
        return 0

    lax.fori_loop(0, into.shape[0] // rows, body, 0)


class LineReduce:
    def __init__(self, nc, parts, acc, landed, sems):
        self.nz, self.z, self.k = line_of(nc)
        self.parts, self.acc, self.landed = parts, acc, landed
        self.side, self.got_side, self.send, self.got = sems

    def to_side(self, place):
        other = {"ctx": 2 * self.z + 1 - self.k}
        return push(
            self.parts.at[2 * place + 1 - self.k], self.acc.at[place], self.side.at[place],
            self.got_side.at[place], other,
        )

    def begin(self):
        for place in range(self.nz):
            self.to_side(place).start()

    def merge(self):
        for place in range(self.nz):
            self.to_side(place).wait_recv()
            add_rows(self.acc.at[place], self.parts.at[2 * place + self.k])

    def along(self, place, up):
        way = 0 if up else 1
        slot = place if up else jnp.where(place == self.z - 1, self.nz, place)
        return push(
            self.acc.at[place], self.landed.at[slot], self.send.at[way, place],
            self.got.at[way, place], {"ctx": 2 * (self.z + (1 if up else -1)) + self.k},
        )

    def arrive(self, place, up, into, slot=None):
        self.along(place, up).wait_recv()
        add_rows(into, self.landed.at[place if slot is None else slot])

    def step(self, tick):
        z, nz = self.z, self.nz
        for place in range(nz):
            for up in (True, False):
                at = tick - (nz - 1 - place) if up else nz - 1 + place - tick
                if not (0 <= at < place if up else place < at <= nz - 1):
                    continue
                first, before = (0, place + 1) if up else (nz - 1, place - 1)

                @pl.when(z == at)
                def _():
                    if at != first:
                        self.arrive(place, up, self.acc.at[place])
                    elif 0 <= before <= nz - 1:
                        self.along(before, up).wait_send()
                    self.along(place, up).start()

    def final(self, total):
        z, nz = self.z, self.nz
        total[...] = self.acc[z].astype(F32)

        @pl.when(z > 0)
        def _():
            self.arrive(z, True, total)

        @pl.when(z < nz - 1)
        def _():
            self.arrive(z, False, total, nz)

    def end(self):
        for place in range(self.nz):
            self.to_side(place).wait_send()
        for place in range(self.nz):
            last = self.nz - 1
            self_up = jnp.logical_and(self.z < place, jnp.logical_or(self.z > 0, place == 1))
            self_down = jnp.logical_and(
                self.z > place, jnp.logical_or(self.z < last, place == last - 1)
            )
            pl.when(self_up)(self.along(place, True).wait_send)
            pl.when(self_down)(self.along(place, False).wait_send)


class SquareReduce:
    def __init__(self, nf, parts, landed, total, sems, inner=False):
        self.nf, self.parts, self.landed, self.total = nf, parts, landed, total
        self.send, self.got = sems
        self.inner = inner
        self.half = total.shape[0] // 2

    def part(self, f, at):
        return self.parts.at[at, f] if self.inner else self.parts.at[f, at]

    @staticmethod
    def landing(nf, shape):
        blocks, rows, cols = shape
        return (6, blocks // 2, rows, cols) if nf == 4 else (nf, blocks, rows, cols)

    def copy(self, n, src, to):
        return push(src, self.landed.at[n], self.send.at[n], self.got.at[n], {"fsdp": to})

    def way(self, h):
        me, fx, fy = square_partners()
        first, second = (fx, fy) if h == 0 else (fy, fx)
        return me, first, second, pl.ds(h * self.half, self.half)

    def firsts(self, h):
        me, first, second, at = self.way(h)
        return (
            self.copy(3 * h, self.part(3 - me, at), first),
            self.copy(3 * h + 1, self.part(first, at), first),
        )

    def second_(self, h):
        _, _, second, _ = self.way(h)
        return self.copy(3 * h + 2, self.landed.at[3 * h], second)

    def others(self):
        me = lax.axis_index("fsdp")
        tos = [lax.rem(me + j, self.nf) for j in range(1, self.nf)]
        every = pl.ds(0, self.total.shape[0])
        return [self.copy(j + 1, self.part(to, every), to) for j, to in enumerate(tos)]

    def begin(self):
        if self.nf == 4:
            for i in range(2):
                for h in range(2):
                    self.firsts(h)[i].start()
        else:
            for out in self.others():
                out.start()

    def add(self, into, other):
        for b in range(into.shape[0]):
            add_rows(into.at[b], other.at[b], min(16, into.shape[1]))

    def step(self):
        if self.nf == 4:
            for h in range(2):
                _, _, second, at = self.way(h)
                self.firsts(h)[0].wait_recv()
                self.add(self.landed.at[3 * h], self.part(second, at))
                self.second_(h).start()

    def final(self, h):
        me = lax.axis_index("fsdp")
        at = pl.ds(h * self.half, self.half)
        if self.nf == 4:
            self.firsts(h)[1].wait_recv()
            into = self.total.at[at]
            into[...] = self.part(me, at)[...]
            self.add(into, self.landed.at[3 * h + 1])
            self.second_(h).wait_recv()
            self.add(into, self.landed.at[3 * h + 2])
        else:
            into = self.total.at[at]
            into[...] = self.part(me, at)[...]
            for j, out in enumerate(self.others()):
                if h == 0:
                    out.wait_recv()
                self.add(into, self.landed.at[j + 1, at])

    def end(self):
        if self.nf == 4:
            for h in range(2):
                for out in (*self.firsts(h), self.second_(h)):
                    out.wait_send()
        else:
            for out in self.others():
                out.wait_send()


class Deal:
    def __init__(self, nc, parts, pieces, sems, here):
        self.nc, self.parts, self.pieces = nc, parts, pieces
        self.send, self.got, self.here = sems[0], sems[1], here
        self.me = lax.axis_index("ctx")

    def to(self, c):
        return push(
            self.parts.at[c], self.pieces.at[self.me], self.send.at[c], self.got.at[self.me], {"ctx": c}
        )

    def stay(self):
        return pltpu.make_async_copy(self.parts.at[self.me], self.pieces.at[self.me], self.here)

    def start(self, h):
        half = self.nc // 2
        for j in range(half):
            c = h * half + lax.rem(self.me + j, half)
            pl.when(c != self.me)(self.to(c).start)

            @pl.when(c == self.me)
            def _():
                self.stay().start()

    def wait(self):
        self.stay().wait()
        for c in range(self.nc):

            @pl.when(c != self.me)
            def _():
                push(
                    self.parts.at[c], self.pieces.at[c], self.send.at[c], self.got.at[c], {"ctx": c}
                ).wait()


def back_kernel(
    nc, nf, cw, span, lengths, hidden, cot, gain, scales, conv_par, heads_par, chan_par, pick,
    normed_in, cot_in, main_in, tail_in, rows_in, proj_in, gg_in, mixed_in, states_in,
    out, d_hidden, grad_in, grad_out, dconv_w, dconv_b, dgain, dheads_out, dnorm_gain,
    normed_t, cot_v, main_v, tail_v, rows_v, proj, gg, mixed, states,
    gated, gated_t, branch, gout, gate_parts, x_parts, acc, landed, total,
    gout_landed, gout_sum, gate_landed, gate_sum, x_landed, x_sum, gate_pieces, x_pieces, gout_mine,
    window, ahead, state_grad, dconv, dheads, dchan,
    small, small_held, small_sum, small_all, gains, gains_held, gains_sum, gains_all,
    load_sems, cot_sems, main_sems, line_sems, way_sems, square_sems, deal_sems, small_sems, route_sems,
    here, line_free,
):
    nz, _, _ = line_of(nc)
    me_c, me_f = lax.axis_index("ctx"), lax.axis_index("fsdp")
    wide, apart = cw // span, DI // span
    cc, ends = cw + 2 * N_STATE, tail_v.shape[1]
    seqs, length = proj.shape[1], proj.shape[2]
    chunks = mixed.shape[0]
    slots = nc * seqs * length

    found = [({"ctx": lax.rem(me_c + j, nc)}, None) for j in range(1, nc)]
    found += [({"fsdp": lax.rem(me_f + j, nf)}, None) for j in range(1, nf)]
    if span > 1:
        lead, place = me_f * nc + me_c, me_c * nf + me_f
        target = {"ctx": lead // nf, "fsdp": lax.rem(lead, nf)}
        source = {"ctx": lax.rem(place, nc), "fsdp": place // nc}
        away = lead != place
        found += [(target, away), (source, away)]
    met = greet(found)

    loads = []
    for i, (src, dst) in enumerate((
        (proj_in, proj), (mixed_in, mixed), (gg_in, gg), (rows_in, rows_v), (normed_in, normed_t),
        (states_in, states),
    )):
        copy = pltpu.make_async_copy(src, dst, load_sems.at[i])
        copy.start()
        loads.append(copy)

    quarter = cot_v.shape[3]

    def cot_part(i):
        return pltpu.make_async_copy(
            cot_in.at[:, :, pl.ds(pl.multiple_of(i * quarter, LANES), quarter)],
            cot_v.at[lax.rem(i, 2)], cot_sems.at[lax.rem(i, 2)],
        )

    def weights_part(f):
        slot = lax.rem(f, 2)
        return (
            pltpu.make_async_copy(main_in.at[f], main_v.at[slot], main_sems.at[0, slot]),
            pltpu.make_async_copy(tail_in.at[f], tail_v.at[slot], main_sems.at[1, slot]),
        )

    def start_weights(f):
        for copy in weights_part(f):
            copy.start()

    for i in range(2):
        cot_part(i).start()
    lines = [
        LineReduce(
            nc, branch, acc, landed,
            (line_sems.at[i, 0], line_sems.at[i, 1], way_sems.at[i, 0], way_sems.at[i, 1]),
        )
        for i in range(2)
    ]
    out_line, dn_line = lines
    square = lambda i, *refs, inner: SquareReduce(
        nf, *refs, (square_sems.at[i, 0], square_sems.at[i, 1]), inner
    )
    gout_square = square(0, gout, gout_landed, gout_sum, inner=False)
    gate_square = square(1, gate_parts, gate_landed, gate_sum, inner=True)
    x_square = square(2, x_parts, x_landed, x_sum, inner=True)
    gate_deal = Deal(nc, gate_sum, gate_pieces, (deal_sems.at[0, 0], deal_sems.at[0, 1]), here.at[0])
    x_deal = Deal(nc, x_sum, x_pieces, (deal_sems.at[1, 0], deal_sems.at[1, 1]), here.at[1])
    pair = lambda i: (small_sems.at[i, 0], small_sems.at[i, 1])
    smalls = (
        Exchange("fsdp", nf, small, small_held, pair(0)),
        Exchange("ctx", nc, small_sum, small_all, pair(1)),
    )
    gain_sums = (
        Exchange("fsdp", nf, gains, gains_held, pair(2)),
        Exchange("ctx", nc, gains_sum, gains_all, pair(3)),
    )

    for ref in (window, ahead, state_grad, dconv, dheads, dchan, small):
        ref[...] = jnp.zeros_like(ref)
    for copy in loads[:3]:
        copy.wait()
    for chunk in range(chunks):
        for s in range(seqs):
            gate_chunk(cw, chunk, s, proj, scales, chan_par, gg, mixed, gated, dchan)

    loads[3].wait()

    def branch_tile(start, size):
        branch[:, :, pl.ds(start, size)] = (
            dot(gated[...].reshape(slots, cw), rows_v[:, :, pl.ds(start, size)].reshape(cw, size))
            .astype(BF16)
            .reshape(nc, seqs * length, size)
        )

    column_tiles(D, branch_tile)
    met()
    out_line.begin()

    gated_t[...] = gated[...].reshape(slots, cw).T

    def gout_part(i, _):
        cot_part(i).wait()
        size = min(quarter, 256)
        for j in range(quarter // size):
            cots = cot_v[lax.rem(i, 2), :, :, j * size : (j + 1) * size].reshape(slots, size)
            at = pl.ds(pl.multiple_of(i * quarter + j * size, LANES), size)
            gout[:, :, :, at] = (
                dot(gated_t[...], cots).reshape(gout.shape[:3] + (size,)).astype(BF16)
            )
        pl.when(i + 2 < D // quarter)(lambda: cot_part(i + 2).start())
        return 0

    lax.fori_loop(0, D // quarter, gout_part, 0)
    gout_square.begin()
    out_line.merge()
    out_line.step(0)
    loads[4].wait()

    def in_tile(parts, base, shift):
        def body(start, size):
            grads = proj[:, :, :, pl.ds(base + start, size)].reshape(slots, size)
            parts[:, :, :, pl.ds(shift + start, size)] = (
                dot(normed_t[...], grads).reshape(parts.shape[:3] + (size,)).astype(BF16)
            )

        return body

    column_tiles(cw, in_tile(gate_parts, 0, 0))
    gate_square.begin()
    for copy in loads[5:]:
        copy.wait()
    for f in range(min(2, nf)):
        start_weights(f)

    def finish_gate():
        for h in range(2):
            gate_square.final(h)
            gate_deal.start(h)

    later = [
        [lambda: out_line.step(1), gout_square.step],
        [lambda: out_line.step(2), gate_square.step],
        [lambda i=i: out_line.step(i) for i in range(3, nz - 1)] + [finish_gate],
    ]
    if nz < 4:
        later[0] = [lambda i=i: out_line.step(i) for i in range(1, nz - 1)] + [gout_square.step]
        later[1] = [gate_square.step]
    for i in range(chunks):
        for s in range(seqs):
            backward_chunk(
                cw, chunks - 1 - i, s, lengths, proj, pick, conv_par, heads_par, chan_par, gg, mixed,
                states, dconv, dheads, dchan, window, ahead, state_grad,
            )
        if i < chunks - 1 and later:
            for act in later.pop(0):
                act()
    for acts in later:
        for act in acts:
            act()

    column_tiles(cw, in_tile(x_parts, cw, 0))
    column_tiles(ends, in_tile(x_parts, 2 * cw, cw), ends)
    x_square.begin()
    out_line.final(total)

    def put_out(i, _):
        at = pl.ds(pl.multiple_of(i * 16, 16), 16)
        out[at] = (total[at] + hidden[at].astype(F32)).astype(BF16)
        return 0

    lax.fori_loop(0, hidden.shape[0] // 16, put_out, 0)
    out_line.end()
    neighbours = [
        ({"ctx": me_c + 1 - 2 * lax.rem(me_c, 2)}, None),
        ({"ctx": me_c + 2}, me_c + 2 < nc),
        ({"ctx": me_c - 2}, me_c - 2 >= 0),
    ]
    freed = signal_all(line_free, neighbours)

    depth = main_v.shape[2]

    def normed_tile(f, _):
        for copy in weights_part(f):
            copy.wait()
        for j in range(max(1, depth // 256)):
            size = min(depth, 256)
            here = pl.ds(j * size, size)
            sums = dot(proj[:, :, :, : 2 * cw].reshape(slots, 2 * cw), main_v[lax.rem(f, 2), :, here])
            sums = sums + dot(proj[:, :, :, 2 * cw :].reshape(slots, ends), tail_v[lax.rem(f, 2), :, here])
            at = pl.ds(pl.multiple_of(f * depth + j * size, LANES), size)
            branch[:, :, at] = sums.astype(BF16).reshape(nc, seqs * length, size)
        pl.when(f + 2 < nf)(lambda: start_weights(f + 2))
        return 0

    lax.fori_loop(0, nf, normed_tile, 0)
    freed()
    dn_line.begin()

    dskip = dot_exact(jnp.broadcast_to(dchan[0:1, :], (8, cw)), head_sum_matrix(cw))[0:1, :]
    row = 0
    for k in range(CONV_K + 1):
        for j in range(cc // LANES):
            small[row : row + 1, :] = dconv[k : k + 1, j * LANES : (j + 1) * LANES]
            row += 1
    for j in range(cw // LANES):
        small[row : row + 1, :] = dchan[1:2, j * LANES : (j + 1) * LANES]
        row += 1
    small[row : row + 1, :] = dheads[0:1, :]
    small[row + 1 : row + 2, :] = dheads[1:2, :]
    small[row + 2 : row + 3, :] = dskip
    smalls[0].begin()
    dn_line.merge()
    for i in range(nz - 1):
        dn_line.step(i)
        if i == 0:
            smalls[0].wait()
            small_sum[...] = smalls[0].total()
            smalls[1].begin()
            for h in range(2):
                gout_square.final(h)
            if span > 1:
                route = push(gout_sum, gout_mine, route_sems.at[0], route_sems.at[1], target)
                stay = lambda: pltpu.make_async_copy(gout_sum, gout_mine, here.at[2])
                pl.when(away)(route.start)
                pl.when(jnp.logical_not(away))(lambda: stay().start())
        if i == 1:
            x_square.step()
    if nz < 3:
        x_square.step()

    dn_line.final(total)
    dnorm = jnp.zeros((1, D), F32)

    def norm_back(i, dnorm):
        at = pl.ds(pl.multiple_of(i * 16, 16), 16)
        src = hidden[at].astype(F32)
        dn = total[at]
        scale = lax.rsqrt(jnp.mean(src * src, axis=1, keepdims=True) + EPS)
        h = dn * gain[...]
        pull = jnp.mean(h * src, axis=1, keepdims=True) * scale * scale
        d_hidden[at] = scale * (h - src * pull) + cot[at].astype(F32)
        return dnorm + jnp.sum(dn * src * scale, axis=0, keepdims=True)

    dnorm = lax.fori_loop(0, hidden.shape[0] // 16, norm_back, dnorm)
    for j in range(D // LANES):
        gains[j : j + 1, :] = dnorm[:, j * LANES : (j + 1) * LANES]
    gain_sums[0].begin()
    for h in range(2):
        x_square.final(h)
        x_deal.start(h)
    gain_sums[0].wait()
    gains_sum[...] = gain_sums[0].total()
    gain_sums[1].begin()

    def ordered(pieces, base):
        for c in range(nc):
            for i in range(span):
                to = base + i * apart + c * wide
                grad_in[:, to : to + wide] = pieces[c, :, i * wide : (i + 1) * wide].astype(F32)

    gate_deal.wait()
    ordered(gate_pieces, 0)
    if span > 1:

        @pl.when(away)
        def _():
            route.wait_recv()
            route.wait_send()

        @pl.when(jnp.logical_not(away))
        def _():
            stay().wait()

        grad_out[...] = gout_mine[...].reshape(grad_out.shape).astype(F32)
    else:
        grad_out[...] = gout_sum[...].astype(F32).reshape(grad_out.shape)
    smalls[1].wait()
    groups = cc // LANES
    for k in range(CONV_K + 1):
        to_ref, to_row = (dconv_w, k) if k < CONV_K else (dconv_b, 0)
        for c in range(nc):
            for j in range(cw // LANES):
                i, inside = j * LANES // wide, j * LANES % wide
                to = i * apart + c * wide + inside
                to_ref[to_row : to_row + 1, to : to + LANES] = small_all[
                    c, k * groups + j : k * groups + j + 1, :
                ]
        for j in range(cw // LANES, groups):
            shared = small_all[0, k * groups + j : k * groups + j + 1, :]
            for c in range(1, nc):
                shared = shared + small_all[c, k * groups + j : k * groups + j + 1, :]
            to = DI + j * LANES - cw
            to_ref[to_row : to_row + 1, to : to + LANES] = shared
    first = (CONV_K + 1) * groups
    by_head = jnp.zeros((8, HEADS), F32)
    for c in range(nc):
        for j in range(cw // LANES):
            i, inside = j * LANES // wide, j * LANES % wide
            to = i * apart + c * wide + inside
            dgain[:, to : to + LANES] = small_all[c, first + j : first + j + 1, :]
        rows = small_all[c, first + cw // LANES : first + cw // LANES + 8, :]
        by_head = by_head + lax.dot_general(
            rows, head_pick(cw, span, c), (((1,), (1,)), ((), ())), precision=EXACT,
            preferred_element_type=F32,
        )
    dheads_out[...] = by_head
    gain_sums[1].wait()
    summed = gain_sums[1].total()
    for j in range(D // LANES):
        dnorm_gain[:, j * LANES : (j + 1) * LANES] = summed[j : j + 1, :]
    dn_line.end()
    gout_square.end()
    gate_square.end()
    x_square.end()
    x_deal.wait()
    ordered(x_pieces, DI)
    shared = x_pieces[0, :, cw:].astype(F32)
    for c in range(1, nc):
        shared = shared + x_pieces[c, :, cw:].astype(F32)
    grad_in[:, 2 * DI :] = shared


def call_back(nc, nf, cw, span, lengths, hidden, cot, gain, *front):
    bigs, params = front[:9], front[9:]
    proj, mixed = bigs[5], bigs[7]
    _, seqs, length, cols = proj.shape
    nz, mine = nc // 2, seqs * length
    slots, q = nc * mine, mixed.shape[2]
    cc, ends, rows = cw + 2 * N_STATE, cols - 2 * cw, D // (nc * nf)
    vmem = pl.BlockSpec(memory_space=pltpu.VMEM)
    anywhere = pl.BlockSpec(memory_space=pl.ANY)
    dma = pltpu.SemaphoreType.DMA
    landing = SquareReduce.landing
    gout = (2, cw // nf // 2, D)
    gate, x = (nc, rows, cw), (nc, rows, cw + ends)
    count = (CONV_K + 1) * (cc // LANES) + cw // LANES + 3
    small = (-(-(count + 5) // 8) * 8, LANES)
    gains = (D // LANES, LANES)
    places = max(nf, 6)
    return pl.pallas_call(
        functools.partial(back_kernel, nc, nf, cw, span),
        in_specs=[pl.BlockSpec(memory_space=pltpu.SMEM)] + [vmem] * 8 + [anywhere] * 9,
        out_specs=[vmem] * 9,
        out_shape=[
            jax.ShapeDtypeStruct((mine, D), BF16),
            jax.ShapeDtypeStruct((mine, D), F32),
            jax.ShapeDtypeStruct((rows, 2 * DI + ends), F32),
            jax.ShapeDtypeStruct((cw // nf, D), F32),
            jax.ShapeDtypeStruct((CONV_K, CH), F32),
            jax.ShapeDtypeStruct((1, CH), F32),
            jax.ShapeDtypeStruct((1, DI), F32),
            jax.ShapeDtypeStruct((8, HEADS), F32),
            jax.ShapeDtypeStruct((1, D), F32),
        ],
        scratch_shapes=[
            pltpu.VMEM(bigs[0].shape, BF16),
            pltpu.VMEM((2, nc, mine, 256), BF16),
            pltpu.VMEM((2,) + bigs[2].shape[1:], BF16),
            pltpu.VMEM((2,) + bigs[3].shape[1:], BF16),
        ]
        + [pltpu.VMEM(a.shape, a.dtype) for a in bigs[4:]]
        + [
            pltpu.VMEM((nc, seqs, length, cw), BF16),
            pltpu.VMEM((cw, slots), BF16),
            pltpu.VMEM((nc, mine, D), BF16),
            pltpu.VMEM((nf,) + gout, BF16),
            pltpu.VMEM((nc, nf, rows, cw), BF16),
            pltpu.VMEM((nc, nf, rows, cw + ends), BF16),
            pltpu.VMEM((nz, mine, D), BF16),
            pltpu.VMEM((nz + 1, mine, D), BF16),
            pltpu.VMEM((mine, D), F32),
            pltpu.VMEM(landing(nf, gout), BF16),
            pltpu.VMEM(gout, BF16),
            pltpu.VMEM(landing(nf, gate), BF16),
            pltpu.VMEM(gate, BF16),
            pltpu.VMEM(landing(nf, x), BF16),
            pltpu.VMEM(x, BF16),
            pltpu.VMEM(gate, BF16),
            pltpu.VMEM(x, BF16),
            pltpu.VMEM(gout, BF16),
            pltpu.VMEM((seqs, q + 8, cc), F32),
            pltpu.VMEM((seqs, q + 8, cc), F32),
            pltpu.VMEM((seqs, N_STATE, cw), F32),
            pltpu.VMEM((8, cc), F32),
            pltpu.VMEM((8, LANES), F32),
            pltpu.VMEM((8, cw), F32),
            pltpu.VMEM(small, F32),
            pltpu.VMEM((nf,) + small, F32),
            pltpu.VMEM(small, F32),
            pltpu.VMEM((nc,) + small, F32),
            pltpu.VMEM(gains, F32),
            pltpu.VMEM((nf,) + gains, F32),
            pltpu.VMEM(gains, F32),
            pltpu.VMEM((nc,) + gains, F32),
            dma((6,)),
            dma((2,)),
            dma((2, 2)),
            dma((2, 2, nz)),
            dma((2, 2, 2, nz)),
            dma((3, 2, places)),
            dma((2, 2, nc)),
            dma((4, 2, max(nc, nf))),
            dma((2,)),
            dma((3,)),
            pltpu.SemaphoreType.REGULAR,
        ],
        compiler_params=pltpu.CompilerParams(
            collective_id=1, has_side_effects=True, vmem_limit_bytes=VMEM_LIMIT
        ),
        name="back",
    )(lengths, hidden, cot, gain, *params, *bigs)


def local(
    hidden,
    cotangent,
    lengths,
    norm_gain,
    input_weight,
    conv_w,
    conv_b,
    dt_bias,
    a_log,
    d_skip,
    gate_gain,
    output_weight,
):
    nc, nf = lax.axis_size("ctx"), lax.axis_size("fsdp")
    mb_count, seq_rows, length = hidden.shape[0], hidden.shape[1], hidden.shape[2]
    seqs = mb_count * seq_rows
    mine = seqs * length
    cw = DI // nc

    span = nf if (DI // nf // nc) % LANES == 0 else 1
    own = hidden.reshape(mine, D)
    cot = cotangent.reshape(mine, D)
    heads_in = jnp.pad(jnp.stack([dt_bias, a_log, d_skip]), ((0, 5), (0, 0)))
    seq_lengths = lengths.reshape(seqs)
    front = call_front(
        nc, nf, cw, span, seq_lengths, own, cot, input_weight.T, output_weight,
        norm_gain[None], conv_w, conv_b[None], heads_in, gate_gain[None],
    )
    out, d_hidden, grad_in, grad_out, dconv_w, dconv_b, dgain, dheads, dnorm_gain = call_back(
        nc, nf, cw, span, seq_lengths, own, cot, norm_gain[None], *front
    )
    shape = hidden.shape
    return (
        out.reshape(shape),
        d_hidden.reshape(shape),
        dnorm_gain[0],
        grad_in,
        dconv_w,
        dconv_b[0],
        dheads[0],
        dheads[1],
        dheads[2],
        dgain[0],
        grad_out,
    )


def solution(mesh):
    tokens, rows, every = P(None, "fsdp", "ctx", None), P("fsdp", None), P()
    spread = P(("ctx", "fsdp"), None)
    in_specs = (
        tokens, tokens, P(None, "fsdp"), every, rows, every, every, every, every, every, every, rows,
    )
    out_specs = (
        tokens, tokens, every, spread, every, every, every, every, every, every, spread,
    )
    return jax.shard_map(local, mesh=mesh, in_specs=in_specs, out_specs=out_specs, check_vma=False)
```

```python
import functools

import jax
import jax.numpy as jnp
from jax import lax
from jax.experimental import pallas as pl
from jax.experimental.pallas import tpu as pltpu
from jax.sharding import PartitionSpec as P

D = 2048
HEADS = 64
HEAD_DIM = 64
N_STATE = 128
CONV_K = 4
DI = 4096
CH = DI + 2 * N_STATE
LANES = 128
EPS = 1e-05
F32 = jnp.float32
BF16 = jnp.bfloat16
EXACT = lax.Precision.HIGHEST
VMEM_LIMIT = 63 * 1024 * 1024


def dot(a, b, ca=1, cb=0):
    return lax.dot_general(
        a.astype(BF16), b.astype(BF16), (((ca,), (cb,)), ((), ())), preferred_element_type=F32
    )


def dot_exact(a, b):
    return lax.dot_general(
        a, b, (((1,), (0,)), ((), ())), precision=EXACT, preferred_element_type=F32
    )


def to_lanes(per_head, width):
    q = per_head.shape[0]
    low = lax.broadcasted_iota(jnp.int32, (q, LANES), 1) < HEAD_DIM
    pairs = []
    for j in range(width // LANES):
        first = jnp.broadcast_to(per_head[:, 2 * j : 2 * j + 1], (q, LANES))
        second = jnp.broadcast_to(per_head[:, 2 * j + 1 : 2 * j + 2], (q, LANES))
        pairs.append(jnp.where(low, first, second))
    return jnp.concatenate(pairs, axis=1)


def head_sum_matrix(width):
    channel = lax.broadcasted_iota(jnp.int32, (width, LANES), 0) // HEAD_DIM
    return (channel == lax.broadcasted_iota(jnp.int32, (width, LANES), 1)).astype(F32)


def split_heads(pair):
    low = lax.broadcasted_iota(jnp.int32, pair.shape, 1) < HEAD_DIM
    zero = jnp.zeros_like(pair)
    return jnp.concatenate([jnp.where(low, pair, zero), jnp.where(low, zero, pair)], axis=0)


def triangle(q, lower):
    rows = lax.broadcasted_iota(jnp.int32, (q, q), 0)
    cols = lax.broadcasted_iota(jnp.int32, (q, q), 1)
    return (rows >= cols) if lower else (rows <= cols)


def softplus(z):
    return jnp.maximum(z, 0.0) + jnp.log(1.0 + jnp.exp(-jnp.abs(z)))


def live_column(lengths_ref, s, chunk, q):
    slots = chunk * q + lax.broadcasted_iota(jnp.int32, (q, LANES), 0)
    return (slots < lengths_ref[s]).astype(F32)


def decays(dt_raw, bias, rate, live):
    q = dt_raw.shape[0]
    z = dt_raw + bias
    step = softplus(z) * live
    cum = dot_exact(triangle(q, True).astype(F32), step * rate)
    return z, step, cum


def head_pick(cw, span, me_c):
    mine, apart, each = cw // HEAD_DIM, HEADS // span, cw // HEAD_DIM // span
    lane = lax.broadcasted_iota(jnp.int32, (HEADS, LANES), 1)
    head = (lane // each) * apart + me_c * each + lax.rem(lane, each)
    row = lax.broadcasted_iota(jnp.int32, (HEADS, LANES), 0)
    return jnp.logical_and(row == head, lane < mine).astype(F32)


def forward_chunk(cw, chunk, s, lengths, proj, pick, conv_w, heads_par, chan_par, mixed_out, state_out, window, state):
    per = 2 if proj.shape[0] % 2 == 0 else 1
    length = proj.shape[2]
    q = per * length
    cc = cw + 2 * N_STATE
    causal = triangle(q, True)
    at = pl.ds(chunk * per, per)
    rows = proj[at, s].reshape(q, proj.shape[3])
    window[s, 8 : 8 + q, :] = rows[:, cw : cw + cc].astype(F32)
    pre = conv_w[CONV_K : CONV_K + 1, :] + conv_w[0:1, :] * window[s, 5 : 5 + q, :]
    for k in range(1, CONV_K):
        pre = pre + conv_w[k : k + 1, :] * window[s, 5 + k : 5 + k + q, :]
    window[s, 0:8, :] = window[s, q : q + 8, :]
    act = pre * jax.nn.sigmoid(pre)
    x = act[:, :cw]
    b = act[:, cw : cw + N_STATE]
    c = act[:, cw + N_STATE :]
    live = live_column(lengths, s, chunk, q)
    _, step, cum = decays(
        dot(rows[:, cw + cc :], pick[...]), heads_par[0:1, :], heads_par[1:2, :], live
    )
    cum_t = cum.T
    last = cum[q - 1 : q, :]
    u = x * to_lanes(step, cw)
    gram = dot(c, b, 1, 1)
    within = []
    for j in range(cw // LANES):
        kernels = []
        for h in (2 * j, 2 * j + 1):
            spread = jnp.where(causal, cum[:, h : h + 1] - cum_t[h : h + 1, :], -1e30)
            kernels.append((gram * jnp.exp(spread)).astype(BF16))
        both = jnp.concatenate(kernels, axis=1)
        within.append(dot(both, split_heads(u[:, j * LANES : (j + 1) * LANES])))
    before = state[s]
    state_out[chunk, s] = before.astype(BF16)
    mixed_out[chunk, s] = (
        jnp.concatenate(within, axis=1)
        + dot(c, before) * to_lanes(jnp.exp(cum), cw)
        + chan_par[0:1, :] * x
    )
    left = to_lanes(jnp.exp(last - cum), cw)
    state[s] = before * to_lanes(jnp.exp(last), cw) + dot(b, left * u, 0, 0)


def slot_columns(scales, chunk, s, row, cw):
    q = scales.shape[3]
    column = jnp.broadcast_to(scales[chunk, s, row : row + 1, :], (LANES, q)).T
    return jnp.concatenate([column] * (cw // LANES), axis=1)


def gated_chunk(cw, chunk, s, proj, scales, chan_par, mixed, gated):
    per = proj.shape[0] // mixed.shape[0]
    length = proj.shape[2]
    q = per * length
    at = pl.ds(chunk * per, per)
    gate = proj[at, s, :, :cw].reshape(q, cw).astype(F32)
    g = mixed[chunk, s] * gate * jax.nn.sigmoid(gate)
    normal = g * slot_columns(scales, chunk, s, 0, cw) * chan_par[1:2, :]
    gated[at, s] = normal.astype(BF16).reshape(per, length, cw)


def gate_chunk(cw, chunk, s, proj, scales, chan_par, gg, mixed, dchan):
    per = proj.shape[0] // mixed.shape[0]
    length = proj.shape[2]
    q = per * length
    at = pl.ds(chunk * per, per)
    gate = proj[at, s, :, :cw].reshape(q, cw).astype(F32)
    scale, pull = (slot_columns(scales, chunk, s, i, cw) for i in range(2))
    grad = gg[at, s].reshape(q, cw)
    sig = jax.nn.sigmoid(gate)
    silu = gate * sig
    m = mixed[chunk, s]
    g = m * silu
    gain = chan_par[1:2, :]
    dchan[1:2, :] += jnp.sum(grad * g * scale, axis=0, keepdims=True)
    dg = scale * (grad * gain - g * pull)
    gg[at, s] = (dg * silu).reshape(per, length, cw)
    dgate = dg * m * (sig * (1.0 + gate * (1.0 - sig)))
    proj[at, s, :, :cw] = dgate.astype(BF16).reshape(per, length, cw)


def backward_chunk(
    cw, chunk, s, lengths, proj, pick, conv_w, heads_par, chan_par, gm_in, mixed_in, state_in,
    dconv, dheads, dchan, window, ahead, state_grad,
):
    per = proj.shape[0] // mixed_in.shape[0]
    length = proj.shape[2]
    q = per * length
    cc = cw + 2 * N_STATE
    causal = triangle(q, True)
    sums = head_sum_matrix(cw)
    at = pl.ds(chunk * per, per)
    rows = proj[at, s, :, cw:].reshape(q, proj.shape[3] - cw)
    conv_in = rows[:, :cc].astype(F32)
    mixed = mixed_in[chunk, s]
    gm = gm_in[at, s].reshape(q, cw)
    if chunk:
        tail = proj[chunk * per - 1, s, length - 16 :, cw : cw + cc].astype(F32)
        window[s, 0:8, :] = tail[8:16]
    else:
        window[s, 0:8, :] = jnp.zeros((8, cc), F32)
    window[s, 8 : 8 + q, :] = conv_in
    pre = conv_w[CONV_K : CONV_K + 1, :] + conv_w[0:1, :] * window[s, 5 : 5 + q, :]
    for k in range(1, CONV_K):
        pre = pre + conv_w[k : k + 1, :] * window[s, 5 + k : 5 + k + q, :]
    sig_pre = jax.nn.sigmoid(pre)
    act = pre * sig_pre
    x = act[:, :cw]
    b = act[:, cw : cw + N_STATE]
    c = act[:, cw + N_STATE :]
    live = live_column(lengths, s, chunk, q)
    z, step, cum = decays(dot(rows[:, cc:], pick[...]), heads_par[0:1, :], heads_par[1:2, :], live)
    cum_t = cum.T
    last = cum[q - 1 : q, :]
    step_l = to_lanes(step, cw)
    u = x * step_l
    gram = dot(c, b, 1, 1)
    dchan[0:1, :] += jnp.sum(gm * x, axis=0, keepdims=True)
    du = []
    dgram = jnp.zeros((q, q), F32)
    for j in range(cw // LANES):
        lanes = slice(j * LANES, (j + 1) * LANES)
        dkernels = dot(gm[:, lanes], split_heads(u[:, lanes]), 1, 1)
        kernels = []
        for i in range(2):
            h = 2 * j + i
            spread = jnp.where(causal, cum[:, h : h + 1] - cum_t[h : h + 1, :], -1e30)
            decay = jnp.exp(spread)
            dgram = dgram + dkernels[:, i * q : (i + 1) * q] * decay
            kernels.append((gram * decay).astype(BF16))
        both = jnp.concatenate(kernels, axis=0)
        du.append(dot(both, split_heads(gm[:, lanes]), 0, 0))
    before = state_in[chunk, s].astype(F32)
    after_grad = state_grad[s]
    v = gm * to_lanes(jnp.exp(cum), cw)
    left = to_lanes(jnp.exp(last - cum), cw)
    du_state = left * dot(b, after_grad)
    du = jnp.concatenate(du, axis=1) + du_state
    dc = dot(dgram, b) + dot(v, before, 1, 1)
    db = dot(dgram, c, 0, 0) + dot(left * u, after_grad, 1, 1)
    end = to_lanes(jnp.exp(last), cw)
    extra = jnp.sum(u * du_state, axis=0, keepdims=True) + end * jnp.sum(
        after_grad * before, axis=0, keepdims=True
    )
    state_grad[s] = end * after_grad + dot(c, v, 0, 0)
    last_row = (lax.broadcasted_iota(jnp.int32, (q, LANES), 0) == q - 1).astype(F32)
    dcum = dot_exact(gm * (mixed - chan_par[0:1, :] * x) - u * du, sums) + last_row * dot_exact(
        jnp.broadcast_to(extra, (8, cw)), sums
    )[0:1, :]
    dlog = dot_exact(triangle(q, False).astype(F32), dcum)
    rate = heads_par[1:2, :]
    dstep = dot_exact(x * du, sums) + dlog * rate
    dheads[1:2, :] += jnp.sum(dlog * step * rate, axis=0, keepdims=True)
    dz = dstep * live * jax.nn.sigmoid(z)
    dheads[0:1, :] += jnp.sum(dz, axis=0, keepdims=True)
    dx = step_l * du + chan_par[0:1, :] * gm
    dpre = jnp.concatenate([dx, db, dc], axis=1) * (sig_pre * (1.0 + pre * (1.0 - sig_pre)))
    ahead[s, 0:q, :] = dpre
    dconv_in = jnp.zeros((q, cc), F32)
    for k in range(CONV_K):
        first = CONV_K - 1 - k
        moved = ahead[s, first : first + q, :]
        dconv_in = dconv_in + conv_w[k : k + 1, :] * moved
        dconv[k : k + 1, :] += jnp.sum(conv_in * moved, axis=0, keepdims=True)
    dconv[CONV_K : CONV_K + 1, :] += jnp.sum(dpre, axis=0, keepdims=True)
    ahead[s, q : q + 8, :] = ahead[s, 0:8, :]
    proj[at, s, :, cw : cw + cc] = dconv_in.astype(BF16).reshape(per, length, cc)
    dz = dot(dz, pick[...], 1, 1).astype(BF16)
    proj[at, s, :, cw + cc :] = dz.reshape(per, length, HEADS)


def column_tiles(n, body, size=256):
    if n <= size:
        body(0, n)
        return

    def one(j, _):
        body(pl.multiple_of(j * size, size), size)
        return 0

    lax.fori_loop(0, n // size, one, 0)


MESH = pl.DeviceIdType.MESH


class push:
    def __init__(self, src, dst, send_sem, recv_sem, device):
        self.args = (src, dst, send_sem, recv_sem, device, MESH)

    def start(self):
        pltpu.make_async_remote_copy(*self.args).start()

    def wait_send(self):
        pltpu.make_async_remote_copy(*self.args).wait_send()

    def wait_recv(self):
        pltpu.make_async_remote_copy(*self.args).wait_recv()

    def wait(self):
        self.wait_send()
        self.wait_recv()


def greet(devices_and_tests):
    return signal_all(pltpu.get_barrier_semaphore(), devices_and_tests)


def signal_all(barrier, devices_and_tests):
    count = 0
    for device, there in devices_and_tests:
        if there is None:
            pl.semaphore_signal(barrier, inc=1, device_id=device, device_id_type=MESH)
            count = count + 1
        else:
            @pl.when(there)
            def _():
                pl.semaphore_signal(barrier, inc=1, device_id=device, device_id_type=MESH)

            count = count + there.astype(jnp.int32)
    return lambda: pl.semaphore_wait(barrier, count)


def line_of(nc):
    me = lax.axis_index("ctx")
    return nc // 2, me // 2, lax.rem(me, 2)


def square_partners():
    me = lax.axis_index("fsdp")
    high, low = me // 2, lax.rem(me, 2)
    return me, high * 2 + (1 - low), (1 - high) * 2 + low


class LineGather:
    def __init__(self, nc, every, sems):
        self.nz, self.z, self.k = line_of(nc)
        self.every = every
        self.up, self.down, self.side, self.got, self.got_side = sems

    def slot(self, place):
        return self.every.at[2 * place + self.k]

    def copies(self, d, below):
        z, k = self.z, self.k
        origin = z - d if below else z + d
        to = z + 1 if below else z - 1
        on = push(
            self.slot(origin), self.slot(origin), (self.up if below else self.down).at[d],
            self.got.at[origin], {"ctx": 2 * to + k},
        )
        side = push(
            self.slot(origin), self.slot(origin), self.side.at[origin], self.got_side.at[origin],
            {"ctx": 2 * z + 1 - k},
        )
        there = origin >= 0 if below else origin <= self.nz - 1
        further = to <= self.nz - 1 if below else to >= 0
        return on, side, there, further

    def begin(self):
        for below in (True, False):
            on, side, _, further = self.copies(0, below)
            pl.when(further)(on.start)
        side.start()

    def step(self, d):
        for below in (True, False):
            on, side, there, further = self.copies(d, below)

            @pl.when(there)
            def _():
                on.wait_recv()
                pl.when(further)(on.start)
                side.start()

    def sides(self, least, most):
        for place in range(self.nz):
            arrived = self.every.at[2 * place + 1 - self.k]
            apart = jnp.abs(place - self.z)
            pl.when(jnp.logical_and(apart >= least, apart <= most))(
                push(
                    arrived, arrived, self.side.at[place], self.got_side.at[place],
                    {"ctx": 2 * self.z + 1 - self.k},
                ).wait_recv
            )

    def end(self):
        for place in range(self.nz):
            arrived = self.every.at[2 * place + 1 - self.k]
            push(
                arrived, arrived, self.side.at[place], self.got_side.at[place],
                {"ctx": 2 * self.z + 1 - self.k},
            ).wait_send()
        for d in range(self.nz - 1):
            for below in (True, False):
                on, _, there, further = self.copies(d, below)
                pl.when(jnp.logical_and(there, further))(on.wait_send)


class SquareGather:
    def __init__(self, nf, every, sems):
        self.nf, self.every = nf, every
        self.send, self.got = sems
        self.half = every.shape[1] // 2

    def peers(self):
        me = lax.axis_index("fsdp")
        if self.nf == 4:
            _, fx, fy = square_partners()
            return [(fx, fx), (fy, fy)]
        return [
            (lax.rem(me + j, self.nf), lax.rem(me + self.nf - j, self.nf))
            for j in range(1, self.nf)
        ]

    def first(self):
        me = lax.axis_index("fsdp")
        for j, (to, frm) in enumerate(self.peers()):
            args = (self.send.at[j], self.got.at[j], {"fsdp": to})
            mine, theirs = self.every.at[me], self.every.at[frm]
            yield push(mine, mine, *args), push(theirs, theirs, *args)

    def second(self):
        me, fx, fy = square_partners()
        pairs = []
        for j, (via, to) in enumerate(((fx, fy), (fy, fx))):
            rows = pl.ds(j * self.half, self.half)
            args = (self.send.at[2 + j], self.got.at[2 + j], {"fsdp": to})
            there, here = self.every.at[via, rows], self.every.at[3 - me, rows]
            pairs.append((push(there, there, *args), push(here, here, *args)))
        return pairs

    def begin(self):
        for out, _ in self.first():
            out.start()

    def step(self):
        for j, (_, arrived) in enumerate(self.first()):
            arrived.wait_recv()
            if self.nf == 4:
                self.second()[j][0].start()

    def far(self):
        if self.nf == 4:
            for _, arrived in self.second():
                arrived.wait_recv()

    def end(self):
        for out, _ in self.first():
            out.wait_send()
        if self.nf == 4:
            for out, _ in self.second():
                out.wait_send()


class ChipGather:
    def __init__(self, nf, every, sems):
        self.nf, self.every = nf, every
        me = lax.axis_index("ctx")
        self.core, self.other = lax.rem(me, 2), {"ctx": me + 1 - 2 * lax.rem(me, 2)}
        self.half = every.shape[1] // 2
        mine = every.at[:, pl.ds(pl.multiple_of(self.core * self.half, 16), self.half)]
        self.square = SquareGather(nf, mine, sems[:2])
        self.send, self.got = sems[2:]

    def side(self, f, core):
        part = self.every.at[f, pl.ds(pl.multiple_of(core * self.half, 16), self.half)]
        return push(part, part, self.send.at[f], self.got.at[f], self.other)

    def near(self):
        return [frm for _, frm in self.square.peers()]

    def begin(self):
        self.square.begin()

    def step(self):
        self.square.step()
        for f in self.near():
            self.side(f, self.core).start()

    def sides(self):
        for f in self.near():
            self.side(f, 1 - self.core).wait_recv()

    def far(self):
        self.square.far()
        if self.nf == 4:
            f = 3 - lax.axis_index("fsdp")
            self.side(f, self.core).start()
            self.side(f, 1 - self.core).wait_recv()

    def end(self):
        self.square.end()
        for f in self.near():
            self.side(f, self.core).wait_send()
        if self.nf == 4:
            self.side(3 - lax.axis_index("fsdp"), self.core).wait_send()


class SquareSpread:
    def __init__(self, nf, source, every, sems):
        self.nf, self.every = nf, every
        self.send, self.got = sems
        self.mine = lax.axis_index("fsdp") == source

    def copies(self):
        me = lax.axis_index("fsdp")
        return [
            push(
                self.every, self.every, self.send.at[j], self.got.at[0],
                {"fsdp": lax.rem(me + j, self.nf)},
            )
            for j in range(1, self.nf)
        ]

    def begin(self):
        for out in self.copies():
            pl.when(self.mine)(out.start)

    def step(self):
        pass

    def far(self):
        if self.nf > 1:
            pl.when(jnp.logical_not(self.mine))(self.copies()[0].wait_recv)

    def end(self):
        for out in self.copies():
            pl.when(self.mine)(out.wait_send)


class Exchange:
    def __init__(self, axis, n, own, every, sems):
        self.axis, self.n, self.own, self.every = axis, n, own, every
        self.send, self.got = sems

    def copies(self):
        me = lax.axis_index(self.axis)
        for j in range(1, self.n):
            to, frm = lax.rem(me + j, self.n), lax.rem(me + self.n - j, self.n)
            args = (self.send.at[j], self.got.at[j], {self.axis: to})
            yield push(self.own, self.every.at[me], *args), push(self.own, self.every.at[frm], *args)

    def begin(self):
        self.every[lax.axis_index(self.axis)] = self.own[...]
        for out, _ in self.copies():
            out.start()

    def wait(self):
        for out, arrived in self.copies():
            arrived.wait_recv()
            out.wait_send()

    def total(self):
        result = self.every[0]
        for i in range(1, self.n):
            result = result + self.every[i]
        return result


def front_kernel(
    nc, nf, cw, span, lengths, hidden, cot, in_w, out_w, norm_gain, conv_w, conv_b, heads_in, gate_gain,
    normed_out, cot_out, main_out, tail_out, gated_out, proj_out, gg_out, mixed_out, states_out, branch_out,
    scales, conv_par, heads_par, chan_par, pick,
    normed_t, cot_v, main_v, tail_v, gated_t, proj, gg, mixed, states, branch, rows_v, normed_v, acc, gated,
    window, state, stats, stats_held, more, more_held,
    line_sems, main_sems, tail_sems, rows_sems, stat_sems, load_sems, keep_sems,
):
    nz, z, k = line_of(nc)
    me_c, me_f = lax.axis_index("ctx"), lax.axis_index("fsdp")
    wide, apart = cw // span, DI // span
    depth = in_w.shape[1]
    seqs, length = proj.shape[1], proj.shape[2]
    per = 2 if nc % 2 == 0 else 1
    q, chunks = per * length, nc // per

    found = [({"ctx": lax.rem(me_c + j, nc)}, None) for j in range(1, nc)]
    found += [({"fsdp": lax.rem(me_f + j, nf)}, None) for j in range(1, nf)]
    met = greet(found)

    loads = []

    def load(src, dst):
        copy = pltpu.make_async_copy(src, dst, load_sems.at[len(loads)])
        copy.start()
        loads.append(copy)

    for part in range(2):
        for i in range(span):
            start = pl.multiple_of(part * DI + i * apart + wide * me_c, LANES)
            load(in_w.at[pl.ds(start, wide)], main_v.at[me_f, pl.ds(part * cw + i * wide, wide)])
    load(in_w.at[pl.ds(2 * DI, tail_v.shape[1])], tail_v.at[me_f])
    weight_loads = len(loads)
    load(cot, cot_v.at[me_c])
    if span > 1:
        load(out_w.at[pl.ds(pl.multiple_of(wide * me_c, 16), wide)], rows_v.at[me_f])
    else:
        lap = out_w.shape[0] // cw
        held = me_f == me_c // lap
        rows_load = pltpu.make_async_copy(
            out_w.at[pl.ds(pl.multiple_of(cw * lax.rem(me_c, lap), 16), cw)], rows_v.at[0],
            load_sems.at[len(loads)],
        )
        pl.when(held)(rows_load.start)

    def norm(i, _):
        at = pl.ds(pl.multiple_of(i * 16, 16), 16)
        src = hidden[at].astype(F32)
        mean = jnp.mean(src * src, axis=1, keepdims=True)
        normed_v[me_c, at] = (src * lax.rsqrt(mean + EPS) * norm_gain[...]).astype(BF16)
        return 0

    lax.fori_loop(0, hidden.shape[0] // 16, norm, 0)

    line = lambda i, every: LineGather(nc, every, [line_sems.at[i, j] for j in range(5)])
    normed_line, cot_line = line(0, normed_v), line(1, cot_v)
    main = SquareGather(nf, main_v, (main_sems.at[0], main_sems.at[1]))
    tails = ChipGather(nf, tail_v, [tail_sems.at[i] for i in range(4)])
    if span > 1:
        rows = SquareGather(nf, rows_v, (rows_sems.at[0], rows_sems.at[1]))
    else:
        rows = SquareSpread(nf, me_c // lap, rows_v.at[0], (rows_sems.at[0], rows_sems.at[1]))
    kept = []

    def keep(src, dst):
        copy = pltpu.make_async_copy(src, dst, keep_sems.at[len(kept)])
        copy.start()
        kept.append(copy)

    for copy in loads[:weight_loads]:
        copy.wait()
    met()
    main.begin()
    normed_line.begin()
    tails.begin()

    pick[...] = head_pick(cw, span, me_c)
    conv_par[...] = jnp.zeros_like(conv_par)
    chan_par[...] = jnp.zeros_like(chan_par)
    for i in range(span):
        here = pl.ds(i * wide, wide)
        there = pl.ds(pl.multiple_of(i * apart + wide * me_c, LANES), wide)
        conv_par[0:CONV_K, here] = conv_w[:, there]
        conv_par[CONV_K : CONV_K + 1, here] = conv_b[:, there]
        chan_par[1:2, here] = gate_gain[:, there]
    conv_par[0:CONV_K, cw:] = conv_w[:, DI:CH]
    conv_par[CONV_K : CONV_K + 1, cw:] = conv_b[:, DI:CH]
    picked = dot_exact(heads_in[...], pick[...])
    heads_par[0:1, :] = picked[0:1, :]
    heads_par[1:2, :] = -jnp.exp(picked[1:2, :])
    heads_par[2:8, :] = jnp.zeros((6, LANES), F32)
    chan_par[0:1, :] = to_lanes(picked[2:3, :], cw)
    window[...] = jnp.zeros_like(window)
    state[...] = jnp.zeros_like(state)

    for copy in loads[weight_loads:]:
        copy.wait()
    if span == 1:
        pl.when(held)(rows_load.wait)
    slots = nc * normed_v.shape[1]

    def project(depths, first, last):
        def part(weights, base):
            def body(start, size):
                sums = None
                for f in depths:
                    a = normed_v[:, :, pl.ds(pl.multiple_of(f * depth, LANES), depth)]
                    term = dot(a.reshape(slots, depth), weights[f, pl.ds(start, size)], 1, 1)
                    sums = term if sums is None else sums + term
                here = pl.ds(base + start, size)
                if not first:
                    sums = sums + acc[:, here]
                if last:
                    proj[:, :, :, here] = sums.astype(BF16).reshape(proj.shape[:3] + (size,))
                else:
                    acc[:, here] = sums

            return body

        column_tiles(2 * cw, part(main_v, 0))
        column_tiles(tail_v.shape[1], part(tail_v, 2 * cw), tail_v.shape[1])

    for d in range(1, min(nz, 3)):
        normed_line.step(d)
    cot_line.begin()
    main.step()
    tails.step()
    for d in range(3, nz):
        normed_line.step(d)
    normed_line.sides(0, nz)
    tails.sides()
    if nf == 4:
        _, fx, fy = square_partners()
        project([me_f, fx, fy], True, False)
    if nz > 1:
        cot_line.step(1)
    main.far()
    tails.far()
    rows.begin()
    if nf == 4:
        project([3 - me_f], False, True)
    else:
        for j in range(nf):
            project([lax.rem(me_f + j, nf)], j == 0, j == nf - 1)
    keep(main_v, main_out)
    keep(tail_v, tail_out)
    keep(proj, proj_out)

    def across(a):
        total = a[:, :LANES]
        for j in range(1, cw // LANES):
            total = total + a[:, j * LANES : (j + 1) * LANES]
        return jnp.sum(total.T, axis=0, keepdims=True)

    def before_norm(chunk, s):
        at = pl.ds(chunk * per, per)
        gate = proj[at, s, :, :cw].reshape(q, cw).astype(F32)
        return at, mixed[chunk, s] * gate * jax.nn.sigmoid(gate)

    for chunk in range(chunks):
        for s in range(seqs):
            forward_chunk(
                cw, chunk, s, lengths, proj, pick, conv_par, heads_par, chan_par, mixed, states,
                window, state,
            )
            _, g = before_norm(chunk, s)
            row = chunk * seqs + s
            stats[row : row + 1, :] = across(g * g)
        if chunk == chunks // 2 - 1:
            rows.step()
    squares = Exchange("ctx", nc, stats, stats_held, (stat_sems.at[0, 0], stat_sems.at[0, 1]))
    squares.begin()
    keep(mixed, mixed_out)
    keep(states, states_out)
    for d in range(2, nz - 1):
        cot_line.step(d)
    mine = normed_v.shape[1]

    def turn(c, _):
        normed_t[:, pl.ds(pl.multiple_of(c * mine, LANES), mine)] = normed_v[c].T
        return 0

    lax.fori_loop(0, nc, turn, 0)
    keep(normed_t, normed_out)
    squares.wait()
    totals = squares.total() * (1.0 / DI)
    for chunk in range(chunks):
        for s in range(seqs):
            row = chunk * seqs + s
            scales[chunk, s, 0:1, :] = lax.rsqrt(totals[row : row + 1, :] + EPS)
            gated_chunk(cw, chunk, s, proj, scales, chan_par, mixed, gated)
    rows.far()

    def branch_tile(start, size):
        part = dot(gated[...].reshape(slots, cw), rows_v[:, :, pl.ds(start, size)].reshape(cw, size))
        part = part.astype(BF16).reshape(nc, seqs, length, size)
        for s in range(seqs):
            branch[s, :, :, pl.ds(start, size)] = part[:, s]

    column_tiles(D, branch_tile)
    keep(branch, branch_out)
    gated_t[...] = gated[...].reshape(slots, cw).T
    keep(gated_t, gated_out)

    if nz > 2:
        cot_line.step(nz - 1)
    cot_line.sides(0, nz)
    keep(cot_v, cot_out)
    cots = cot_v[...].reshape(slots, D)
    weights = rows_v[...].reshape(cw, D)
    half = min(cw, 256)
    for i in range(cw // half):
        gg[:, :, :, i * half : (i + 1) * half] = dot(
            cots, weights[i * half : (i + 1) * half], 1, 1
        ).reshape(gg.shape[:3] + (half,))
    keep(gg, gg_out)
    for chunk in range(chunks):
        for s in range(seqs):
            at, g = before_norm(chunk, s)
            row = chunk * seqs + s
            more[row : row + 1, :] = across(gg[at, s].reshape(q, cw) * chan_par[1:2, :] * g)
    pulls = Exchange("ctx", nc, more, more_held, (stat_sems.at[1, 0], stat_sems.at[1, 1]))
    pulls.begin()
    pulls.wait()
    totals = pulls.total() * (1.0 / DI)
    for chunk in range(chunks):
        for s in range(seqs):
            row = chunk * seqs + s
            scale = scales[chunk, s, 0:1, :]
            scales[chunk, s, 1:2, :] = scale * scale * totals[row : row + 1, :]
            scales[chunk, s, 2:8, :] = jnp.zeros((6, q), F32)
    for part in (main, tails, rows, normed_line, cot_line):
        part.end()
    for copy in kept:
        copy.wait()


def call_front(nc, nf, cw, span, lengths, hidden, cot, in_w, out_w, norm_gain, conv_w, conv_b, heads_in, gate_gain):
    nz = nc // 2
    mine = hidden.shape[0]
    seqs = lengths.shape[0]
    length = mine // seqs
    per = 2 if nc % 2 == 0 else 1
    q, chunks, cc = per * length, nc // per, cw + 2 * N_STATE
    depth, wide, ends = in_w.shape[1], cw // span, in_w.shape[0] - 2 * DI
    cols = 2 * cw + ends
    vmem = pl.BlockSpec(memory_space=pltpu.VMEM)
    anywhere = pl.BlockSpec(memory_space=pl.ANY)
    dma = pltpu.SemaphoreType.DMA
    big = [
        ((D, nc * mine), BF16),
        ((nc, mine, D), BF16),
        ((nf, 2 * cw, depth), BF16),
        ((nf, ends, depth), BF16),
        ((cw, nc * mine), BF16),
        ((nc, seqs, length, cols), BF16),
        ((nc, seqs, length, cw), F32),
        ((chunks, seqs, q, cw), F32),
        ((chunks, seqs, N_STATE, cw), BF16),
        ((seqs, nc, length, D), BF16),
    ]
    small = [
        ((chunks, seqs, 8, q), F32),
        ((8, cc), F32),
        ((8, LANES), F32),
        ((8, cw), F32),
        ((HEADS, LANES), F32),
    ]
    held = big + [
        ((span, wide, D), BF16),
        ((nc, mine, D), BF16),
        ((nc * mine, cols), F32),
        ((nc, seqs, length, cw), BF16),
        ((seqs, q + 8, cc), F32),
        ((seqs, N_STATE, cw), F32),
    ]
    held += [((chunks * seqs, q), F32), ((nc, chunks * seqs, q), F32)] * 2
    places = max(nf, 4)
    return pl.pallas_call(
        functools.partial(front_kernel, nc, nf, cw, span),
        in_specs=[pl.BlockSpec(memory_space=pltpu.SMEM), vmem, vmem, anywhere, anywhere]
        + [vmem] * 5,
        out_specs=[anywhere] * len(big) + [vmem] * len(small),
        out_shape=[jax.ShapeDtypeStruct(*a) for a in big + small],
        scratch_shapes=[pltpu.VMEM(*a) for a in held]
        + [
            dma((2, 5, nz)),
            dma((2, places)),
            dma((4, places)),
            dma((2, places)),
            dma((2, 2, nc)),
            dma((2 * span + 3,)),
            dma((10,)),
        ],
        compiler_params=pltpu.CompilerParams(
            collective_id=0, has_side_effects=True, vmem_limit_bytes=VMEM_LIMIT
        ),
        name="front",
    )(lengths, hidden, cot, in_w, out_w, norm_gain, conv_w, conv_b, heads_in, gate_gain)


def add_rows(into, other, rows=16):
    def body(i, _):
        at = pl.ds(pl.multiple_of(i * rows, rows), rows)
        into[at] = (into[at].astype(F32) + other[at].astype(F32)).astype(into.dtype)
        return 0

    lax.fori_loop(0, into.shape[0] // rows, body, 0)


class LineReduce:
    def __init__(self, nc, parts, acc, landed, sems):
        self.nz, self.z, self.k = line_of(nc)
        self.parts, self.acc, self.landed = parts, acc, landed
        self.side, self.got_side, self.send, self.got = sems

    def to_side(self, place):
        other = {"ctx": 2 * self.z + 1 - self.k}
        return push(
            self.parts.at[2 * place + 1 - self.k], self.acc.at[place], self.side.at[place],
            self.got_side.at[place], other,
        )

    def begin(self):
        for place in range(self.nz):
            self.to_side(place).start()

    def merge(self):
        for place in range(self.nz):
            self.to_side(place).wait_recv()
            add_rows(self.acc.at[place], self.parts.at[2 * place + self.k])

    def along(self, place, up):
        way = 0 if up else 1
        slot = place if up else jnp.where(place == self.z - 1, self.nz, place)
        return push(
            self.acc.at[place], self.landed.at[slot], self.send.at[way, place],
            self.got.at[way, place], {"ctx": 2 * (self.z + (1 if up else -1)) + self.k},
        )

    def arrive(self, place, up, into, slot=None):
        self.along(place, up).wait_recv()
        add_rows(into, self.landed.at[place if slot is None else slot])

    def step(self, tick):
        z, nz = self.z, self.nz
        for place in range(nz):
            for up in (True, False):
                at = tick - (nz - 1 - place) if up else nz - 1 + place - tick
                if not (0 <= at < place if up else place < at <= nz - 1):
                    continue
                first, before = (0, place + 1) if up else (nz - 1, place - 1)

                @pl.when(z == at)
                def _():
                    if at != first:
                        self.arrive(place, up, self.acc.at[place])
                    elif 0 <= before <= nz - 1:
                        self.along(before, up).wait_send()
                    self.along(place, up).start()

    def final(self, total):
        z, nz = self.z, self.nz
        total[...] = self.acc[z].astype(F32)

        @pl.when(z > 0)
        def _():
            self.arrive(z, True, total)

        @pl.when(z < nz - 1)
        def _():
            self.arrive(z, False, total, nz)

    def end(self):
        for place in range(self.nz):
            self.to_side(place).wait_send()
        for place in range(self.nz):
            last = self.nz - 1
            self_up = jnp.logical_and(self.z < place, jnp.logical_or(self.z > 0, place == 1))
            self_down = jnp.logical_and(
                self.z > place, jnp.logical_or(self.z < last, place == last - 1)
            )
            pl.when(self_up)(self.along(place, True).wait_send)
            pl.when(self_down)(self.along(place, False).wait_send)


class SquareReduce:
    def __init__(self, nf, parts, landed, total, sems, inner=False, shift=0):
        self.nf, self.parts, self.landed, self.total = nf, parts, landed, total
        self.send, self.got = sems
        self.inner, self.shift = inner, shift
        self.half = total.shape[0] // 2

    def part(self, f, at):
        if self.inner:
            return self.parts.at[at, f]
        return self.parts.at[lax.rem(f + self.nf - self.shift, self.nf), at]

    @staticmethod
    def landing(nf, shape):
        blocks, rows, cols = shape
        return (6, blocks // 2, rows, cols) if nf == 4 else (nf, blocks, rows, cols)

    def copy(self, n, src, to):
        return push(src, self.landed.at[n], self.send.at[n], self.got.at[n], {"fsdp": to})

    def way(self, h):
        me, fx, fy = square_partners()
        first, second = (fx, fy) if h == 0 else (fy, fx)
        return me, first, second, pl.ds(h * self.half, self.half)

    def firsts(self, h):
        me, first, second, at = self.way(h)
        return (
            self.copy(3 * h, self.part(3 - me, at), first),
            self.copy(3 * h + 1, self.part(first, at), first),
        )

    def second_(self, h):
        _, _, second, _ = self.way(h)
        return self.copy(3 * h + 2, self.landed.at[3 * h], second)

    def others(self):
        me = lax.axis_index("fsdp")
        tos = [lax.rem(me + j, self.nf) for j in range(1, self.nf)]
        every = pl.ds(0, self.total.shape[0])
        return [self.copy(j + 1, self.part(to, every), to) for j, to in enumerate(tos)]

    def begin(self):
        if self.nf == 4:
            for i in range(2):
                for h in range(2):
                    self.firsts(h)[i].start()
        else:
            for out in self.others():
                out.start()

    def add(self, into, other):
        for b in range(into.shape[0]):
            add_rows(into.at[b], other.at[b], min(16, into.shape[1]))

    def step(self):
        if self.nf == 4:
            for h in range(2):
                _, _, second, at = self.way(h)
                self.firsts(h)[0].wait_recv()
                self.add(self.landed.at[3 * h], self.part(second, at))
                self.second_(h).start()

    def final(self, h):
        me = lax.axis_index("fsdp")
        at = pl.ds(h * self.half, self.half)
        if self.nf == 4:
            self.firsts(h)[1].wait_recv()
            into = self.total.at[at]
            into[...] = self.part(me, at)[...]
            self.add(into, self.landed.at[3 * h + 1])
            self.second_(h).wait_recv()
            self.add(into, self.landed.at[3 * h + 2])
        else:
            into = self.total.at[at]
            into[...] = self.part(me, at)[...]
            for j, out in enumerate(self.others()):
                if h == 0:
                    out.wait_recv()
                self.add(into, self.landed.at[j + 1, at])

    def end(self):
        if self.nf == 4:
            for h in range(2):
                for out in (*self.firsts(h), self.second_(h)):
                    out.wait_send()
        else:
            for out in self.others():
                out.wait_send()


class Deal:
    def __init__(self, nc, parts, pieces, sems, here):
        self.nc, self.parts, self.pieces = nc, parts, pieces
        self.send, self.got, self.here = sems[0], sems[1], here
        self.me = lax.axis_index("ctx")

    def to(self, c):
        return push(
            self.parts.at[c], self.pieces.at[self.me], self.send.at[c], self.got.at[self.me], {"ctx": c}
        )

    def stay(self):
        return pltpu.make_async_copy(self.parts.at[self.me], self.pieces.at[self.me], self.here)

    def start(self, h):
        half = self.nc // 2
        for j in range(half):
            c = h * half + lax.rem(self.me + j, half)
            pl.when(c != self.me)(self.to(c).start)

            @pl.when(c == self.me)
            def _():
                self.stay().start()

    def wait(self):
        self.stay().wait()
        for c in range(self.nc):

            @pl.when(c != self.me)
            def _():
                push(
                    self.parts.at[c], self.pieces.at[c], self.send.at[c], self.got.at[c], {"ctx": c}
                ).wait()


def back_kernel(
    nc, nf, cw, span, lengths, hidden, cot, gain, scales, conv_par, heads_par, chan_par, pick,
    normed_in, cot_in, main_in, tail_in, gated_in, proj_in, gg_in, mixed_in, states_in, branch_in,
    out, d_hidden, grad_in, grad_out, dconv_w, dconv_b, dgain, dheads_out, dnorm_gain,
    normed_t, cot_v, main_v, tail_v, gated_t, proj, gg, mixed, states,
    dnormed, gout, gate_parts, x_parts, acc, landed, total,
    gout_landed, gout_sum, gate_landed, gate_sum, x_landed, x_sum, gate_pieces, x_pieces, gout_mine,
    window, ahead, state_grad, dconv, dheads, dchan,
    small, small_held, small_sum, small_all, gains, gains_held, gains_sum, gains_all,
    load_sems, cot_sems, main_sems, line_sems, way_sems, square_sems, deal_sems, small_sems, route_sems,
    here, line_free, branch_sem,
):
    nz, _, _ = line_of(nc)
    me_c, me_f = lax.axis_index("ctx"), lax.axis_index("fsdp")
    wide, apart = cw // span, DI // span
    cc, ends = cw + 2 * N_STATE, tail_v.shape[1]
    seqs, length = proj.shape[1], proj.shape[2]
    chunks = mixed.shape[0]
    slots = nc * seqs * length

    found = [({"ctx": lax.rem(me_c + j, nc)}, None) for j in range(1, nc)]
    found += [({"fsdp": lax.rem(me_f + j, nf)}, None) for j in range(1, nf)]
    if span > 1:
        turn = lax.rem(me_c // 2, nf)
        lead, place = lax.rem(me_f + nf - turn, nf) * nc + me_c, me_c * nf + me_f
        target = {"ctx": lead // nf, "fsdp": lax.rem(lead, nf)}
        origin = lax.rem(place, nc)
        source = {"ctx": origin, "fsdp": lax.rem(place // nc + lax.rem(origin // 2, nf), nf)}
        away = lead != place
        found += [(target, away), (source, away)]
    met = greet(found)

    loads = []
    branch_load = pltpu.make_async_copy(branch_in, dnormed, branch_sem)
    branch_load.start()
    for i, (src, dst) in enumerate((
        (proj_in, proj), (mixed_in, mixed), (gg_in, gg), (gated_in, gated_t), (normed_in, normed_t),
        (states_in, states),
    )):
        copy = pltpu.make_async_copy(src, dst, load_sems.at[i])
        copy.start()
        loads.append(copy)

    quarter = cot_v.shape[3]

    def cot_part(i):
        return pltpu.make_async_copy(
            cot_in.at[:, :, pl.ds(pl.multiple_of(i * quarter, LANES), quarter)],
            cot_v.at[lax.rem(i, 2)], cot_sems.at[lax.rem(i, 2)],
        )

    def weights_part(f):
        slot = lax.rem(f, 2)
        return (
            pltpu.make_async_copy(main_in.at[f], main_v.at[slot], main_sems.at[0, slot]),
            pltpu.make_async_copy(tail_in.at[f], tail_v.at[slot], main_sems.at[1, slot]),
        )

    def start_weights(f):
        for copy in weights_part(f):
            copy.start()

    for i in range(2):
        cot_part(i).start()
    every_line = [
        LineReduce(
            nc, dnormed.at[i % seqs], acc.at[i % seqs], landed.at[i % seqs],
            (line_sems.at[i, 0], line_sems.at[i, 1], way_sems.at[i, 0], way_sems.at[i, 1]),
        )
        for i in range(2 * seqs)
    ]
    out_lines, lines = every_line[:seqs], every_line[seqs:]
    neighbours = [
        ({"ctx": me_c + 1 - 2 * lax.rem(me_c, 2)}, None),
        ({"ctx": me_c + 2}, me_c + 2 < nc),
        ({"ctx": me_c - 2}, me_c - 2 >= 0),
    ]

    def put_out(s):
        rows = pl.ds(s * length, length)
        out_lines[s].final(total.at[rows])
        out[rows] = (total[rows] + hidden[rows].astype(F32)).astype(BF16)
        out_lines[s].end()
        freed.append(signal_all(line_free.at[s], neighbours))

    freed = []
    square = lambda i, *refs, **how: SquareReduce(
        nf, *refs, (square_sems.at[i, 0], square_sems.at[i, 1]), **how
    )
    gout_square = square(0, gout, gout_landed, gout_sum, shift=turn if span > 1 else 0)
    gate_square = square(1, gate_parts, gate_landed, gate_sum, inner=True)
    x_square = square(2, x_parts, x_landed, x_sum, inner=True)
    gate_deal = Deal(nc, gate_sum, gate_pieces, (deal_sems.at[0, 0], deal_sems.at[0, 1]), here.at[0])
    x_deal = Deal(nc, x_sum, x_pieces, (deal_sems.at[1, 0], deal_sems.at[1, 1]), here.at[1])
    pair = lambda i: (small_sems.at[i, 0], small_sems.at[i, 1])
    smalls = (
        Exchange("fsdp", nf, small, small_held, pair(0)),
        Exchange("ctx", nc, small_sum, small_all, pair(1)),
    )
    gain_sums = (
        Exchange("fsdp", nf, gains, gains_held, pair(2)),
        Exchange("ctx", nc, gains_sum, gains_all, pair(3)),
    )

    for ref in (window, ahead, state_grad, dconv, dheads, dchan, small):
        ref[...] = jnp.zeros_like(ref)
    branch_load.wait()
    met()
    for line in out_lines:
        line.begin()
    for copy in loads[:3]:
        copy.wait()
    for chunk in range(chunks):
        for s in range(seqs):
            gate_chunk(cw, chunk, s, proj, scales, chan_par, gg, mixed, dchan)

    def out_acts(s):
        return [out_lines[s].merge] + [lambda i=i: out_lines[s].step(i) for i in range(nz - 1)]

    first, second = (out_acts(s) for s in (0, seqs - 1))
    first.pop(0)()
    first.pop(0)() if first else None

    loads[3].wait()

    def gout_part(i, _):
        cot_part(i).wait()
        size = min(quarter, 256)
        for j in range(quarter // size):
            cots = cot_v[lax.rem(i, 2), :, :, j * size : (j + 1) * size].reshape(slots, size)
            at = pl.ds(pl.multiple_of(i * quarter + j * size, LANES), size)
            gout[:, :, :, at] = (
                dot(gated_t[...], cots).reshape(gout.shape[:3] + (size,)).astype(BF16)
            )
        pl.when(i + 2 < D // quarter)(lambda: cot_part(i + 2).start())
        return 0

    lax.fori_loop(0, D // quarter, gout_part, 0)
    gout_square.begin()
    first.pop(0)() if first else None
    if seqs > 1:
        second.pop(0)()
        second.pop(0)() if second else None
    loads[4].wait()

    def in_tile(parts, base, shift):
        def body(start, size):
            grads = proj[:, :, :, pl.ds(base + start, size)].reshape(slots, size)
            parts[:, :, :, pl.ds(shift + start, size)] = (
                dot(normed_t[...], grads).reshape(parts.shape[:3] + (size,)).astype(BF16)
            )

        return body

    column_tiles(cw, in_tile(gate_parts, 0, 0))
    gate_square.begin()
    while first:
        first.pop(0)()
    for copy in loads[5:]:
        copy.wait()

    if span > 1:
        route = push(gout_sum, gout_mine, route_sems.at[0], route_sems.at[1], target)
        stay = lambda: pltpu.make_async_copy(gout_sum, gout_mine, here.at[2])

    def finish_gout():
        for h in range(2):
            gout_square.final(h)
        if span > 1:
            pl.when(away)(route.start)
            pl.when(jnp.logical_not(away))(lambda: stay().start())

    def finish_gate():
        for h in range(2):
            gate_square.final(h)
            gate_deal.start(h)

    depth = main_v.shape[2]
    narrow = min(depth, 256)

    def normed_part(s):
        def body(f, _):
            for copy in weights_part(f):
                copy.wait()
            for j in range(depth // narrow):
                here = pl.ds(j * narrow, narrow)
                grads = proj[:, s].reshape(nc * length, proj.shape[3])
                sums = dot(grads[:, : 2 * cw], main_v[lax.rem(f, 2), :, here])
                sums = sums + dot(grads[:, 2 * cw :], tail_v[lax.rem(f, 2), :, here])
                at = pl.ds(pl.multiple_of(f * depth + j * narrow, LANES), narrow)
                dnormed[s, :, :, at] = sums.astype(BF16).reshape(nc, length, narrow)
            pl.when(f + 2 < nf)(lambda: start_weights(f + 2))
            return 0

        lax.fori_loop(0, nf, body, 0)

    def line_acts(line):
        return [line.merge] + [lambda i=i: line.step(i) for i in range(nz - 1)]

    later = [lambda: put_out(0), gout_square.step, gate_square.step, finish_gout]
    if seqs > 1:
        later = second[:1] + later[:1] + second[1:] + later[1:2]
    for s in range(seqs):
        for f in range(min(2, nf)):
            start_weights(f)
        for i in range(chunks):
            backward_chunk(
                cw, chunks - 1 - i, s, lengths, proj, pick, conv_par, heads_par, chan_par, gg, mixed,
                states, dconv, dheads, dchan, window, ahead, state_grad,
            )
            if later:
                later.pop(0)()
        if s == seqs - 1:
            column_tiles(cw, in_tile(x_parts, cw, 0))
            column_tiles(ends, in_tile(x_parts, 2 * cw, cw), ends)
            x_square.begin()
        while later and not (s < len(freed)):
            later.pop(0)()
        normed_part(s)
        freed[s]()
        lines[s].begin()
        if s < seqs - 1:
            acts = line_acts(lines[s])
            later += acts[:2] + [
                lambda: (put_out(1), gate_square.step()), *acts[2:3], finish_gout, *acts[3:], finish_gate
            ]

    for act in later:
        act()

    dskip = dot_exact(jnp.broadcast_to(dchan[0:1, :], (8, cw)), head_sum_matrix(cw))[0:1, :]
    row = 0
    for k in range(CONV_K + 1):
        for j in range(cc // LANES):
            small[row : row + 1, :] = dconv[k : k + 1, j * LANES : (j + 1) * LANES]
            row += 1
    for j in range(cw // LANES):
        small[row : row + 1, :] = dchan[1:2, j * LANES : (j + 1) * LANES]
        row += 1
    small[row : row + 1, :] = dheads[0:1, :]
    small[row + 1 : row + 2, :] = dheads[1:2, :]
    small[row + 2 : row + 3, :] = dskip
    smalls[0].begin()
    acts = line_acts(lines[-1])
    acts.pop(0)()
    acts.pop(0)() if acts else None
    smalls[0].wait()
    small_sum[...] = smalls[0].total()
    smalls[1].begin()
    acts.pop(0)() if acts else None
    x_square.step()
    for act in acts:
        act()
    for s in range(seqs):
        lines[s].final(total.at[pl.ds(s * length, length)])
    dnorm = jnp.zeros((1, D), F32)

    def norm_back(i, dnorm):
        at = pl.ds(pl.multiple_of(i * 16, 16), 16)
        src = hidden[at].astype(F32)
        dn = total[at]
        scale = lax.rsqrt(jnp.mean(src * src, axis=1, keepdims=True) + EPS)
        h = dn * gain[...]
        pull = jnp.mean(h * src, axis=1, keepdims=True) * scale * scale
        d_hidden[at] = scale * (h - src * pull) + cot[at].astype(F32)
        return dnorm + jnp.sum(dn * src * scale, axis=0, keepdims=True)

    dnorm = lax.fori_loop(0, hidden.shape[0] // 16, norm_back, dnorm)
    for j in range(D // LANES):
        gains[j : j + 1, :] = dnorm[:, j * LANES : (j + 1) * LANES]
    gain_sums[0].begin()
    for h in range(2):
        x_square.final(h)
        x_deal.start(h)
    gain_sums[0].wait()
    gains_sum[...] = gain_sums[0].total()
    gain_sums[1].begin()

    def ordered(pieces, base):
        for c in range(nc):
            for i in range(span):
                to = base + i * apart + c * wide
                grad_in[:, to : to + wide] = pieces[c, :, i * wide : (i + 1) * wide].astype(F32)

    gate_deal.wait()
    ordered(gate_pieces, 0)
    if span > 1:

        @pl.when(away)
        def _():
            route.wait_recv()
            route.wait_send()

        @pl.when(jnp.logical_not(away))
        def _():
            stay().wait()

        grad_out[...] = gout_mine[...].reshape(grad_out.shape).astype(F32)
    else:
        grad_out[...] = gout_sum[...].astype(F32).reshape(grad_out.shape)
    smalls[1].wait()
    groups = cc // LANES
    for k in range(CONV_K + 1):
        to_ref, to_row = (dconv_w, k) if k < CONV_K else (dconv_b, 0)
        for c in range(nc):
            for j in range(cw // LANES):
                i, inside = j * LANES // wide, j * LANES % wide
                to = i * apart + c * wide + inside
                to_ref[to_row : to_row + 1, to : to + LANES] = small_all[
                    c, k * groups + j : k * groups + j + 1, :
                ]
        for j in range(cw // LANES, groups):
            shared = small_all[0, k * groups + j : k * groups + j + 1, :]
            for c in range(1, nc):
                shared = shared + small_all[c, k * groups + j : k * groups + j + 1, :]
            to = DI + j * LANES - cw
            to_ref[to_row : to_row + 1, to : to + LANES] = shared
    first = (CONV_K + 1) * groups
    by_head = jnp.zeros((8, HEADS), F32)
    for c in range(nc):
        for j in range(cw // LANES):
            i, inside = j * LANES // wide, j * LANES % wide
            to = i * apart + c * wide + inside
            dgain[:, to : to + LANES] = small_all[c, first + j : first + j + 1, :]
        rows = small_all[c, first + cw // LANES : first + cw // LANES + 8, :]
        by_head = by_head + lax.dot_general(
            rows, head_pick(cw, span, c), (((1,), (1,)), ((), ())), precision=EXACT,
            preferred_element_type=F32,
        )
    dheads_out[...] = by_head
    gain_sums[1].wait()
    summed = gain_sums[1].total()
    for j in range(D // LANES):
        dnorm_gain[:, j * LANES : (j + 1) * LANES] = summed[j : j + 1, :]
    for line in lines:
        line.end()
    gout_square.end()
    gate_square.end()
    x_square.end()
    x_deal.wait()
    ordered(x_pieces, DI)
    shared = x_pieces[0, :, cw:].astype(F32)
    for c in range(1, nc):
        shared = shared + x_pieces[c, :, cw:].astype(F32)
    grad_in[:, 2 * DI :] = shared


def call_back(nc, nf, cw, span, lengths, hidden, cot, gain, *front):
    bigs, params = front[:10], front[10:]
    proj, mixed = bigs[5], bigs[7]
    _, seqs, length, cols = proj.shape
    nz, mine = nc // 2, seqs * length
    slots, q = nc * mine, mixed.shape[2]
    cc, ends, rows = cw + 2 * N_STATE, cols - 2 * cw, D // (nc * nf)
    vmem = pl.BlockSpec(memory_space=pltpu.VMEM)
    anywhere = pl.BlockSpec(memory_space=pl.ANY)
    dma = pltpu.SemaphoreType.DMA
    landing = SquareReduce.landing
    gout = (2, cw // nf // 2, D)
    gate, x = (nc, rows, cw), (nc, rows, cw + ends)
    count = (CONV_K + 1) * (cc // LANES) + cw // LANES + 3
    small = (-(-(count + 5) // 8) * 8, LANES)
    gains = (D // LANES, LANES)
    places = max(nf, 6)
    return pl.pallas_call(
        functools.partial(back_kernel, nc, nf, cw, span),
        in_specs=[pl.BlockSpec(memory_space=pltpu.SMEM)] + [vmem] * 8 + [anywhere] * 10,
        out_specs=[vmem] * 9,
        out_shape=[
            jax.ShapeDtypeStruct((mine, D), BF16),
            jax.ShapeDtypeStruct((mine, D), F32),
            jax.ShapeDtypeStruct((rows, 2 * DI + ends), F32),
            jax.ShapeDtypeStruct((cw // nf, D), F32),
            jax.ShapeDtypeStruct((CONV_K, CH), F32),
            jax.ShapeDtypeStruct((1, CH), F32),
            jax.ShapeDtypeStruct((1, DI), F32),
            jax.ShapeDtypeStruct((8, HEADS), F32),
            jax.ShapeDtypeStruct((1, D), F32),
        ],
        scratch_shapes=[
            pltpu.VMEM(bigs[0].shape, BF16),
            pltpu.VMEM((2, nc, mine, 256), BF16),
            pltpu.VMEM((2,) + bigs[2].shape[1:], BF16),
            pltpu.VMEM((2,) + bigs[3].shape[1:], BF16),
        ]
        + [pltpu.VMEM(a.shape, a.dtype) for a in bigs[4:9]]
        + [
            pltpu.VMEM((seqs, nc, length, D), BF16),
            pltpu.VMEM((nf,) + gout, BF16),
            pltpu.VMEM((nc, nf, rows, cw), BF16),
            pltpu.VMEM((nc, nf, rows, cw + ends), BF16),
            pltpu.VMEM((seqs, nz, length, D), BF16),
            pltpu.VMEM((seqs, nz + 1, length, D), BF16),
            pltpu.VMEM((mine, D), F32),
            pltpu.VMEM(landing(nf, gout), BF16),
            pltpu.VMEM(gout, BF16),
            pltpu.VMEM(landing(nf, gate), BF16),
            pltpu.VMEM(gate, BF16),
            pltpu.VMEM(landing(nf, x), BF16),
            pltpu.VMEM(x, BF16),
            pltpu.VMEM(gate, BF16),
            pltpu.VMEM(x, BF16),
            pltpu.VMEM(gout, BF16),
            pltpu.VMEM((seqs, q + 8, cc), F32),
            pltpu.VMEM((seqs, q + 8, cc), F32),
            pltpu.VMEM((seqs, N_STATE, cw), F32),
            pltpu.VMEM((8, cc), F32),
            pltpu.VMEM((8, LANES), F32),
            pltpu.VMEM((8, cw), F32),
            pltpu.VMEM(small, F32),
            pltpu.VMEM((nf,) + small, F32),
            pltpu.VMEM(small, F32),
            pltpu.VMEM((nc,) + small, F32),
            pltpu.VMEM(gains, F32),
            pltpu.VMEM((nf,) + gains, F32),
            pltpu.VMEM(gains, F32),
            pltpu.VMEM((nc,) + gains, F32),
            dma((6,)),
            dma((2,)),
            dma((2, 2)),
            dma((2 * seqs, 2, nz)),
            dma((2 * seqs, 2, 2, nz)),
            dma((3, 2, places)),
            dma((2, 2, nc)),
            dma((4, 2, max(nc, nf))),
            dma((2,)),
            dma((3,)),
            pltpu.SemaphoreType.REGULAR((seqs,)),
            pltpu.SemaphoreType.DMA,
        ],
        compiler_params=pltpu.CompilerParams(
            collective_id=1, has_side_effects=True, vmem_limit_bytes=VMEM_LIMIT
        ),
        cost_estimate=pl.CostEstimate(
            flops=120_000_000_000, bytes_accessed=200_000_000, transcendentals=0
        ),
        name="back",
    )(lengths, hidden, cot, gain, *params, *bigs)


def finish_kernel(*refs):
    ins, outs, held, sems = refs[:8], refs[8:18], refs[18:26], refs[26]
    copies = [
        pltpu.make_async_copy(src, dst, sems.at[i]) for i, (src, dst) in enumerate(zip(ins, held))
    ]
    for copy in copies:
        copy.start()
    for copy in copies:
        copy.wait()
    for i in range(4):
        outs[i][...] = held[i][...]
    dconv_b, dgain, dheads, dnorm = held[4:]
    outs[4][...] = dconv_b[0]
    for i in range(3):
        outs[5 + i][...] = dheads[i]
    outs[8][...] = dgain[0]
    outs[9][...] = dnorm[0]


def call_finish(*results):
    shapes = [a.shape for a in results[:4]]
    shapes += [(CH,), (HEADS,), (HEADS,), (HEADS,), (DI,), (D,)]
    anywhere, vmem = pl.BlockSpec(memory_space=pl.ANY), pl.BlockSpec(memory_space=pltpu.VMEM)
    return pl.pallas_call(
        finish_kernel,
        in_specs=[anywhere] * 8,
        out_specs=[vmem] * 10,
        out_shape=[jax.ShapeDtypeStruct(a, F32) for a in shapes],
        scratch_shapes=[pltpu.VMEM(a.shape, F32) for a in results] + [pltpu.SemaphoreType.DMA((8,))],
        compiler_params=pltpu.CompilerParams(vmem_limit_bytes=VMEM_LIMIT),
        name="finish",
    )(*results)


def local(
    hidden,
    cotangent,
    lengths,
    norm_gain,
    input_weight,
    conv_w,
    conv_b,
    dt_bias,
    a_log,
    d_skip,
    gate_gain,
    output_weight,
):
    nc, nf = lax.axis_size("ctx"), lax.axis_size("fsdp")
    mb_count, seq_rows, length = hidden.shape[0], hidden.shape[1], hidden.shape[2]
    seqs = mb_count * seq_rows
    mine = seqs * length
    cw = DI // nc

    span = nf if (DI // nf // nc) % LANES == 0 else 1
    own = hidden.reshape(mine, D)
    cot = cotangent.reshape(mine, D)
    heads_in = jnp.pad(jnp.stack([dt_bias, a_log, d_skip]), ((0, 5), (0, 0)))
    seq_lengths = lengths.reshape(seqs)
    front = call_front(
        nc, nf, cw, span, seq_lengths, own, cot, input_weight.T, output_weight,
        norm_gain[None], conv_w, conv_b[None], heads_in, gate_gain[None],
    )
    out, *results = call_back(nc, nf, cw, span, seq_lengths, own, cot, norm_gain[None], *front)
    d_hidden, grad_in, grad_out, dconv_w, dconv_b, dbias, dalog, dskip, dgain, dnorm = call_finish(
        *results
    )
    shape = hidden.shape
    return (
        out.reshape(shape),
        d_hidden.reshape(shape),
        dnorm,
        grad_in,
        dconv_w,
        dconv_b,
        dbias,
        dalog,
        dskip,
        dgain,
        grad_out,
    )


def solution(mesh):
    tokens, rows, every = P(None, "fsdp", "ctx", None), P("fsdp", None), P()
    spread = P(("ctx", "fsdp"), None)
    in_specs = (
        tokens, tokens, P(None, "fsdp"), every, rows, every, every, every, every, every, every, rows,
    )
    out_specs = (
        tokens, tokens, every, spread, every, every, every, every, every, every, spread,
    )
    return jax.shard_map(local, mesh=mesh, in_specs=in_specs, out_specs=out_specs, check_vma=False)
```

```python
import functools

import jax
import jax.numpy as jnp
from jax import lax
from jax.experimental import pallas as pl
from jax.experimental.pallas import tpu as pltpu
from jax.sharding import PartitionSpec as P

D = 2048
HEADS = 64
HEAD_DIM = 64
N_STATE = 128
CONV_K = 4
DI = 4096
CH = DI + 2 * N_STATE
LANES = 128
EPS = 1e-05
F32 = jnp.float32
BF16 = jnp.bfloat16
EXACT = lax.Precision.HIGHEST
VMEM_LIMIT = 63 * 1024 * 1024


def dot(a, b, ca=1, cb=0):
    return lax.dot_general(
        a.astype(BF16), b.astype(BF16), (((ca,), (cb,)), ((), ())), preferred_element_type=F32
    )


def dot_exact(a, b):
    return lax.dot_general(
        a, b, (((1,), (0,)), ((), ())), precision=EXACT, preferred_element_type=F32
    )


def to_lanes(per_head, width):
    q = per_head.shape[0]
    low = lax.broadcasted_iota(jnp.int32, (q, LANES), 1) < HEAD_DIM
    pairs = []
    for j in range(width // LANES):
        first = jnp.broadcast_to(per_head[:, 2 * j : 2 * j + 1], (q, LANES))
        second = jnp.broadcast_to(per_head[:, 2 * j + 1 : 2 * j + 2], (q, LANES))
        pairs.append(jnp.where(low, first, second))
    return jnp.concatenate(pairs, axis=1)


def head_sum_matrix(width):
    channel = lax.broadcasted_iota(jnp.int32, (width, LANES), 0) // HEAD_DIM
    return (channel == lax.broadcasted_iota(jnp.int32, (width, LANES), 1)).astype(F32)


def split_heads(pair):
    low = lax.broadcasted_iota(jnp.int32, pair.shape, 1) < HEAD_DIM
    zero = jnp.zeros_like(pair)
    return jnp.concatenate([jnp.where(low, pair, zero), jnp.where(low, zero, pair)], axis=0)


def triangle(q, lower):
    rows = lax.broadcasted_iota(jnp.int32, (q, q), 0)
    cols = lax.broadcasted_iota(jnp.int32, (q, q), 1)
    return (rows >= cols) if lower else (rows <= cols)


def softplus(z):
    return jnp.maximum(z, 0.0) + jnp.log(1.0 + jnp.exp(-jnp.abs(z)))


def live_column(lengths_ref, s, chunk, q):
    slots = chunk * q + lax.broadcasted_iota(jnp.int32, (q, LANES), 0)
    return (slots < lengths_ref[s]).astype(F32)


def decays(dt_raw, bias, rate, live):
    q = dt_raw.shape[0]
    z = dt_raw + bias
    step = softplus(z) * live
    cum = dot_exact(triangle(q, True).astype(F32), step * rate)
    return z, step, cum


def head_pick(cw, span, me_c):
    mine, apart, each = cw // HEAD_DIM, HEADS // span, cw // HEAD_DIM // span
    lane = lax.broadcasted_iota(jnp.int32, (HEADS, LANES), 1)
    head = (lane // each) * apart + me_c * each + lax.rem(lane, each)
    row = lax.broadcasted_iota(jnp.int32, (HEADS, LANES), 0)
    return jnp.logical_and(row == head, lane < mine).astype(F32)


def forward_chunk(cw, chunk, s, lengths, proj, pick, conv_w, heads_par, chan_par, mixed_out, state_out, window, state):
    per = 2 if proj.shape[0] % 2 == 0 else 1
    length = proj.shape[2]
    q = per * length
    cc = cw + 2 * N_STATE
    causal = triangle(q, True)
    at = pl.ds(chunk * per, per)
    rows = proj[at, s].reshape(q, proj.shape[3])
    window[s, 8 : 8 + q, :] = rows[:, cw : cw + cc].astype(F32)
    pre = conv_w[CONV_K : CONV_K + 1, :] + conv_w[0:1, :] * window[s, 5 : 5 + q, :]
    for k in range(1, CONV_K):
        pre = pre + conv_w[k : k + 1, :] * window[s, 5 + k : 5 + k + q, :]
    window[s, 0:8, :] = window[s, q : q + 8, :]
    act = pre * jax.nn.sigmoid(pre)
    x = act[:, :cw]
    b = act[:, cw : cw + N_STATE]
    c = act[:, cw + N_STATE :]
    live = live_column(lengths, s, chunk, q)
    _, step, cum = decays(
        dot(rows[:, cw + cc :], pick[...]), heads_par[0:1, :], heads_par[1:2, :], live
    )
    cum_t = cum.T
    last = cum[q - 1 : q, :]
    u = x * to_lanes(step, cw)
    gram = dot(c, b, 1, 1)
    within = []
    for j in range(cw // LANES):
        kernels = []
        for h in (2 * j, 2 * j + 1):
            spread = jnp.where(causal, cum[:, h : h + 1] - cum_t[h : h + 1, :], -1e30)
            kernels.append((gram * jnp.exp(spread)).astype(BF16))
        both = jnp.concatenate(kernels, axis=1)
        within.append(dot(both, split_heads(u[:, j * LANES : (j + 1) * LANES])))
    before = state[s]
    state_out[chunk, s] = before.astype(BF16)
    mixed_out[chunk, s] = (
        jnp.concatenate(within, axis=1)
        + dot(c, before) * to_lanes(jnp.exp(cum), cw)
        + chan_par[0:1, :] * x
    )
    left = to_lanes(jnp.exp(last - cum), cw)
    state[s] = before * to_lanes(jnp.exp(last), cw) + dot(b, left * u, 0, 0)


def slot_columns(scales, chunk, s, row, cw):
    q = scales.shape[3]
    column = jnp.broadcast_to(scales[chunk, s, row : row + 1, :], (LANES, q)).T
    return jnp.concatenate([column] * (cw // LANES), axis=1)


def gated_chunk(cw, chunk, s, proj, scales, chan_par, mixed, gated):
    per = proj.shape[0] // mixed.shape[0]
    length = proj.shape[2]
    q = per * length
    at = pl.ds(chunk * per, per)
    gate = proj[at, s, :, :cw].reshape(q, cw).astype(F32)
    g = mixed[chunk, s] * gate * jax.nn.sigmoid(gate)
    normal = g * slot_columns(scales, chunk, s, 0, cw) * chan_par[1:2, :]
    gated[at, s] = normal.astype(BF16).reshape(per, length, cw)


def gate_chunk(cw, chunk, s, proj, scales, chan_par, gg, mixed, dchan):
    per = proj.shape[0] // mixed.shape[0]
    length = proj.shape[2]
    q = per * length
    at = pl.ds(chunk * per, per)
    gate = proj[at, s, :, :cw].reshape(q, cw).astype(F32)
    scale, pull = (slot_columns(scales, chunk, s, i, cw) for i in range(2))
    grad = gg[at, s].reshape(q, cw)
    sig = jax.nn.sigmoid(gate)
    silu = gate * sig
    m = mixed[chunk, s]
    g = m * silu
    gain = chan_par[1:2, :]
    dchan[1:2, :] += jnp.sum(grad * g * scale, axis=0, keepdims=True)
    dg = scale * (grad * gain - g * pull)
    gg[at, s] = (dg * silu).reshape(per, length, cw)
    dgate = dg * m * (sig * (1.0 + gate * (1.0 - sig)))
    proj[at, s, :, :cw] = dgate.astype(BF16).reshape(per, length, cw)


def backward_chunk(
    cw, chunk, s, lengths, proj, pick, conv_w, heads_par, chan_par, gm_in, mixed_in, state_in,
    dconv, dheads, dchan, window, ahead, state_grad,
):
    per = proj.shape[0] // mixed_in.shape[0]
    length = proj.shape[2]
    q = per * length
    cc = cw + 2 * N_STATE
    causal = triangle(q, True)
    sums = head_sum_matrix(cw)
    at = pl.ds(chunk * per, per)
    rows = proj[at, s, :, cw:].reshape(q, proj.shape[3] - cw)
    conv_in = rows[:, :cc].astype(F32)
    mixed = mixed_in[chunk, s]
    gm = gm_in[at, s].reshape(q, cw)
    if chunk:
        tail = proj[chunk * per - 1, s, length - 16 :, cw : cw + cc].astype(F32)
        window[s, 0:8, :] = tail[8:16]
    else:
        window[s, 0:8, :] = jnp.zeros((8, cc), F32)
    window[s, 8 : 8 + q, :] = conv_in
    pre = conv_w[CONV_K : CONV_K + 1, :] + conv_w[0:1, :] * window[s, 5 : 5 + q, :]
    for k in range(1, CONV_K):
        pre = pre + conv_w[k : k + 1, :] * window[s, 5 + k : 5 + k + q, :]
    sig_pre = jax.nn.sigmoid(pre)
    act = pre * sig_pre
    x = act[:, :cw]
    b = act[:, cw : cw + N_STATE]
    c = act[:, cw + N_STATE :]
    live = live_column(lengths, s, chunk, q)
    z, step, cum = decays(dot(rows[:, cc:], pick[...]), heads_par[0:1, :], heads_par[1:2, :], live)
    cum_t = cum.T
    last = cum[q - 1 : q, :]
    step_l = to_lanes(step, cw)
    u = x * step_l
    gram = dot(c, b, 1, 1)
    dchan[0:1, :] += jnp.sum(gm * x, axis=0, keepdims=True)
    du = []
    dgram = jnp.zeros((q, q), F32)
    for j in range(cw // LANES):
        lanes = slice(j * LANES, (j + 1) * LANES)
        dkernels = dot(gm[:, lanes], split_heads(u[:, lanes]), 1, 1)
        kernels = []
        for i in range(2):
            h = 2 * j + i
            spread = jnp.where(causal, cum[:, h : h + 1] - cum_t[h : h + 1, :], -1e30)
            decay = jnp.exp(spread)
            dgram = dgram + dkernels[:, i * q : (i + 1) * q] * decay
            kernels.append((gram * decay).astype(BF16))
        both = jnp.concatenate(kernels, axis=0)
        du.append(dot(both, split_heads(gm[:, lanes]), 0, 0))
    before = state_in[chunk, s].astype(F32)
    after_grad = state_grad[s]
    v = gm * to_lanes(jnp.exp(cum), cw)
    left = to_lanes(jnp.exp(last - cum), cw)
    du_state = left * dot(b, after_grad)
    du = jnp.concatenate(du, axis=1) + du_state
    dc = dot(dgram, b) + dot(v, before, 1, 1)
    db = dot(dgram, c, 0, 0) + dot(left * u, after_grad, 1, 1)
    end = to_lanes(jnp.exp(last), cw)
    extra = jnp.sum(u * du_state, axis=0, keepdims=True) + end * jnp.sum(
        after_grad * before, axis=0, keepdims=True
    )
    state_grad[s] = end * after_grad + dot(c, v, 0, 0)
    last_row = (lax.broadcasted_iota(jnp.int32, (q, LANES), 0) == q - 1).astype(F32)
    dcum = dot_exact(gm * (mixed - chan_par[0:1, :] * x) - u * du, sums) + last_row * dot_exact(
        jnp.broadcast_to(extra, (8, cw)), sums
    )[0:1, :]
    dlog = dot_exact(triangle(q, False).astype(F32), dcum)
    rate = heads_par[1:2, :]
    dstep = dot_exact(x * du, sums) + dlog * rate
    dheads[1:2, :] += jnp.sum(dlog * step * rate, axis=0, keepdims=True)
    dz = dstep * live * jax.nn.sigmoid(z)
    dheads[0:1, :] += jnp.sum(dz, axis=0, keepdims=True)
    dx = step_l * du + chan_par[0:1, :] * gm
    dpre = jnp.concatenate([dx, db, dc], axis=1) * (sig_pre * (1.0 + pre * (1.0 - sig_pre)))
    ahead[s, 0:q, :] = dpre
    dconv_in = jnp.zeros((q, cc), F32)
    for k in range(CONV_K):
        first = CONV_K - 1 - k
        moved = ahead[s, first : first + q, :]
        dconv_in = dconv_in + conv_w[k : k + 1, :] * moved
        dconv[k : k + 1, :] += jnp.sum(conv_in * moved, axis=0, keepdims=True)
    dconv[CONV_K : CONV_K + 1, :] += jnp.sum(dpre, axis=0, keepdims=True)
    ahead[s, q : q + 8, :] = ahead[s, 0:8, :]
    proj[at, s, :, cw : cw + cc] = dconv_in.astype(BF16).reshape(per, length, cc)
    dz = dot(dz, pick[...], 1, 1).astype(BF16)
    proj[at, s, :, cw + cc :] = dz.reshape(per, length, HEADS)


def column_tiles(n, body, size=256):
    if n <= size:
        body(0, n)
        return

    def one(j, _):
        body(pl.multiple_of(j * size, size), size)
        return 0

    lax.fori_loop(0, n // size, one, 0)


MESH = pl.DeviceIdType.MESH


class push:
    def __init__(self, src, dst, send_sem, recv_sem, device):
        self.args = (src, dst, send_sem, recv_sem, device, MESH)

    def start(self):
        pltpu.make_async_remote_copy(*self.args).start()

    def wait_send(self):
        pltpu.make_async_remote_copy(*self.args).wait_send()

    def wait_recv(self):
        pltpu.make_async_remote_copy(*self.args).wait_recv()

    def wait(self):
        self.wait_send()
        self.wait_recv()


def greet(devices_and_tests):
    return signal_all(pltpu.get_barrier_semaphore(), devices_and_tests)


def signal_all(barrier, devices_and_tests):
    count = 0
    for device, there in devices_and_tests:
        if there is None:
            pl.semaphore_signal(barrier, inc=1, device_id=device, device_id_type=MESH)
            count = count + 1
        else:
            @pl.when(there)
            def _():
                pl.semaphore_signal(barrier, inc=1, device_id=device, device_id_type=MESH)

            count = count + there.astype(jnp.int32)
    return lambda: pl.semaphore_wait(barrier, count)


def line_of(nc):
    me = lax.axis_index("ctx")
    return nc // 2, me // 2, lax.rem(me, 2)


def square_partners():
    me = lax.axis_index("fsdp")
    high, low = me // 2, lax.rem(me, 2)
    return me, high * 2 + (1 - low), (1 - high) * 2 + low


class LineGather:
    def __init__(self, nc, every, sems):
        self.nz, self.z, self.k = line_of(nc)
        self.every = every
        self.up, self.down, self.side, self.got, self.got_side = sems

    def slot(self, place):
        return self.every.at[2 * place + self.k]

    def copies(self, d, below):
        z, k = self.z, self.k
        origin = z - d if below else z + d
        to = z + 1 if below else z - 1
        on = push(
            self.slot(origin), self.slot(origin), (self.up if below else self.down).at[d],
            self.got.at[origin], {"ctx": 2 * to + k},
        )
        side = push(
            self.slot(origin), self.slot(origin), self.side.at[origin], self.got_side.at[origin],
            {"ctx": 2 * z + 1 - k},
        )
        there = origin >= 0 if below else origin <= self.nz - 1
        further = to <= self.nz - 1 if below else to >= 0
        return on, side, there, further

    def begin(self):
        for below in (True, False):
            on, side, _, further = self.copies(0, below)
            pl.when(further)(on.start)
        side.start()

    def step(self, d):
        for below in (True, False):
            on, side, there, further = self.copies(d, below)

            @pl.when(there)
            def _():
                on.wait_recv()
                pl.when(further)(on.start)
                side.start()

    def sides(self, least, most):
        for place in range(self.nz):
            arrived = self.every.at[2 * place + 1 - self.k]
            apart = jnp.abs(place - self.z)
            pl.when(jnp.logical_and(apart >= least, apart <= most))(
                push(
                    arrived, arrived, self.side.at[place], self.got_side.at[place],
                    {"ctx": 2 * self.z + 1 - self.k},
                ).wait_recv
            )

    def end(self):
        for place in range(self.nz):
            arrived = self.every.at[2 * place + 1 - self.k]
            push(
                arrived, arrived, self.side.at[place], self.got_side.at[place],
                {"ctx": 2 * self.z + 1 - self.k},
            ).wait_send()
        for d in range(self.nz - 1):
            for below in (True, False):
                on, _, there, further = self.copies(d, below)
                pl.when(jnp.logical_and(there, further))(on.wait_send)


class SquareGather:
    def __init__(self, nf, every, sems):
        self.nf, self.every = nf, every
        self.send, self.got = sems
        self.half = every.shape[1] // 2

    def peers(self):
        me = lax.axis_index("fsdp")
        if self.nf == 4:
            _, fx, fy = square_partners()
            return [(fx, fx), (fy, fy)]
        return [
            (lax.rem(me + j, self.nf), lax.rem(me + self.nf - j, self.nf))
            for j in range(1, self.nf)
        ]

    def first(self):
        me = lax.axis_index("fsdp")
        for j, (to, frm) in enumerate(self.peers()):
            args = (self.send.at[j], self.got.at[j], {"fsdp": to})
            mine, theirs = self.every.at[me], self.every.at[frm]
            yield push(mine, mine, *args), push(theirs, theirs, *args)

    def second(self):
        me, fx, fy = square_partners()
        pairs = []
        for j, (via, to) in enumerate(((fx, fy), (fy, fx))):
            rows = pl.ds(j * self.half, self.half)
            args = (self.send.at[2 + j], self.got.at[2 + j], {"fsdp": to})
            there, here = self.every.at[via, rows], self.every.at[3 - me, rows]
            pairs.append((push(there, there, *args), push(here, here, *args)))
        return pairs

    def begin(self):
        for out, _ in self.first():
            out.start()

    def step(self):
        for j, (_, arrived) in enumerate(self.first()):
            arrived.wait_recv()
            if self.nf == 4:
                self.second()[j][0].start()

    def far(self):
        if self.nf == 4:
            for _, arrived in self.second():
                arrived.wait_recv()

    def end(self):
        for out, _ in self.first():
            out.wait_send()
        if self.nf == 4:
            for out, _ in self.second():
                out.wait_send()


class ChipGather:
    def __init__(self, nf, every, sems):
        self.nf, self.every = nf, every
        me = lax.axis_index("ctx")
        self.core, self.other = lax.rem(me, 2), {"ctx": me + 1 - 2 * lax.rem(me, 2)}
        self.half = every.shape[1] // 2
        mine = every.at[:, pl.ds(pl.multiple_of(self.core * self.half, 16), self.half)]
        self.square = SquareGather(nf, mine, sems[:2])
        self.send, self.got = sems[2:]

    def side(self, f, core):
        part = self.every.at[f, pl.ds(pl.multiple_of(core * self.half, 16), self.half)]
        return push(part, part, self.send.at[f], self.got.at[f], self.other)

    def near(self):
        return [frm for _, frm in self.square.peers()]

    def begin(self):
        self.square.begin()

    def step(self):
        self.square.step()
        for f in self.near():
            self.side(f, self.core).start()

    def sides(self):
        for f in self.near():
            self.side(f, 1 - self.core).wait_recv()

    def far(self):
        self.square.far()
        if self.nf == 4:
            f = 3 - lax.axis_index("fsdp")
            self.side(f, self.core).start()
            self.side(f, 1 - self.core).wait_recv()

    def end(self):
        self.square.end()
        for f in self.near():
            self.side(f, self.core).wait_send()
        if self.nf == 4:
            self.side(3 - lax.axis_index("fsdp"), self.core).wait_send()


class SquareSpread:
    def __init__(self, nf, source, every, sems):
        self.nf, self.every = nf, every
        self.send, self.got = sems
        self.mine = lax.axis_index("fsdp") == source

    def copies(self):
        me = lax.axis_index("fsdp")
        return [
            push(
                self.every, self.every, self.send.at[j], self.got.at[0],
                {"fsdp": lax.rem(me + j, self.nf)},
            )
            for j in range(1, self.nf)
        ]

    def begin(self):
        for out in self.copies():
            pl.when(self.mine)(out.start)

    def step(self):
        pass

    def far(self):
        if self.nf > 1:
            pl.when(jnp.logical_not(self.mine))(self.copies()[0].wait_recv)

    def end(self):
        for out in self.copies():
            pl.when(self.mine)(out.wait_send)


class Exchange:
    def __init__(self, axis, n, own, every, sems):
        self.axis, self.n, self.own, self.every = axis, n, own, every
        self.send, self.got = sems

    def copies(self):
        me = lax.axis_index(self.axis)
        for j in range(1, self.n):
            to, frm = lax.rem(me + j, self.n), lax.rem(me + self.n - j, self.n)
            args = (self.send.at[j], self.got.at[j], {self.axis: to})
            yield push(self.own, self.every.at[me], *args), push(self.own, self.every.at[frm], *args)

    def begin(self):
        self.every[lax.axis_index(self.axis)] = self.own[...]
        for out, _ in self.copies():
            out.start()

    def wait(self):
        for out, arrived in self.copies():
            arrived.wait_recv()
            out.wait_send()

    def total(self):
        result = self.every[0]
        for i in range(1, self.n):
            result = result + self.every[i]
        return result


def front_kernel(
    nc, nf, cw, span, lengths, hidden, cot, in_w, out_w, norm_gain, conv_w, conv_b, heads_in, gate_gain,
    normed_out, cot_out, main_out, tail_out, gated_out, proj_out, gg_out, mixed_out, states_out, branch_out,
    scales, conv_par, heads_par, chan_par, pick,
    normed_t, cot_v, main_v, tail_v, gated_t, proj, gg, mixed, states, branch, rows_v, normed_v, acc, gated,
    window, state, stats, stats_held, more, more_held,
    line_sems, main_sems, tail_sems, rows_sems, stat_sems, load_sems, keep_sems,
):
    nz, z, k = line_of(nc)
    me_c, me_f = lax.axis_index("ctx"), lax.axis_index("fsdp")
    wide, apart = cw // span, DI // span
    depth = in_w.shape[1]
    seqs, length = proj.shape[1], proj.shape[2]
    per = 2 if nc % 2 == 0 else 1
    q, chunks = per * length, nc // per

    found = [({"ctx": lax.rem(me_c + j, nc)}, None) for j in range(1, nc)]
    found += [({"fsdp": lax.rem(me_f + j, nf)}, None) for j in range(1, nf)]
    met = greet(found)

    loads = []

    def load(src, dst):
        copy = pltpu.make_async_copy(src, dst, load_sems.at[len(loads)])
        copy.start()
        loads.append(copy)

    for part in range(2):
        for i in range(span):
            start = pl.multiple_of(part * DI + i * apart + wide * me_c, LANES)
            load(in_w.at[pl.ds(start, wide)], main_v.at[me_f, pl.ds(part * cw + i * wide, wide)])
    load(in_w.at[pl.ds(2 * DI, tail_v.shape[1])], tail_v.at[me_f])
    weight_loads = len(loads)
    load(cot, cot_v.at[me_c])
    if span > 1:
        load(out_w.at[pl.ds(pl.multiple_of(wide * me_c, 16), wide)], rows_v.at[me_f])
    else:
        lap = out_w.shape[0] // cw
        held = me_f == me_c // lap
        rows_load = pltpu.make_async_copy(
            out_w.at[pl.ds(pl.multiple_of(cw * lax.rem(me_c, lap), 16), cw)], rows_v.at[0],
            load_sems.at[len(loads)],
        )
        pl.when(held)(rows_load.start)

    def norm(i, _):
        at = pl.ds(pl.multiple_of(i * 16, 16), 16)
        src = hidden[at].astype(F32)
        mean = jnp.mean(src * src, axis=1, keepdims=True)
        normed_v[me_c, at] = (src * lax.rsqrt(mean + EPS) * norm_gain[...]).astype(BF16)
        return 0

    lax.fori_loop(0, hidden.shape[0] // 16, norm, 0)

    line = lambda i, every: LineGather(nc, every, [line_sems.at[i, j] for j in range(5)])
    normed_line, cot_line = line(0, normed_v), line(1, cot_v)
    main = SquareGather(nf, main_v, (main_sems.at[0], main_sems.at[1]))
    tails = ChipGather(nf, tail_v, [tail_sems.at[i] for i in range(4)])
    if span > 1:
        rows = SquareGather(nf, rows_v, (rows_sems.at[0], rows_sems.at[1]))
    else:
        rows = SquareSpread(nf, me_c // lap, rows_v.at[0], (rows_sems.at[0], rows_sems.at[1]))
    kept = []

    def keep(src, dst):
        copy = pltpu.make_async_copy(src, dst, keep_sems.at[len(kept)])
        copy.start()
        kept.append(copy)

    for copy in loads[:weight_loads]:
        copy.wait()
    met()
    main.begin()
    normed_line.begin()
    tails.begin()

    pick[...] = head_pick(cw, span, me_c)
    conv_par[...] = jnp.zeros_like(conv_par)
    chan_par[...] = jnp.zeros_like(chan_par)
    for i in range(span):
        here = pl.ds(i * wide, wide)
        there = pl.ds(pl.multiple_of(i * apart + wide * me_c, LANES), wide)
        conv_par[0:CONV_K, here] = conv_w[:, there]
        conv_par[CONV_K : CONV_K + 1, here] = conv_b[:, there]
        chan_par[1:2, here] = gate_gain[:, there]
    conv_par[0:CONV_K, cw:] = conv_w[:, DI:CH]
    conv_par[CONV_K : CONV_K + 1, cw:] = conv_b[:, DI:CH]
    picked = dot_exact(heads_in[...], pick[...])
    heads_par[0:1, :] = picked[0:1, :]
    heads_par[1:2, :] = -jnp.exp(picked[1:2, :])
    heads_par[2:8, :] = jnp.zeros((6, LANES), F32)
    chan_par[0:1, :] = to_lanes(picked[2:3, :], cw)
    window[...] = jnp.zeros_like(window)
    state[...] = jnp.zeros_like(state)

    for copy in loads[weight_loads:]:
        copy.wait()
    if span == 1:
        pl.when(held)(rows_load.wait)
    slots = nc * normed_v.shape[1]

    def project(depths, first, last):
        def part(weights, base):
            def body(start, size):
                sums = None
                for f in depths:
                    a = normed_v[:, :, pl.ds(pl.multiple_of(f * depth, LANES), depth)]
                    term = dot(a.reshape(slots, depth), weights[f, pl.ds(start, size)], 1, 1)
                    sums = term if sums is None else sums + term
                here = pl.ds(base + start, size)
                if not first:
                    sums = sums + acc[:, here]
                if last:
                    proj[:, :, :, here] = sums.astype(BF16).reshape(proj.shape[:3] + (size,))
                else:
                    acc[:, here] = sums

            return body

        column_tiles(2 * cw, part(main_v, 0))
        column_tiles(tail_v.shape[1], part(tail_v, 2 * cw), tail_v.shape[1])

    for d in range(1, min(nz, 3)):
        normed_line.step(d)
    cot_line.begin()
    main.step()
    tails.step()
    for d in range(3, nz):
        normed_line.step(d)
    normed_line.sides(0, nz)
    tails.sides()
    if nf == 4:
        _, fx, fy = square_partners()
        project([me_f, fx, fy], True, False)
    if nz > 1:
        cot_line.step(1)
    main.far()
    tails.far()
    rows.begin()
    if nf == 4:
        project([3 - me_f], False, True)
    else:
        for j in range(nf):
            project([lax.rem(me_f + j, nf)], j == 0, j == nf - 1)
    keep(main_v, main_out)
    keep(tail_v, tail_out)
    keep(proj, proj_out)

    def across(a):
        total = a[:, :LANES]
        for j in range(1, cw // LANES):
            total = total + a[:, j * LANES : (j + 1) * LANES]
        return jnp.sum(total.T, axis=0, keepdims=True)

    def before_norm(chunk, s):
        at = pl.ds(chunk * per, per)
        gate = proj[at, s, :, :cw].reshape(q, cw).astype(F32)
        return at, mixed[chunk, s] * gate * jax.nn.sigmoid(gate)

    for chunk in range(chunks):
        for s in range(seqs):
            forward_chunk(
                cw, chunk, s, lengths, proj, pick, conv_par, heads_par, chan_par, mixed, states,
                window, state,
            )
            _, g = before_norm(chunk, s)
            row = chunk * seqs + s
            stats[row : row + 1, :] = across(g * g)
        if chunk == chunks // 2 - 1:
            rows.step()
    squares = Exchange("ctx", nc, stats, stats_held, (stat_sems.at[0, 0], stat_sems.at[0, 1]))
    squares.begin()
    keep(mixed, mixed_out)
    keep(states, states_out)
    for d in range(2, nz - 1):
        cot_line.step(d)
    mine = normed_v.shape[1]

    def turn(c, _):
        normed_t[:, pl.ds(pl.multiple_of(c * mine, LANES), mine)] = normed_v[c].T
        return 0

    lax.fori_loop(0, nc, turn, 0)
    keep(normed_t, normed_out)
    squares.wait()
    totals = squares.total() * (1.0 / DI)
    for chunk in range(chunks):
        for s in range(seqs):
            row = chunk * seqs + s
            scales[chunk, s, 0:1, :] = lax.rsqrt(totals[row : row + 1, :] + EPS)
            gated_chunk(cw, chunk, s, proj, scales, chan_par, mixed, gated)
    rows.far()

    def branch_tile(start, size):
        part = dot(gated[...].reshape(slots, cw), rows_v[:, :, pl.ds(start, size)].reshape(cw, size))
        part = part.astype(BF16).reshape(nc, seqs, length, size)
        for s in range(seqs):
            branch[s, :, :, pl.ds(start, size)] = part[:, s]

    column_tiles(D, branch_tile)
    keep(branch, branch_out)
    gated_t[...] = gated[...].reshape(slots, cw).T
    keep(gated_t, gated_out)

    if nz > 2:
        cot_line.step(nz - 1)
    cot_line.sides(0, nz)
    keep(cot_v, cot_out)
    cots = cot_v[...].reshape(slots, D)
    weights = rows_v[...].reshape(cw, D)
    half = min(cw, 256)
    for i in range(cw // half):
        gg[:, :, :, i * half : (i + 1) * half] = dot(
            cots, weights[i * half : (i + 1) * half], 1, 1
        ).reshape(gg.shape[:3] + (half,))
    keep(gg, gg_out)
    for chunk in range(chunks):
        for s in range(seqs):
            at, g = before_norm(chunk, s)
            row = chunk * seqs + s
            more[row : row + 1, :] = across(gg[at, s].reshape(q, cw) * chan_par[1:2, :] * g)
    pulls = Exchange("ctx", nc, more, more_held, (stat_sems.at[1, 0], stat_sems.at[1, 1]))
    pulls.begin()
    pulls.wait()
    totals = pulls.total() * (1.0 / DI)
    for chunk in range(chunks):
        for s in range(seqs):
            row = chunk * seqs + s
            scale = scales[chunk, s, 0:1, :]
            scales[chunk, s, 1:2, :] = scale * scale * totals[row : row + 1, :]
            scales[chunk, s, 2:8, :] = jnp.zeros((6, q), F32)
    for part in (main, tails, rows, normed_line, cot_line):
        part.end()
    for copy in kept:
        copy.wait()


def call_front(nc, nf, cw, span, lengths, hidden, cot, in_w, out_w, norm_gain, conv_w, conv_b, heads_in, gate_gain):
    nz = nc // 2
    mine = hidden.shape[0]
    seqs = lengths.shape[0]
    length = mine // seqs
    per = 2 if nc % 2 == 0 else 1
    q, chunks, cc = per * length, nc // per, cw + 2 * N_STATE
    depth, wide, ends = in_w.shape[1], cw // span, in_w.shape[0] - 2 * DI
    cols = 2 * cw + ends
    vmem = pl.BlockSpec(memory_space=pltpu.VMEM)
    anywhere = pl.BlockSpec(memory_space=pl.ANY)
    dma = pltpu.SemaphoreType.DMA
    big = [
        ((D, nc * mine), BF16),
        ((nc, mine, D), BF16),
        ((nf, 2 * cw, depth), BF16),
        ((nf, ends, depth), BF16),
        ((cw, nc * mine), BF16),
        ((nc, seqs, length, cols), BF16),
        ((nc, seqs, length, cw), F32),
        ((chunks, seqs, q, cw), F32),
        ((chunks, seqs, N_STATE, cw), BF16),
        ((seqs, nc, length, D), BF16),
    ]
    small = [
        ((chunks, seqs, 8, q), F32),
        ((8, cc), F32),
        ((8, LANES), F32),
        ((8, cw), F32),
        ((HEADS, LANES), F32),
    ]
    held = big + [
        ((span, wide, D), BF16),
        ((nc, mine, D), BF16),
        ((nc * mine, cols), F32),
        ((nc, seqs, length, cw), BF16),
        ((seqs, q + 8, cc), F32),
        ((seqs, N_STATE, cw), F32),
    ]
    held += [((chunks * seqs, q), F32), ((nc, chunks * seqs, q), F32)] * 2
    places = max(nf, 4)
    return pl.pallas_call(
        functools.partial(front_kernel, nc, nf, cw, span),
        in_specs=[pl.BlockSpec(memory_space=pltpu.SMEM), vmem, vmem, anywhere, anywhere]
        + [vmem] * 5,
        out_specs=[anywhere] * len(big) + [vmem] * len(small),
        out_shape=[jax.ShapeDtypeStruct(*a) for a in big + small],
        scratch_shapes=[pltpu.VMEM(*a) for a in held]
        + [
            dma((2, 5, nz)),
            dma((2, places)),
            dma((4, places)),
            dma((2, places)),
            dma((2, 2, nc)),
            dma((2 * span + 3,)),
            dma((10,)),
        ],
        compiler_params=pltpu.CompilerParams(
            collective_id=0, has_side_effects=True, vmem_limit_bytes=VMEM_LIMIT
        ),
        name="front",
    )(lengths, hidden, cot, in_w, out_w, norm_gain, conv_w, conv_b, heads_in, gate_gain)


def add_rows(into, other, rows=16):
    def body(i, _):
        at = pl.ds(pl.multiple_of(i * rows, rows), rows)
        into[at] = (into[at].astype(F32) + other[at].astype(F32)).astype(into.dtype)
        return 0

    lax.fori_loop(0, into.shape[0] // rows, body, 0)


class LineReduce:
    def __init__(self, nc, parts, acc, landed, sems):
        self.nz, self.z, self.k = line_of(nc)
        self.parts, self.acc, self.landed = parts, acc, landed
        self.side, self.got_side, self.send, self.got = sems

    def to_side(self, place):
        other = {"ctx": 2 * self.z + 1 - self.k}
        return push(
            self.parts.at[2 * place + 1 - self.k], self.acc.at[place], self.side.at[place],
            self.got_side.at[place], other,
        )

    def begin(self):
        for place in range(self.nz):
            self.to_side(place).start()

    def merge(self):
        for place in range(self.nz):
            self.to_side(place).wait_recv()
            add_rows(self.acc.at[place], self.parts.at[2 * place + self.k])

    def along(self, place, up):
        way = 0 if up else 1
        slot = place if up else jnp.where(place == self.z - 1, self.nz, place)
        return push(
            self.acc.at[place], self.landed.at[slot], self.send.at[way, place],
            self.got.at[way, place], {"ctx": 2 * (self.z + (1 if up else -1)) + self.k},
        )

    def arrive(self, place, up, into, slot=None):
        self.along(place, up).wait_recv()
        add_rows(into, self.landed.at[place if slot is None else slot])

    def step(self, tick):
        z, nz = self.z, self.nz
        for place in range(nz):
            for up in (True, False):
                at = tick - (nz - 1 - place) if up else nz - 1 + place - tick
                if not (0 <= at < place if up else place < at <= nz - 1):
                    continue
                first, before = (0, place + 1) if up else (nz - 1, place - 1)

                @pl.when(z == at)
                def _():
                    if at != first:
                        self.arrive(place, up, self.acc.at[place])
                    elif 0 <= before <= nz - 1:
                        self.along(before, up).wait_send()
                    self.along(place, up).start()

    def final(self, total):
        z, nz = self.z, self.nz
        total[...] = self.acc[z].astype(F32)

        @pl.when(z > 0)
        def _():
            self.arrive(z, True, total)

        @pl.when(z < nz - 1)
        def _():
            self.arrive(z, False, total, nz)

    def end(self):
        for place in range(self.nz):
            self.to_side(place).wait_send()
        for place in range(self.nz):
            last = self.nz - 1
            self_up = jnp.logical_and(self.z < place, jnp.logical_or(self.z > 0, place == 1))
            self_down = jnp.logical_and(
                self.z > place, jnp.logical_or(self.z < last, place == last - 1)
            )
            pl.when(self_up)(self.along(place, True).wait_send)
            pl.when(self_down)(self.along(place, False).wait_send)


class SquareReduce:
    def __init__(self, nf, parts, landed, total, sems, inner=False, shift=0):
        self.nf, self.parts, self.landed, self.total = nf, parts, landed, total
        self.send, self.got = sems
        self.inner, self.shift = inner, shift
        self.half = total.shape[0] // 2

    def part(self, f, at):
        if self.inner:
            return self.parts.at[at, f]
        return self.parts.at[lax.rem(f + self.nf - self.shift, self.nf), at]

    @staticmethod
    def landing(nf, shape):
        blocks, rows, cols = shape
        return (6, blocks // 2, rows, cols) if nf == 4 else (nf, blocks, rows, cols)

    def copy(self, n, src, to):
        return push(src, self.landed.at[n], self.send.at[n], self.got.at[n], {"fsdp": to})

    def way(self, h):
        me, fx, fy = square_partners()
        first, second = (fx, fy) if h == 0 else (fy, fx)
        return me, first, second, pl.ds(h * self.half, self.half)

    def firsts(self, h):
        me, first, second, at = self.way(h)
        return (
            self.copy(3 * h, self.part(3 - me, at), first),
            self.copy(3 * h + 1, self.part(first, at), first),
        )

    def second_(self, h):
        _, _, second, _ = self.way(h)
        return self.copy(3 * h + 2, self.landed.at[3 * h], second)

    def others(self):
        me = lax.axis_index("fsdp")
        tos = [lax.rem(me + j, self.nf) for j in range(1, self.nf)]
        every = pl.ds(0, self.total.shape[0])
        return [self.copy(j + 1, self.part(to, every), to) for j, to in enumerate(tos)]

    def begin(self):
        if self.nf == 4:
            for i in range(2):
                for h in range(2):
                    self.firsts(h)[i].start()
        else:
            for out in self.others():
                out.start()

    def add(self, into, other):
        for b in range(into.shape[0]):
            add_rows(into.at[b], other.at[b], min(16, into.shape[1]))

    def step(self):
        if self.nf == 4:
            for h in range(2):
                _, _, second, at = self.way(h)
                self.firsts(h)[0].wait_recv()
                self.add(self.landed.at[3 * h], self.part(second, at))
                self.second_(h).start()

    def final(self, h):
        me = lax.axis_index("fsdp")
        at = pl.ds(h * self.half, self.half)
        if self.nf == 4:
            self.firsts(h)[1].wait_recv()
            into = self.total.at[at]
            into[...] = self.part(me, at)[...]
            self.add(into, self.landed.at[3 * h + 1])
            self.second_(h).wait_recv()
            self.add(into, self.landed.at[3 * h + 2])
        else:
            into = self.total.at[at]
            into[...] = self.part(me, at)[...]
            for j, out in enumerate(self.others()):
                if h == 0:
                    out.wait_recv()
                self.add(into, self.landed.at[j + 1, at])

    def end(self):
        if self.nf == 4:
            for h in range(2):
                for out in (*self.firsts(h), self.second_(h)):
                    out.wait_send()
        else:
            for out in self.others():
                out.wait_send()


class Deal:
    def __init__(self, nc, parts, pieces, sems, here):
        self.nc, self.parts, self.pieces = nc, parts, pieces
        self.send, self.got, self.here = sems[0], sems[1], here
        self.me = lax.axis_index("ctx")

    def to(self, c):
        return push(
            self.parts.at[c], self.pieces.at[self.me], self.send.at[c], self.got.at[self.me], {"ctx": c}
        )

    def stay(self):
        return pltpu.make_async_copy(self.parts.at[self.me], self.pieces.at[self.me], self.here)

    def start(self, h):
        half = self.nc // 2
        for j in range(half):
            c = h * half + lax.rem(self.me + j, half)
            pl.when(c != self.me)(self.to(c).start)

            @pl.when(c == self.me)
            def _():
                self.stay().start()

    def wait(self):
        self.stay().wait()
        for c in range(self.nc):

            @pl.when(c != self.me)
            def _():
                push(
                    self.parts.at[c], self.pieces.at[c], self.send.at[c], self.got.at[c], {"ctx": c}
                ).wait()


def back_kernel(
    nc, nf, cw, span, lengths, hidden, cot, gain, scales, conv_par, heads_par, chan_par, pick,
    normed_in, cot_in, main_in, tail_in, gated_in, proj_in, gg_in, mixed_in, states_in, branch_in,
    out, d_hidden, grad_in, grad_out, dconv_w, dconv_b, dgain, dheads_out, dnorm_gain,
    normed_t, cot_v, main_v, tail_v, gated_t, proj, gg, mixed, states,
    dnormed, gout, gate_parts, x_parts, acc, landed, total,
    gout_landed, gout_sum, gate_landed, gate_sum, x_landed, x_sum, gate_pieces, x_pieces, gout_mine,
    window, ahead, state_grad, dconv, dheads, dchan,
    small, small_held, small_sum, small_all, gains, gains_held, gains_sum, gains_all,
    load_sems, cot_sems, main_sems, line_sems, way_sems, square_sems, deal_sems, small_sems, route_sems,
    here, line_free, branch_sem,
):
    nz, _, _ = line_of(nc)
    me_c, me_f = lax.axis_index("ctx"), lax.axis_index("fsdp")
    wide, apart = cw // span, DI // span
    cc, ends = cw + 2 * N_STATE, tail_v.shape[1]
    seqs, length = proj.shape[1], proj.shape[2]
    chunks = mixed.shape[0]
    slots = nc * seqs * length

    found = [({"ctx": lax.rem(me_c + j, nc)}, None) for j in range(1, nc)]
    found += [({"fsdp": lax.rem(me_f + j, nf)}, None) for j in range(1, nf)]
    if span > 1:
        turn = lax.rem(me_c // 2, nf)
        lead, place = lax.rem(me_f + nf - turn, nf) * nc + me_c, me_c * nf + me_f
        target = {"ctx": lead // nf, "fsdp": lax.rem(lead, nf)}
        origin = lax.rem(place, nc)
        source = {"ctx": origin, "fsdp": lax.rem(place // nc + lax.rem(origin // 2, nf), nf)}
        away = lead != place
        found += [(target, away), (source, away)]
    met = greet(found)

    loads = []
    branch_load = pltpu.make_async_copy(branch_in, dnormed, branch_sem)
    branch_load.start()
    for i, (src, dst) in enumerate((
        (proj_in, proj), (mixed_in, mixed), (gg_in, gg), (gated_in, gated_t), (normed_in, normed_t),
        (states_in, states),
    )):
        copy = pltpu.make_async_copy(src, dst, load_sems.at[i])
        copy.start()
        loads.append(copy)

    quarter = cot_v.shape[3]

    def cot_part(i):
        return pltpu.make_async_copy(
            cot_in.at[:, :, pl.ds(pl.multiple_of(i * quarter, LANES), quarter)],
            cot_v.at[lax.rem(i, 2)], cot_sems.at[lax.rem(i, 2)],
        )

    def weights_part(f):
        slot = lax.rem(f, 2)
        return (
            pltpu.make_async_copy(main_in.at[f], main_v.at[slot], main_sems.at[0, slot]),
            pltpu.make_async_copy(tail_in.at[f], tail_v.at[slot], main_sems.at[1, slot]),
        )

    def start_weights(f):
        for copy in weights_part(f):
            copy.start()

    for i in range(2):
        cot_part(i).start()
    every_line = [
        LineReduce(
            nc, dnormed.at[i % seqs], acc.at[i % seqs], landed.at[i % seqs],
            (line_sems.at[i, 0], line_sems.at[i, 1], way_sems.at[i, 0], way_sems.at[i, 1]),
        )
        for i in range(2 * seqs)
    ]
    out_lines, lines = every_line[:seqs], every_line[seqs:]
    neighbours = [
        ({"ctx": me_c + 1 - 2 * lax.rem(me_c, 2)}, None),
        ({"ctx": me_c + 2}, me_c + 2 < nc),
        ({"ctx": me_c - 2}, me_c - 2 >= 0),
    ]

    def put_out(s):
        rows = pl.ds(s * length, length)
        out_lines[s].final(total.at[rows])
        out[rows] = (total[rows] + hidden[rows].astype(F32)).astype(BF16)
        out_lines[s].end()
        freed.append(signal_all(line_free.at[s], neighbours))

    freed = []
    square = lambda i, *refs, **how: SquareReduce(
        nf, *refs, (square_sems.at[i, 0], square_sems.at[i, 1]), **how
    )
    gout_square = square(0, gout, gout_landed, gout_sum, shift=turn if span > 1 else 0)
    gate_square = square(1, gate_parts, gate_landed, gate_sum, inner=True)
    x_square = square(2, x_parts, x_landed, x_sum, inner=True)
    gate_deal = Deal(nc, gate_sum, gate_pieces, (deal_sems.at[0, 0], deal_sems.at[0, 1]), here.at[0])
    x_deal = Deal(nc, x_sum, x_pieces, (deal_sems.at[1, 0], deal_sems.at[1, 1]), here.at[1])
    pair = lambda i: (small_sems.at[i, 0], small_sems.at[i, 1])
    smalls = (
        Exchange("fsdp", nf, small, small_held, pair(0)),
        Exchange("ctx", nc, small_sum, small_all, pair(1)),
    )
    gain_sums = (
        Exchange("fsdp", nf, gains, gains_held, pair(2)),
        Exchange("ctx", nc, gains_sum, gains_all, pair(3)),
    )

    for ref in (window, ahead, state_grad, dconv, dheads, dchan, small):
        ref[...] = jnp.zeros_like(ref)
    branch_load.wait()
    met()
    for line in out_lines:
        line.begin()
    for copy in loads[:3]:
        copy.wait()
    for chunk in range(chunks):
        for s in range(seqs):
            gate_chunk(cw, chunk, s, proj, scales, chan_par, gg, mixed, dchan)

    def out_acts(s):
        return [out_lines[s].merge] + [lambda i=i: out_lines[s].step(i) for i in range(nz - 1)]

    first, second = (out_acts(s) for s in (0, seqs - 1))
    first.pop(0)()
    first.pop(0)() if first else None

    loads[3].wait()

    def gout_part(i, _):
        cot_part(i).wait()
        size = min(quarter, 256)
        for j in range(quarter // size):
            cots = cot_v[lax.rem(i, 2), :, :, j * size : (j + 1) * size].reshape(slots, size)
            at = pl.ds(pl.multiple_of(i * quarter + j * size, LANES), size)
            gout[:, :, :, at] = (
                dot(gated_t[...], cots).reshape(gout.shape[:3] + (size,)).astype(BF16)
            )
        pl.when(i + 2 < D // quarter)(lambda: cot_part(i + 2).start())
        return 0

    lax.fori_loop(0, D // quarter, gout_part, 0)
    gout_square.begin()
    first.pop(0)() if first else None
    if seqs > 1:
        second.pop(0)()
        second.pop(0)() if second else None
    loads[4].wait()

    def in_tile(parts, base, shift):
        def body(start, size):
            grads = proj[:, :, :, pl.ds(base + start, size)].reshape(slots, size)
            parts[:, :, :, pl.ds(shift + start, size)] = (
                dot(normed_t[...], grads).reshape(parts.shape[:3] + (size,)).astype(BF16)
            )

        return body

    column_tiles(cw, in_tile(gate_parts, 0, 0))
    gate_square.begin()
    while first:
        first.pop(0)()
    for copy in loads[5:]:
        copy.wait()

    if span > 1:
        route = push(gout_sum, gout_mine, route_sems.at[0], route_sems.at[1], target)
        stay = lambda: pltpu.make_async_copy(gout_sum, gout_mine, here.at[2])

    def finish_gout():
        for h in range(2):
            gout_square.final(h)
        if span > 1:
            pl.when(away)(route.start)
            pl.when(jnp.logical_not(away))(lambda: stay().start())

    def finish_gate():
        for h in range(2):
            gate_square.final(h)
            gate_deal.start(h)

    depth = main_v.shape[2]
    narrow = min(depth, 256)

    def normed_part(s):
        def body(f, _):
            for copy in weights_part(f):
                copy.wait()
            for j in range(depth // narrow):
                here = pl.ds(j * narrow, narrow)
                grads = proj[:, s].reshape(nc * length, proj.shape[3])
                sums = dot(grads[:, : 2 * cw], main_v[lax.rem(f, 2), :, here])
                sums = sums + dot(grads[:, 2 * cw :], tail_v[lax.rem(f, 2), :, here])
                at = pl.ds(pl.multiple_of(f * depth + j * narrow, LANES), narrow)
                dnormed[s, :, :, at] = sums.astype(BF16).reshape(nc, length, narrow)
            pl.when(f + 2 < nf)(lambda: start_weights(f + 2))
            return 0

        lax.fori_loop(0, nf, body, 0)

    def line_acts(line):
        return [line.merge] + [lambda i=i: line.step(i) for i in range(nz - 1)]

    later = [
        second[:1], [gout_square.step], [lambda: put_out(0)] + second[1:2],
        [finish_gout] + second[2:],
    ]
    for s in range(seqs):
        for f in range(min(2, nf)):
            start_weights(f)
        for i in range(chunks):
            backward_chunk(
                cw, chunks - 1 - i, s, lengths, proj, pick, conv_par, heads_par, chan_par, gg, mixed,
                states, dconv, dheads, dchan, window, ahead, state_grad,
            )
            if later:
                for act in later.pop(0):
                    act()
        if s == seqs - 1:
            column_tiles(cw, in_tile(x_parts, cw, 0))
            column_tiles(ends, in_tile(x_parts, 2 * cw, cw), ends)
            x_square.begin()
        normed_part(s)
        freed[s]()
        lines[s].begin()
        if s < seqs - 1:
            acts = line_acts(lines[s])
            for left in later:
                for act in left:
                    act()
            later = [
                acts[:2], [lambda: put_out(seqs - 1), gate_square.step], acts[2:3],
                acts[3:] + [finish_gate],
            ]

    for left in later:
        for act in left:
            act()

    dskip = dot_exact(jnp.broadcast_to(dchan[0:1, :], (8, cw)), head_sum_matrix(cw))[0:1, :]
    row = 0
    for k in range(CONV_K + 1):
        for j in range(cc // LANES):
            small[row : row + 1, :] = dconv[k : k + 1, j * LANES : (j + 1) * LANES]
            row += 1
    for j in range(cw // LANES):
        small[row : row + 1, :] = dchan[1:2, j * LANES : (j + 1) * LANES]
        row += 1
    small[row : row + 1, :] = dheads[0:1, :]
    small[row + 1 : row + 2, :] = dheads[1:2, :]
    small[row + 2 : row + 3, :] = dskip
    smalls[0].begin()
    acts = line_acts(lines[-1])
    acts.pop(0)()
    acts.pop(0)() if acts else None
    smalls[0].wait()
    small_sum[...] = smalls[0].total()
    smalls[1].begin()
    acts.pop(0)() if acts else None
    x_square.step()
    for act in acts:
        act()
    for s in range(seqs):
        lines[s].final(total.at[pl.ds(s * length, length)])
    dnorm = jnp.zeros((1, D), F32)

    def norm_back(i, dnorm):
        at = pl.ds(pl.multiple_of(i * 16, 16), 16)
        src = hidden[at].astype(F32)
        dn = total[at]
        scale = lax.rsqrt(jnp.mean(src * src, axis=1, keepdims=True) + EPS)
        h = dn * gain[...]
        pull = jnp.mean(h * src, axis=1, keepdims=True) * scale * scale
        d_hidden[at] = scale * (h - src * pull) + cot[at].astype(F32)
        return dnorm + jnp.sum(dn * src * scale, axis=0, keepdims=True)

    dnorm = lax.fori_loop(0, hidden.shape[0] // 16, norm_back, dnorm)
    for j in range(D // LANES):
        gains[j : j + 1, :] = dnorm[:, j * LANES : (j + 1) * LANES]
    gain_sums[0].begin()
    for h in range(2):
        x_square.final(h)
        x_deal.start(h)
    gain_sums[0].wait()
    gains_sum[...] = gain_sums[0].total()
    gain_sums[1].begin()

    def ordered(pieces, base):
        for c in range(nc):
            for i in range(span):
                to = base + i * apart + c * wide
                grad_in[:, to : to + wide] = pieces[c, :, i * wide : (i + 1) * wide].astype(F32)

    gate_deal.wait()
    ordered(gate_pieces, 0)
    if span > 1:

        @pl.when(away)
        def _():
            route.wait_recv()
            route.wait_send()

        @pl.when(jnp.logical_not(away))
        def _():
            stay().wait()

        grad_out[...] = gout_mine[...].reshape(grad_out.shape).astype(F32)
    else:
        grad_out[...] = gout_sum[...].astype(F32).reshape(grad_out.shape)
    smalls[1].wait()
    groups = cc // LANES
    for k in range(CONV_K + 1):
        to_ref, to_row = (dconv_w, k) if k < CONV_K else (dconv_b, 0)
        for c in range(nc):
            for j in range(cw // LANES):
                i, inside = j * LANES // wide, j * LANES % wide
                to = i * apart + c * wide + inside
                to_ref[to_row : to_row + 1, to : to + LANES] = small_all[
                    c, k * groups + j : k * groups + j + 1, :
                ]
        for j in range(cw // LANES, groups):
            shared = small_all[0, k * groups + j : k * groups + j + 1, :]
            for c in range(1, nc):
                shared = shared + small_all[c, k * groups + j : k * groups + j + 1, :]
            to = DI + j * LANES - cw
            to_ref[to_row : to_row + 1, to : to + LANES] = shared
    first = (CONV_K + 1) * groups
    by_head = jnp.zeros((8, HEADS), F32)
    for c in range(nc):
        for j in range(cw // LANES):
            i, inside = j * LANES // wide, j * LANES % wide
            to = i * apart + c * wide + inside
            dgain[:, to : to + LANES] = small_all[c, first + j : first + j + 1, :]
        rows = small_all[c, first + cw // LANES : first + cw // LANES + 8, :]
        by_head = by_head + lax.dot_general(
            rows, head_pick(cw, span, c), (((1,), (1,)), ((), ())), precision=EXACT,
            preferred_element_type=F32,
        )
    dheads_out[...] = by_head
    gain_sums[1].wait()
    summed = gain_sums[1].total()
    for j in range(D // LANES):
        dnorm_gain[:, j * LANES : (j + 1) * LANES] = summed[j : j + 1, :]
    for line in lines:
        line.end()
    gout_square.end()
    gate_square.end()
    x_square.end()
    x_deal.wait()
    ordered(x_pieces, DI)
    shared = x_pieces[0, :, cw:].astype(F32)
    for c in range(1, nc):
        shared = shared + x_pieces[c, :, cw:].astype(F32)
    grad_in[:, 2 * DI :] = shared


def call_back(nc, nf, cw, span, lengths, hidden, cot, gain, *front):
    bigs, params = front[:10], front[10:]
    proj, mixed = bigs[5], bigs[7]
    _, seqs, length, cols = proj.shape
    nz, mine = nc // 2, seqs * length
    slots, q = nc * mine, mixed.shape[2]
    cc, ends, rows = cw + 2 * N_STATE, cols - 2 * cw, D // (nc * nf)
    vmem = pl.BlockSpec(memory_space=pltpu.VMEM)
    anywhere = pl.BlockSpec(memory_space=pl.ANY)
    dma = pltpu.SemaphoreType.DMA
    landing = SquareReduce.landing
    gout = (2, cw // nf // 2, D)
    gate, x = (nc, rows, cw), (nc, rows, cw + ends)
    count = (CONV_K + 1) * (cc // LANES) + cw // LANES + 3
    small = (-(-(count + 5) // 8) * 8, LANES)
    gains = (D // LANES, LANES)
    places = max(nf, 6)
    return pl.pallas_call(
        functools.partial(back_kernel, nc, nf, cw, span),
        in_specs=[pl.BlockSpec(memory_space=pltpu.SMEM)] + [vmem] * 8 + [anywhere] * 10,
        out_specs=[vmem] * 9,
        out_shape=[
            jax.ShapeDtypeStruct((mine, D), BF16),
            jax.ShapeDtypeStruct((mine, D), F32),
            jax.ShapeDtypeStruct((rows, 2 * DI + ends), F32),
            jax.ShapeDtypeStruct((cw // nf, D), F32),
            jax.ShapeDtypeStruct((CONV_K, CH), F32),
            jax.ShapeDtypeStruct((1, CH), F32),
            jax.ShapeDtypeStruct((1, DI), F32),
            jax.ShapeDtypeStruct((8, HEADS), F32),
            jax.ShapeDtypeStruct((1, D), F32),
        ],
        scratch_shapes=[
            pltpu.VMEM(bigs[0].shape, BF16),
            pltpu.VMEM((2, nc, mine, 256), BF16),
            pltpu.VMEM((2,) + bigs[2].shape[1:], BF16),
            pltpu.VMEM((2,) + bigs[3].shape[1:], BF16),
        ]
        + [pltpu.VMEM(a.shape, a.dtype) for a in bigs[4:9]]
        + [
            pltpu.VMEM((seqs, nc, length, D), BF16),
            pltpu.VMEM((nf,) + gout, BF16),
            pltpu.VMEM((nc, nf, rows, cw), BF16),
            pltpu.VMEM((nc, nf, rows, cw + ends), BF16),
            pltpu.VMEM((seqs, nz, length, D), BF16),
            pltpu.VMEM((seqs, nz + 1, length, D), BF16),
            pltpu.VMEM((mine, D), F32),
            pltpu.VMEM(landing(nf, gout), BF16),
            pltpu.VMEM(gout, BF16),
            pltpu.VMEM(landing(nf, gate), BF16),
            pltpu.VMEM(gate, BF16),
            pltpu.VMEM(landing(nf, x), BF16),
            pltpu.VMEM(x, BF16),
            pltpu.VMEM(gate, BF16),
            pltpu.VMEM(x, BF16),
            pltpu.VMEM(gout, BF16),
            pltpu.VMEM((seqs, q + 8, cc), F32),
            pltpu.VMEM((seqs, q + 8, cc), F32),
            pltpu.VMEM((seqs, N_STATE, cw), F32),
            pltpu.VMEM((8, cc), F32),
            pltpu.VMEM((8, LANES), F32),
            pltpu.VMEM((8, cw), F32),
            pltpu.VMEM(small, F32),
            pltpu.VMEM((nf,) + small, F32),
            pltpu.VMEM(small, F32),
            pltpu.VMEM((nc,) + small, F32),
            pltpu.VMEM(gains, F32),
            pltpu.VMEM((nf,) + gains, F32),
            pltpu.VMEM(gains, F32),
            pltpu.VMEM((nc,) + gains, F32),
            dma((6,)),
            dma((2,)),
            dma((2, 2)),
            dma((2 * seqs, 2, nz)),
            dma((2 * seqs, 2, 2, nz)),
            dma((3, 2, places)),
            dma((2, 2, nc)),
            dma((4, 2, max(nc, nf))),
            dma((2,)),
            dma((3,)),
            pltpu.SemaphoreType.REGULAR((seqs,)),
            pltpu.SemaphoreType.DMA,
        ],
        compiler_params=pltpu.CompilerParams(
            collective_id=1, has_side_effects=True, vmem_limit_bytes=VMEM_LIMIT
        ),
        cost_estimate=pl.CostEstimate(
            flops=120_000_000_000, bytes_accessed=200_000_000, transcendentals=0
        ),
        name="back",
    )(lengths, hidden, cot, gain, *params, *bigs)


def finish_kernel(*refs):
    ins, outs, held, sems = refs[:8], refs[8:18], refs[18:26], refs[26]
    copies = [
        pltpu.make_async_copy(src, dst, sems.at[i]) for i, (src, dst) in enumerate(zip(ins, held))
    ]
    for copy in copies:
        copy.start()
    for copy in copies:
        copy.wait()
    for i in range(4):
        outs[i][...] = held[i][...]
    dconv_b, dgain, dheads, dnorm = held[4:]
    outs[4][...] = dconv_b[0]
    for i in range(3):
        outs[5 + i][...] = dheads[i]
    outs[8][...] = dgain[0]
    outs[9][...] = dnorm[0]


def call_finish(*results):
    shapes = [a.shape for a in results[:4]]
    shapes += [(CH,), (HEADS,), (HEADS,), (HEADS,), (DI,), (D,)]
    anywhere, vmem = pl.BlockSpec(memory_space=pl.ANY), pl.BlockSpec(memory_space=pltpu.VMEM)
    return pl.pallas_call(
        finish_kernel,
        in_specs=[anywhere] * 8,
        out_specs=[vmem] * 10,
        out_shape=[jax.ShapeDtypeStruct(a, F32) for a in shapes],
        scratch_shapes=[pltpu.VMEM(a.shape, F32) for a in results] + [pltpu.SemaphoreType.DMA((8,))],
        compiler_params=pltpu.CompilerParams(vmem_limit_bytes=VMEM_LIMIT),
        name="finish",
    )(*results)


def local(
    hidden,
    cotangent,
    lengths,
    norm_gain,
    input_weight,
    conv_w,
    conv_b,
    dt_bias,
    a_log,
    d_skip,
    gate_gain,
    output_weight,
):
    nc, nf = lax.axis_size("ctx"), lax.axis_size("fsdp")
    mb_count, seq_rows, length = hidden.shape[0], hidden.shape[1], hidden.shape[2]
    seqs = mb_count * seq_rows
    mine = seqs * length
    cw = DI // nc

    span = nf if (DI // nf // nc) % LANES == 0 else 1
    own = hidden.reshape(mine, D)
    cot = cotangent.reshape(mine, D)
    heads_in = jnp.pad(jnp.stack([dt_bias, a_log, d_skip]), ((0, 5), (0, 0)))
    seq_lengths = lengths.reshape(seqs)
    front = call_front(
        nc, nf, cw, span, seq_lengths, own, cot, input_weight.T, output_weight,
        norm_gain[None], conv_w, conv_b[None], heads_in, gate_gain[None],
    )
    out, *results = call_back(nc, nf, cw, span, seq_lengths, own, cot, norm_gain[None], *front)
    d_hidden, grad_in, grad_out, dconv_w, dconv_b, dbias, dalog, dskip, dgain, dnorm = call_finish(
        *results
    )
    shape = hidden.shape
    return (
        out.reshape(shape),
        d_hidden.reshape(shape),
        dnorm,
        grad_in,
        dconv_w,
        dconv_b,
        dbias,
        dalog,
        dskip,
        dgain,
        grad_out,
    )


def solution(mesh):
    tokens, rows, every = P(None, "fsdp", "ctx", None), P("fsdp", None), P()
    spread = P(("ctx", "fsdp"), None)
    in_specs = (
        tokens, tokens, P(None, "fsdp"), every, rows, every, every, every, every, every, every, rows,
    )
    out_specs = (
        tokens, tokens, every, spread, every, every, every, every, every, every, spread,
    )
    return jax.shard_map(local, mesh=mesh, in_specs=in_specs, out_specs=out_specs, check_vma=False)
```
